128 devices in a mesh: gx: 4 (over x), gy: 32 (over z, y, core).
Axes of the slice: x: 4, y: 4, z: 4, core: 2. Of those that a mesh axis runs over, the one named last changes fastest.
Arguments:
- port_loads: float32 [64, 393216], P(None, ('gx', 'gy')), may hold values from -80 to 80
- port_stiff: float32 [3, 2, 512, 512], replicated, may hold values from -1 to 4, as said below
- bubble_inverse: float32 [3, 64, 64], replicated, may hold values from -1 to 1, as said below
- coupling: float32 [2048, 64, 512], P(('gx', 'gy')), may hold values from -0.125 to 0.125
- theta_table: float32 [16, 2], replicated, may hold values from 0.5 to 2
- comp_arch: int32 [2048], P(('gx', 'gy')), may hold values from 0 to 2
- comp_param: int32 [2048], P(('gx', 'gy')), may hold values from 0 to 15
- port_refs: int32 [2048, 8], P(('gx', 'gy')), may hold values from 0 to 63, as said below
- slot_mask: int32 [2048, 8], P(('gx', 'gy')), may hold values from 0 to 1, as said below
- cut_source: int32 [128, 16], P(('gx', 'gy')), may hold values from 0 to 47, as said below
Outputs:
- solution: float32 [64, 393216], P(None, ('gx', 'gy'))
- residual: float32 [64, 393216], P(None, ('gx', 'gy'))
The draws below stay inside these ranges and needn't reach their ends.
Inputs may be any that keep to these rules, and one draw needn't show every extreme that they name: `port_refs`: each slot names one of a device's 48 owned ports (0 to 47) or one of 16 ghost ports, ghost g being port cut_source[k - 1, g] of the previous device. Slots 0 to 2 of one device's components name each owned port exactly once between them. `slot_mask`: 1 on the first 4 to 8 slots of each component and 0 after them; 0 on ghost references of the first device's components. `cut_source`: each row names 16 distinct owned ports. `port_stiff`: each matrix is symmetric positive definite. `bubble_inverse`: each matrix is symmetric positive definite.
All inputs are finite; a program needn't handle non-finite values.
Results may differ from the reference program's by a relative error of at most 0.0003.
Values sent between devices are 32-bit elements; how exact they have to be, the bound alone decides.
A program may use at most 128 MiB of HBM per device.

```python
import math
import jax
import jax.numpy as jnp
from jax import lax

DOF = 64
BUB = 64
SLOTS = 8
COLS = 64
TERMS = 2
ARCH = 3
PARAMS = 16
ITERS = 2
COMP_DEV = 16
OWN_DEV = 48
CUT = 16
SHARDS = 128
COMPONENTS = 2048
PORTS = 6144


def draw_port_loads(key, part):
    key = jax.random.fold_in(key, 11)
    subkeys = jax.random.split(key, 3)
    length_all = PORTS * DOF
    port_index = (jnp.arange(length_all) // DOF).astype(jnp.float32)
    rising = 1.0 + 2.0 * port_index / max(PORTS - 1, 1)
    jitter = jnp.exp(jax.random.uniform(subkeys[1], (PORTS,), jnp.float32, -0.7, 0.4))
    column_scale = jnp.exp(jax.random.uniform(subkeys[2], (COLS, 1), jnp.float32, -1.2, 1.1))
    sample = jnp.clip(jax.random.normal(subkeys[0], (COLS, length_all), jnp.float32), -5.0, 5.0)
    return sample * column_scale * rising[None, :] * jnp.repeat(jitter, DOF)[None, :]


def draw_port_stiff(key, part):
    key = jax.random.fold_in(key, 23)
    subkeys = jax.random.split(key, 2)
    port_width = SLOTS * DOF
    full_shape = (ARCH, TERMS, port_width, port_width)
    sample = jax.random.normal(subkeys[0], full_shape, jnp.float32)
    spread = 0.28 / port_width ** 0.5
    mirror = (sample + jnp.swapaxes(sample, 2, 3)) * spread
    diagonal = jax.random.uniform(subkeys[1], (ARCH, TERMS, port_width, 1), jnp.float32, 2.0, 4.0)
    identity = jnp.arange(port_width)[:, None] == jnp.arange(port_width)[None, :]
    return jnp.where(identity, diagonal, mirror)


def draw_bubble_inverse(key, part):
    key = jax.random.fold_in(key, 29)
    subkeys = jax.random.split(key, 2)
    full_shape = (ARCH, BUB, BUB)
    sample = jax.random.normal(subkeys[0], full_shape, jnp.float32)
    spread = 0.056 / BUB ** 0.5
    mirror = (sample + jnp.swapaxes(sample, 1, 2)) * spread
    diagonal = jnp.exp(jax.random.uniform(subkeys[1], (ARCH, BUB, 1), jnp.float32, -0.69, 0.0))
    identity = jnp.arange(BUB)[:, None] == jnp.arange(BUB)[None, :]
    return jnp.where(identity, diagonal, mirror)


def port_layout(key):
    key = jax.random.fold_in(key, 7)
    subkeys = jax.random.split(key, 3)
    shard_keys = jax.random.split(subkeys[0], SHARDS)
    shuffled = jax.vmap(lambda item: jax.random.permutation(item, OWN_DEV))(shard_keys).astype(jnp.int32)
    leading = shuffled.reshape(SHARDS, COMP_DEV, 3)
    trailing = jax.random.randint(subkeys[1], (SHARDS, COMP_DEV, SLOTS - 3), 0, OWN_DEV + CUT).astype(jnp.int32)
    references = jnp.concatenate([leading, trailing], axis=2).reshape(COMPONENTS, SLOTS)
    counts = jax.random.randint(subkeys[2], (COMPONENTS, 1), 4, SLOTS + 1)
    position = jnp.arange(SLOTS)[None, :]
    shard_index = (jnp.arange(COMPONENTS) // COMP_DEV)[:, None]
    slot_alive = (position < counts) & jnp.logical_not((shard_index == 0) & (references >= OWN_DEV))
    return (references.astype(jnp.int32), slot_alive.astype(jnp.int32))


def draw_port_refs(key, part):
    return port_layout(key)[0]


def draw_slot_mask(key, part):
    return port_layout(key)[1]


def draw_cut_source(key, part):
    key = jax.random.fold_in(key, 31)
    shard_keys = jax.random.split(key, SHARDS)
    shuffled = jax.vmap(lambda item: jax.random.permutation(item, OWN_DEV))(shard_keys)
    return shuffled[:, :CUT].astype(jnp.int32)


def plant(result, rng, low, largest):
    longest = result.shape.index(max(result.shape))
    spots = []
    for shift in (0, 1):
        where = [jax.random.randint(jax.random.fold_in(rng, axis), (), 0, length) for axis, length in enumerate(result.shape)]
        where[longest] = (where[longest] + shift) % result.shape[longest]
        spots.append(tuple(where))
    return result.at[spots[0]].set(low).at[spots[1]].set(largest)


def levels(key, dims, cuts, low, largest):
    def one(dim, parts):
        heights = jax.random.uniform(jax.random.fold_in(jax.random.fold_in(key, 6), dim), (parts,), jnp.float32, low / len(cuts), largest / len(cuts))
        return jnp.repeat(jnp.exp(heights), dims[dim] // parts).reshape((-1,) + (1,) * (len(dims) - dim - 1))

    loudness = one(*cuts[0])
    for cut in cuts[1:]:
        loudness = loudness * one(*cut)
    return loudness


def centred(stream_key, shape, scale, bound, shards=(), dtype=jnp.bfloat16):
    array = scale * jax.random.normal(stream_key, shape, jnp.float32)
    if shards:
        array = array * levels(stream_key, shape, shards, -0.22, 0.18)
    return jnp.clip(array, -bound, bound).astype(dtype)


def setup_inputs(seed: int = 0) -> dict:
    keys = jax.random.split(jax.random.key(seed), 11)
    return {
        "port_loads": draw_port_loads(jax.random.fold_in(keys[10], 71), 0),
        "port_stiff": draw_port_stiff(jax.random.fold_in(keys[10], 71), 0),
        "bubble_inverse": draw_bubble_inverse(jax.random.fold_in(keys[10], 71), 0),
        "coupling": centred(keys[3], (COMPONENTS, BUB, SLOTS * DOF), (4 * SLOTS * DOF) ** -0.5, 0.125, ((0, 128),), jnp.float32),
        "theta_table": jnp.clip(jnp.exp(jax.random.uniform(keys[4], (PARAMS, TERMS), jnp.float32, math.log(0.5), math.log(2.0))), 0.5, 2.0),
        "comp_arch": plant(jax.random.randint(keys[5], (COMPONENTS,), 0, ARCH), jax.random.fold_in(keys[5], 1), 0, ARCH - 1).astype(jnp.int32),
        "comp_param": plant(jax.random.randint(keys[6], (COMPONENTS,), 0, PARAMS), jax.random.fold_in(keys[6], 1), 0, PARAMS - 1).astype(jnp.int32),
        "port_refs": draw_port_refs(jax.random.fold_in(keys[10], 71), 0),
        "slot_mask": draw_slot_mask(jax.random.fold_in(keys[10], 71), 0),
        "cut_source": draw_cut_source(jax.random.fold_in(keys[10], 71), 0),
    }


precise = lax.Precision.HIGHEST

def schur_blocks(port_stiff, bubble_inverse, coupling, theta_table, comp_arch, comp_param):
    arch_count, term_count, block_width, unused_width = port_stiff.shape
    components = coupling.shape[0]
    bubble_count = coupling.shape[1]
    param_count = theta_table.shape[0]
    arch_hot = (comp_arch[:, None] == jnp.arange(arch_count)[None, :]).astype(jnp.float32)
    param_hot = (comp_param[:, None] == jnp.arange(param_count)[None, :]).astype(jnp.float32)
    thetas = jnp.dot(param_hot, theta_table, precision=precise)
    weights = (arch_hot[:, :, None] * thetas[:, None, :]).reshape(components, arch_count * term_count)
    stiff_table = port_stiff.reshape(arch_count * term_count, block_width, block_width)
    group_size = math_gcd(components, 8)
    groups = components // group_size

    def build(block_data):
        weight_rows, hot_rows, theta_rows, bubble_coupling = block_data
        stiffness = jnp.einsum('ck,kij->cij', weight_rows, stiff_table, precision=precise)
        inverse = jnp.einsum('ca,aij->cij', hot_rows, bubble_inverse, precision=precise)
        moved_rows = jnp.einsum('cab,cbj->caj', inverse, bubble_coupling, precision=precise)
        bubble = jnp.einsum('cai,caj->cij', bubble_coupling, moved_rows, precision=precise)
        return stiffness - theta_rows[:, 0, None, None] * bubble
    block_data = (weights.reshape(groups, group_size, arch_count * term_count), arch_hot.reshape(groups, group_size, arch_count), thetas.reshape(groups, group_size, term_count), coupling.reshape(groups, group_size, bubble_count, block_width))
    built = lax.map(build, block_data)
    return built.reshape(components, block_width, block_width)

def math_gcd(first, second):
    while second:
        first, second = (second, first % second)
    return first

def gram_matrix(left, right):
    return lax.dot_general(left, right, (((1,), (1,)), ((), ())), precision=precise)

def solve_spd(matrix, rhs_block):
    factor = jnp.linalg.cholesky(matrix)
    return jax.scipy.linalg.cho_solve((factor, True), rhs_block)

def reference(port_loads, port_stiff, bubble_inverse, coupling, theta_table, comp_arch, comp_param, port_refs, slot_mask, cut_source):
    block_width = SLOTS * DOF
    device = (jnp.arange(COMPONENTS) // COMP_DEV).astype(jnp.int32)
    before = jnp.maximum(device - 1, 0).astype(jnp.int32)
    ghost_slot = jnp.clip(port_refs - OWN_DEV, 0, CUT - 1).astype(jnp.int32)
    ghost_port = before[:, None] * OWN_DEV + cut_source[before[:, None], ghost_slot]
    global_refs = jnp.where(port_refs < OWN_DEV, device[:, None] * OWN_DEV + port_refs, ghost_port).astype(jnp.int32)
    slot_alive = slot_mask.astype(jnp.float32)
    shard_data = (coupling.reshape(SHARDS, COMP_DEV, BUB, block_width), comp_arch.reshape(SHARDS, COMP_DEV), comp_param.reshape(SHARDS, COMP_DEV), global_refs.reshape(SHARDS, COMP_DEV * SLOTS), slot_alive.reshape(SHARDS, COMP_DEV * SLOTS))

    def operate(vector):
        field = vector.reshape(COLS, PORTS, DOF)

        def add_shard(summed, data):
            bubble_coupling, arch_ids, param_ids, refs, alive = data
            schur = schur_blocks(port_stiff, bubble_inverse, bubble_coupling, theta_table, arch_ids, param_ids)
            picked = jnp.take(field, refs, axis=1) * alive[None, :, None]
            picked = picked.reshape(COLS, COMP_DEV, block_width)
            product = jnp.einsum('kcj,cij->kci', picked, schur, precision=precise)
            product = product.reshape(COLS, COMP_DEV * SLOTS, DOF) * alive[None, :, None]
            return (summed.at[:, refs].add(product), None)
        summed, unused = lax.scan(add_shard, jnp.zeros((COLS, PORTS, DOF), jnp.float32), shard_data)
        return summed.reshape(COLS, PORTS * DOF)
    solution = jnp.zeros((COLS, PORTS * DOF), jnp.float32)
    residual = port_loads
    direction = port_loads
    current = gram_matrix(residual, residual)
    for iteration in range(ITERS):
        product = operate(direction)
        curve = gram_matrix(direction, product)
        step_size = solve_spd(curve, current)
        solution = solution + jnp.dot(step_size.T, direction, precision=precise)
        residual = residual - jnp.dot(step_size.T, product, precision=precise)
        if iteration + 1 < ITERS:
            following = gram_matrix(residual, residual)
            ratio = solve_spd(current, following)
            direction = residual + jnp.dot(ratio.T, direction, precision=precise)
            current = following
    return (solution, residual)
```

```python
import functools

import jax
import jax.numpy as jnp
from jax import lax
from jax.experimental import pallas as pl
from jax.experimental.pallas import tpu as pltpu
from jax.sharding import PartitionSpec as P

MESH = pl.DeviceIdType.MESH
F32 = jnp.float32
BF16 = jnp.bfloat16


def parts(value):
    high = value.astype(BF16)
    return high, (value - high.astype(F32)).astype(BF16)


def mm(left, right):
    return jnp.dot(left, right, preferred_element_type=F32)


def mm_tn(left, right):
    return lax.dot_general(left, right, (((0,), (0,)), ((), ())), preferred_element_type=F32)


def exact(left, right):
    return lax.dot_general(
        left,
        right,
        (((1,), (0,)), ((), ())),
        precision=lax.Precision.HIGHEST,
        preferred_element_type=F32,
    )


def peers_of(mesh_sizes):
    sizes_x, sizes_y = mesh_sizes
    groups = []
    stride = 1
    for size in (2, 4):
        if sizes_y // stride > 1:
            size = min(size, sizes_y // stride)
            groups.append(("gy", stride, size))
            stride *= size
    if sizes_y // stride > 1:
        groups.append(("gy", stride, sizes_y // stride))
    if sizes_x > 1:
        groups.append(("gx", 1, sizes_x))
    return groups


def system_kernel(
    sizes,
    groups,
    table,
    arch,
    param,
    theta,
    inverse,
    loads_hbm,
    stiff_hbm,
    coupling_hbm,
    first_nat,
    second_nat,
    grams,
    loads,
    stiff,
    coupling,
    blocks,
    field,
    running,
    load_parts,
    first_parts,
    landed,
    send_a,
    recv_a,
    send_l,
    recv_l,
    send_p,
    recv_p,
    send_t,
    recv_t,
    sums,
    slots,
    load_sem,
    send_sem,
    recv_sem,
    sum_send,
    sum_recv,
):
    sizes_x, sizes_y = sizes
    comps = coupling.shape[0]
    dofs = field.shape[1]
    cols = loads.shape[0]
    owned = loads.shape[1] // dofs
    slot_count = 8
    refs = comps * slot_count
    width = slot_count * dofs
    cut = 2 * send_a.shape[0]
    half = cut // 2
    ext = owned + cut
    at_prev, at_last, at_cut, at_inv = refs, 2 * refs, 2 * refs + ext, 2 * refs + ext + cut

    my_x, my_y = lax.axis_index("gx"), lax.axis_index("gy")
    here = my_x * sizes_y + my_y
    total = sizes_x * sizes_y
    after = lax.rem(here + 1, total)
    before = lax.rem(here + total - 1, total)
    next_id = (after // sizes_y, lax.rem(after, sizes_y))
    prev_id = (before // sizes_y, lax.rem(before, sizes_y))

    def peer(group, offset):
        axis, stride, size = group
        if axis == "gx":
            return (lax.rem(my_x + offset, size), my_y)
        place = lax.rem(my_y // stride, size)
        other = lax.rem(place + offset, size)
        return (my_x, my_y + (other - place) * stride)

    load_copy = pltpu.make_async_copy(loads_hbm, loads, load_sem.at[0])
    load_copy.start()
    stiff_copy = pltpu.make_async_copy(stiff_hbm, stiff, load_sem.at[1])
    stiff_copy.start()
    coupling_copy = pltpu.make_async_copy(coupling_hbm, coupling, load_sem.at[2])
    coupling_copy.start()

    barrier = pltpu.get_barrier_semaphore()
    targets = [next_id, prev_id]
    for group in groups:
        for offset in range(1, group[2]):
            targets.append(peer(group, offset))
    for target in targets:
        pl.semaphore_signal(barrier, inc=1, device_id=target, device_id_type=MESH)

    lane = lax.broadcasted_iota(jnp.int32, (dofs, 128), 1)
    left_lanes = lane < cols

    def fold(value):
        return value + pltpu.roll(value, cols, 1)

    def split(full):
        high = full.astype(BF16).astype(F32)
        return jnp.where(left_lanes, high, full - high).astype(BF16)

    def send(index, source, target_ref, device):
        return pltpu.make_async_remote_copy(
            src_ref=source,
            dst_ref=target_ref,
            send_sem=send_sem.at[index],
            recv_sem=recv_sem.at[index],
            device_id=device,
            device_id_type=MESH,
        )

    def expand(received):
        def body(g, carry):
            pair = received[g]
            landed[g] = jnp.where(left_lanes, pair, 0.0)
            landed[g + half] = jnp.where(left_lanes, 0.0, pair)
            return carry

        lax.fori_loop(0, half, body, 0)

    def pack_ghosts(target):
        def body(g, carry):
            one = fold(running[table[at_last + owned + g]])
            two = fold(running[table[at_last + owned + half + g]])
            target[g] = jnp.where(left_lanes, one, two)
            return carry

        lax.fori_loop(0, half, body, 0)

    def apply():
        def body(c, carry):
            first = c * slot_count
            picked = jnp.concatenate(
                [field[table[first + j]] for j in range(slot_count)], axis=0
            )
            product = mm(blocks[c], jnp.concatenate([picked, picked], axis=0))
            for j in range(slot_count):
                running[first + j] = (
                    running[table[at_prev + first + j]] + product[j * dofs : (j + 1) * dofs]
                )
            return carry

        lax.fori_loop(0, comps, body, 0)

    def gram(left, right):
        both = mm(left, right)
        rows = both[:cols] + both[cols:]
        full = fold(rows)
        return jnp.where(left_lanes[: cols // 2], full[: cols // 2], full[cols // 2 :])

    load_copy.wait()

    def spread(b, carry):
        at = pl.ds(pl.multiple_of(b * 128, 128), 128)
        piece = loads[:, at]
        high, low = parts(piece)
        load_parts[:cols, at] = high
        load_parts[cols:, at] = low
        turned = jnp.concatenate([piece, piece], axis=0).T
        running[2 * b] = turned[:dofs]
        running[2 * b + 1] = turned[dofs:]
        field[2 * b] = split(turned[:dofs])
        field[2 * b + 1] = split(turned[dofs:])
        return carry

    lax.fori_loop(0, owned // 2, spread, 0)

    def pack_cut(g, carry):
        one = running[table[at_cut + g]]
        two = running[table[at_cut + half + g]]
        send_a[g] = jnp.where(left_lanes, one, two)
        return carry

    lax.fori_loop(0, half, pack_cut, 0)
    pl.semaphore_wait(barrier, len(targets))
    ghosts = send(0, send_a, recv_a, next_id)
    ghosts.start()

    running[refs] = jnp.zeros((dofs, 128), F32)
    landed[cut] = jnp.zeros((dofs, 128), F32)
    field[ext] = jnp.zeros((dofs, 128), BF16)
    quarter = cols // 2
    sums[0, :quarter] = gram(load_parts[...], field[:owned].reshape(owned * dofs, 128))

    stiff_copy.wait()
    coupling_copy.wait()

    def form(c, carry):
        kind = arch[c]
        row = param[c]
        weight0, weight1 = theta[row, 0], theta[row, 1]
        couple_high, couple_low = parts(coupling[c])
        inverse_high, inverse_low = parts(inverse[kind])
        moved = (
            mm(inverse_high, couple_high)
            + mm(inverse_high, couple_low)
            + mm(inverse_low, couple_high)
        )
        moved_high, moved_low = parts(moved)
        left = jnp.concatenate([couple_high, couple_low, couple_high], axis=0)
        right = jnp.concatenate([moved_high, moved_high, moved_low], axis=0)
        for start in range(0, width, 128):
            rows = pl.ds(start, 128)
            bubble = mm_tn(left[:, start : start + 128], right)
            block = weight0 * (stiff[2 * kind, rows, :] - bubble) + weight1 * stiff[2 * kind + 1, rows, :]
            high, low = parts(block)
            blocks[c, rows, :width] = high
            blocks[c, rows, width:] = low
        return carry

    lax.fori_loop(0, comps, form, 0)

    ghosts.wait()

    def take_ghosts(g, carry):
        pair = recv_a[g]
        other = pltpu.roll(pair, cols, 1)
        field[owned + g] = split(jnp.where(left_lanes, pair, other))
        field[owned + half + g] = split(jnp.where(left_lanes, other, pair))
        return carry

    lax.fori_loop(0, half, take_ghosts, 0)

    apply()

    def pack_local(g, carry):
        one = fold(running[table[at_last + table[at_cut + g]]])
        two = fold(running[table[at_last + table[at_cut + half + g]]])
        send_l[g] = jnp.where(left_lanes, one, two)
        return carry

    pack_ghosts(send_p)
    back = send(1, send_p, recv_p, prev_id)
    back.start()
    lax.fori_loop(0, half, pack_local, 0)
    forth = send(2, send_l, recv_l, next_id)
    forth.start()
    back.wait()
    expand(recv_p)

    def natural(one, two, out, at):
        turned = jnp.concatenate([one, two], axis=0).T[:cols]
        if out is not None:
            out[:, at] = turned
        return turned

    def first_owned(b, carry):
        at = pl.ds(pl.multiple_of(b * 128, 128), 128)
        pair = []
        for p in (2 * b, 2 * b + 1):
            full = fold(running[table[at_last + p]] + landed[table[at_inv + p]])
            field[p] = split(full)
            pair.append(full)
        high, low = parts(natural(pair[0], pair[1], first_nat, at))
        first_parts[:cols, at] = high
        first_parts[cols:, at] = low
        return carry

    lax.fori_loop(0, owned // 2, first_owned, 0)
    forth.wait()
    expand(recv_l)

    def first_ghost(b, carry):
        at = pl.ds(pl.multiple_of(owned * dofs + b * 128, 128), 128)
        pair = []
        for g in (2 * b, 2 * b + 1):
            full = fold(running[table[at_last + owned + g]] + landed[g])
            field[owned + g] = split(full)
            pair.append(full)
        high, low = parts(natural(pair[0], pair[1], None, at))
        first_parts[:cols, at] = high
        first_parts[cols:, at] = low
        return carry

    lax.fori_loop(0, half, first_ghost, 0)

    first_field = field[:owned].reshape(owned * dofs, 128)
    sums[0, quarter : 2 * quarter] = gram(load_parts[...], first_field)
    sums[0, 2 * quarter : 3 * quarter] = gram(first_parts[:, : owned * dofs], first_field)

    apply()

    pack_ghosts(send_t)
    last_back = send(3, send_t, recv_t, prev_id)
    last_back.start()

    def second_partial(p, carry):
        field[p] = split(fold(running[table[at_last + p]]))
        return carry

    lax.fori_loop(0, ext, second_partial, 0)
    sums[0, 3 * quarter :] = gram(first_parts[...], field[:ext].reshape(ext * dofs, 128))

    def exchange(level):
        group = groups[level]
        copies = []
        for offset in range(1, group[2]):
            at = 3 * level + offset - 1
            copy = pltpu.make_async_remote_copy(
                src_ref=sums.at[level],
                dst_ref=slots.at[at],
                send_sem=sum_send.at[at],
                recv_sem=sum_recv.at[at],
                device_id=peer(group, offset),
                device_id_type=MESH,
            )
            copy.start()
            copies.append(copy)
        return copies

    def collect(level, copies):
        for copy in copies:
            copy.wait()
        value = sums[level]
        for number in range(len(copies)):
            value = value + slots[3 * level + number]
        if level + 1 < len(groups):
            sums[level + 1] = value
        else:
            grams[...] = value

    copies = exchange(0)
    last_back.wait()
    expand(recv_t)

    def second_owned(b, carry):
        at = pl.ds(pl.multiple_of(b * 128, 128), 128)
        pair = []
        for p in (2 * b, 2 * b + 1):
            pair.append(fold(running[table[at_last + p]] + landed[table[at_inv + p]]))
        natural(pair[0], pair[1], second_nat, at)
        return carry

    lax.fori_loop(0, owned // 2, second_owned, 0)
    for level in range(len(groups)):
        collect(level, copies)
        if level + 1 < len(groups):
            copies = exchange(level + 1)


def eliminate(matrix):
    size = matrix.shape[0]
    row_index = lax.broadcasted_iota(jnp.int32, (size, 1), 0)
    value = matrix
    for k in range(size):
        pivot_row = value[k : k + 1, :]
        column = value[:, k : k + 1]
        scaled = pivot_row * (1.0 / pivot_row[:, k : k + 1])
        value = jnp.where(row_index == k, scaled, value - column * scaled)
    return value


def combine_kernel(grams, loads, first, second, solution, residual):
    cols = loads.shape[0]
    half = cols // 2

    def matrix(number):
        packed = grams[number * half : (number + 1) * half, :]
        other = pltpu.roll(packed, cols, 1)
        return jnp.concatenate([packed, other], axis=0)[:, :cols]

    load_gram, cross, square, cube = [matrix(number) for number in range(4)]
    solved = eliminate(jnp.concatenate([cross, square, load_gram], axis=1))
    moved = solved[:, cols : 2 * cols]
    step = solved[:, 2 * cols :]
    inner = cube - exact(square, moved)
    rest = cross - exact(square, step)
    small = eliminate(jnp.concatenate([inner, rest], axis=1))
    second_weight = small[:, cols:]
    first_weight = step - exact(moved, second_weight)

    top_high, top_low = parts(first_weight.T)
    low_high, low_low = parts(second_weight.T)
    left = jnp.concatenate(
        [top_high, top_high, top_low, low_high, low_high, low_low], axis=1
    )

    def body(b, carry):
        at = pl.ds(pl.multiple_of(b * 512, 512), 512)
        load_piece, first_piece = loads[:, at], first[:, at]
        load_high, load_low = parts(load_piece)
        first_high, first_low = parts(first_piece)
        second_high, second_low = parts(second[:, at])
        solution[:, at] = mm(
            left,
            jnp.concatenate(
                [load_high, load_low, load_high, first_high, first_low, first_high], axis=0
            ),
        )
        residual[:, at] = load_piece - mm(
            left,
            jnp.concatenate(
                [first_high, first_low, first_high, second_high, second_low, second_high], axis=0
            ),
        )
        return carry

    lax.fori_loop(0, loads.shape[1] // 512, body, 0)


def local(
    sizes,
    port_loads,
    port_stiff,
    bubble_inverse,
    coupling,
    theta_table,
    comp_arch,
    comp_param,
    port_refs,
    slot_mask,
    cut_source,
):
    cols = port_loads.shape[0]
    comps, slot_count = port_refs.shape
    width = port_stiff.shape[2]
    dofs = width // slot_count
    cut = cut_source.shape[1]
    owned = port_loads.shape[1] // dofs
    refs = comps * slot_count
    ext = owned + cut
    archs, terms = port_stiff.shape[:2]

    flat = port_refs.reshape(-1)
    alive = slot_mask.reshape(-1) != 0
    position = jnp.arange(refs, dtype=jnp.int32)
    picks = jnp.where(alive, flat, ext)
    earlier = (flat[:, None] == flat[None, :]) & alive[None, :] & (position[None, :] < position[:, None])
    previous = jnp.max(jnp.where(earlier, position[None, :], -1), axis=1)
    previous = jnp.where((previous < 0) | ~alive, refs, previous)
    ports = jnp.arange(ext, dtype=jnp.int32)
    last = jnp.max(jnp.where(picks[None, :] == ports[:, None], position[None, :], -1), axis=1)
    last = jnp.where(last < 0, refs, last)
    sources = cut_source[0]
    matches = sources[None, :] == ports[:owned, None]
    back = jnp.min(jnp.where(matches, jnp.arange(cut, dtype=jnp.int32)[None, :], cut), axis=1)
    table = jnp.concatenate([picks, previous, last, sources, back])

    groups = peers_of(sizes)
    levels = len(groups)
    smem = pl.BlockSpec(memory_space=pltpu.SMEM)
    vmem = pl.BlockSpec(memory_space=pltpu.VMEM)
    hbm = pl.BlockSpec(memory_space=pl.ANY)
    exchange = pltpu.VMEM((cut // 2, dofs, 128), F32)
    half = cols // 2
    flops = 2 * comps * cols * width * width * 9
    first, second, grams = pl.pallas_call(
        functools.partial(system_kernel, sizes, groups),
        out_shape=(
            jax.ShapeDtypeStruct(port_loads.shape, F32),
            jax.ShapeDtypeStruct(port_loads.shape, F32),
            jax.ShapeDtypeStruct((4 * half, 128), F32),
        ),
        in_specs=[smem, smem, smem, smem, vmem, hbm, hbm, hbm],
        out_specs=(vmem, vmem, vmem),
        scratch_shapes=[
            pltpu.VMEM(port_loads.shape, F32),
            pltpu.VMEM((archs * terms, width, width), F32),
            pltpu.VMEM(coupling.shape, F32),
            pltpu.VMEM((comps, width, 2 * width), BF16),
            pltpu.VMEM((ext + 1, dofs, 128), BF16),
            pltpu.VMEM((refs + 1, dofs, 128), F32),
            pltpu.VMEM((2 * cols, owned * dofs), BF16),
            pltpu.VMEM((2 * cols, ext * dofs), BF16),
            pltpu.VMEM((cut + 1, dofs, 128), F32),
        ]
        + [exchange] * 8
        + [
            pltpu.VMEM((levels, 4 * half, 128), F32),
            pltpu.VMEM((3 * levels, 4 * half, 128), F32),
            pltpu.SemaphoreType.DMA((3,)),
            pltpu.SemaphoreType.DMA((4,)),
            pltpu.SemaphoreType.DMA((4,)),
            pltpu.SemaphoreType.DMA((3 * levels,)),
            pltpu.SemaphoreType.DMA((3 * levels,)),
        ],
        compiler_params=pltpu.CompilerParams(
            collective_id=0, has_side_effects=True, vmem_limit_bytes=60 * 1024 * 1024
        ),
        cost_estimate=pl.CostEstimate(flops=flops, bytes_accessed=12 << 20, transcendentals=0),
        name="system",
    )(
        table,
        comp_arch,
        comp_param,
        theta_table,
        bubble_inverse,
        port_loads,
        port_stiff.reshape(archs * terms, width, width),
        coupling,
    )
    return pl.pallas_call(
        combine_kernel,
        out_shape=(
            jax.ShapeDtypeStruct(port_loads.shape, F32),
            jax.ShapeDtypeStruct(port_loads.shape, F32),
        ),
        in_specs=[vmem, vmem, vmem, vmem],
        out_specs=(vmem, vmem),
        compiler_params=pltpu.CompilerParams(vmem_limit_bytes=60 * 1024 * 1024),
        cost_estimate=pl.CostEstimate(flops=1 << 28, bytes_accessed=4 << 20, transcendentals=0),
        name="combine",
    )(grams, port_loads, first, second)


def solution(mesh):
    sizes = (mesh.shape["gx"], mesh.shape["gy"])
    placed = (
        P(None, ("gx", "gy")),
        P(),
        P(),
        P(("gx", "gy"), None, None),
        P(),
        P(("gx", "gy")),
        P(("gx", "gy")),
        P(("gx", "gy"), None),
        P(("gx", "gy"), None),
        P(("gx", "gy"), None),
    )
    return jax.shard_map(
        functools.partial(local, sizes),
        mesh=mesh,
        in_specs=placed,
        out_specs=(P(None, ("gx", "gy")), P(None, ("gx", "gy"))),
        check_vma=False,
    )
```

```python
import functools

import jax
import jax.numpy as jnp
from jax import lax
from jax.experimental import pallas as pl
from jax.experimental.pallas import tpu as pltpu
from jax.sharding import PartitionSpec as P

MESH = pl.DeviceIdType.MESH
APPLY = 4
FORM = 2
F32 = jnp.float32
BF16 = jnp.bfloat16


def parts(value):
    high = value.astype(BF16)
    return high, (value - high.astype(F32)).astype(BF16)


def mm(left, right):
    return jnp.dot(left, right, preferred_element_type=F32)


def mm_tn(left, right):
    return lax.dot_general(left, right, (((0,), (0,)), ((), ())), preferred_element_type=F32)


def exact(left, right):
    return lax.dot_general(
        left,
        right,
        (((1,), (0,)), ((), ())),
        precision=lax.Precision.HIGHEST,
        preferred_element_type=F32,
    )


def peers_of(mesh_sizes):
    sizes_x, sizes_y = mesh_sizes
    groups = []
    stride = 1
    for size in (2, 4):
        if sizes_y // stride > 1:
            size = min(size, sizes_y // stride)
            groups.append(("gy", stride, size))
            stride *= size
    if sizes_y // stride > 1:
        groups.append(("gy", stride, sizes_y // stride))
    if sizes_x > 1:
        groups.append(("gx", 1, sizes_x))
    return groups


def system_kernel(
    sizes,
    groups,
    arch,
    param,
    theta,
    refs_hbm,
    mask_hbm,
    cut_hbm,
    inverse_hbm,
    loads_hbm,
    stiff_hbm,
    coupling_hbm,
    first_out,
    second_out,
    small_out,
    refs_in,
    mask_in,
    cut_in,
    inverse,
    loads,
    stiff_top,
    stiff_low,
    coupling,
    couple_parts,
    blocks,
    field,
    running,
    load_parts,
    first_parts,
    second_parts,
    landed,
    send_a,
    recv_a,
    send_l,
    recv_l,
    send_p,
    recv_p,
    send_t,
    recv_t,
    sums,
    slots,
    index_rows,
    index,
    load_sem,
    send_sem,
    recv_sem,
    sum_send,
    sum_recv,
):
    sizes_x, sizes_y = sizes
    comps = coupling.shape[0]
    bubbles = coupling.shape[1]
    cols, dofs = loads.shape[0], field.shape[2] // 2
    owned = loads.shape[1] // dofs
    slot_count = refs_in.shape[0]
    refs = comps * slot_count
    width = slot_count * dofs
    cut = cut_in.shape[1]
    half = cut // 2
    ext = owned + cut
    quarter_comps = comps // 4
    PICK, PREV, LAST, CUT, BACK = range(5)

    my_x, my_y = lax.axis_index("gx"), lax.axis_index("gy")
    here = my_x * sizes_y + my_y
    total = sizes_x * sizes_y
    after = lax.rem(here + 1, total)
    before = lax.rem(here + total - 1, total)
    next_id = (after // sizes_y, lax.rem(after, sizes_y))
    prev_id = (before // sizes_y, lax.rem(before, sizes_y))

    def peer(group, offset):
        axis, stride, size = group
        if axis == "gx":
            return (lax.rem(my_x + offset, size), my_y)
        place = lax.rem(my_y // stride, size)
        other = lax.rem(place + offset, size)
        return (my_x, my_y + (other - place) * stride)

    small_copies = []
    for number, (source, target) in enumerate(
        ((refs_hbm, refs_in), (mask_hbm, mask_in), (cut_hbm, cut_in), (inverse_hbm, inverse))
    ):
        copy = pltpu.make_async_copy(source, target, load_sem.at[1 + number])
        copy.start()
        small_copies.append(copy)
    load_copy = pltpu.make_async_copy(loads_hbm, loads, load_sem.at[0])
    load_copy.start()
    coupling_copy = pltpu.make_async_copy(coupling_hbm, coupling, load_sem.at[5])
    coupling_copy.start()
    middle_at = width // 2
    bands = ((0, 0, stiff_top), (middle_at, middle_at, stiff_low))
    stiff_copies = []
    for band, (start, begin, target) in enumerate(bands):
        at = (slice(None), pl.ds(start, middle_at), pl.ds(begin, width - begin))
        copy = pltpu.make_async_copy(stiff_hbm.at[at], target, load_sem.at[6 + band])
        copy.start()
        stiff_copies.append(copy)

    barrier = pltpu.get_barrier_semaphore()
    targets = [next_id, prev_id]
    for group in groups:
        for offset in range(1, group[2]):
            targets.append(peer(group, offset))
    for target in targets:
        pl.semaphore_signal(barrier, inc=1, device_id=target, device_id_type=MESH)

    left_lanes = lax.broadcasted_iota(jnp.int32, (cols, 128), 1) < dofs
    left_both = lax.broadcasted_iota(jnp.int32, (2 * cols, 128), 1) < dofs

    def fold(value):
        return value + pltpu.roll(value, dofs, 1)

    def keep(place, full):
        field[place, :cols], field[place, cols:] = parts(full)

    def keep_pair(target, at, one, two):
        target[:cols, at], target[cols:, at] = parts(jnp.where(left_lanes, one, two))

    def lanes_of(b):
        return pl.ds(pl.multiple_of(b * 128, 128), 128)

    def send(number, source, target_ref, device):
        return pltpu.make_async_remote_copy(
            src_ref=source,
            dst_ref=target_ref,
            send_sem=send_sem.at[number],
            recv_sem=recv_sem.at[number],
            device_id=device,
            device_id_type=MESH,
        )

    def loop(count, unroll, body):
        def step(b, carry):
            for u in range(unroll):
                body(b * unroll + u)
            return carry

        lax.fori_loop(0, count // unroll, step, 0)

    def unpack(pair):
        other = pltpu.roll(pair, dofs, 1)
        return jnp.where(left_lanes, pair, other), jnp.where(left_lanes, other, pair)

    def expand(received):
        def body(g):
            landed[g], landed[g + half] = unpack(received[g])

        loop(half, 4, body)

    def widen(row):
        return jnp.concatenate(
            [row, jnp.zeros((row.shape[0], 128 - row.shape[1]), row.dtype)], axis=1
        )

    for copy in small_copies:
        copy.wait()
    picks = widen(jnp.where(mask_in[...] != 0, refs_in[...], ext)).T[:comps]
    comp_lane = lax.broadcasted_iota(jnp.int32, (comps, refs), 1)
    comp_row = lax.broadcasted_iota(jnp.int32, (comps, refs), 0)
    wide = jnp.zeros((comps, refs), jnp.int32)
    for j in range(slot_count):
        wide = jnp.where(comp_lane == comp_row * slot_count + j, picks[:, j : j + 1], wide)
    pick_row = jnp.sum(wide, axis=0, keepdims=True)
    pick_row = jnp.clip(pick_row, 0, ext)
    down = lax.broadcasted_iota(jnp.int32, (refs, 128), 0)
    across = lax.broadcasted_iota(jnp.int32, (refs, 128), 1)
    pick_down = jnp.broadcast_to(pick_row, (refs, refs)).T
    same = (pick_down == pick_row) & (pick_down < ext) & (down < across)
    previous = jnp.max(jnp.where(same, down, -1), axis=0, keepdims=True)
    final = jnp.max(jnp.where((pick_down == across) & (across < ext), down, -1), axis=0, keepdims=True)
    cut_rows = widen(cut_in[...])
    lane_row = lax.broadcasted_iota(jnp.int32, (1, 128), 1)
    cut_marked = jnp.where(lane_row < cut, cut_rows, -1)
    cut_down = jnp.broadcast_to(cut_marked, (refs, 128)).T
    back_row = jnp.max(jnp.where(cut_down == across, down, -1), axis=0, keepdims=True)
    index_rows[PICK : PICK + 1, :] = pick_row
    index_rows[PREV : PREV + 1, :] = jnp.where(previous < 0, refs, previous)
    index_rows[LAST : LAST + 1, :] = jnp.where(final < 0, refs, final)
    index_rows[CUT : CUT + 1, :] = jnp.clip(cut_rows, 0, owned - 1)
    index_rows[BACK : BACK + 1, :] = jnp.where(back_row < 0, cut, back_row)
    index_copy = pltpu.make_async_copy(index_rows, index, load_sem.at[10])
    index_copy.start()
    def pack(target, source):
        def body(g):
            target[g] = jnp.where(left_lanes, source(g), source(g + half))

        loop(half, 4, body)

    def ghost_total(g):
        return running[index[LAST, owned + g]]

    def apply(start, count):
        def pick(c):
            first = c * slot_count
            return jnp.concatenate(
                [
                    jnp.where(
                        left_both, field[index[PICK, first + j]], field[index[PICK, first + j + 1]]
                    )
                    for j in range(0, slot_count, 2)
                ],
                axis=1,
            )

        def times(c, left, side):
            at = side * width
            near = pl.ds(at, middle_at)
            far = pl.ds(at + middle_at, middle_at)
            return jnp.concatenate(
                [
                    mm(left[:, :middle_at], blocks[c, :middle_at, near])
                    + mm_nt(left[:, middle_at:], blocks[c, :middle_at, far]),
                    mm(left, blocks[c, :, far]),
                ],
                axis=1,
            )

        def multiply(c, picked):
            both = times(c, picked, 0)
            return both[:cols] + both[cols:] + times(c, picked[:cols], 1)

        def add(c, product):
            first = c * slot_count
            for j in range(0, slot_count, 2):
                one, two = unpack(product[:, j * dofs : (j + 2) * dofs])
                running[first + j] = running[index[PREV, first + j]] + one
                running[first + j + 1] = running[index[PREV, first + j + 1]] + two

        def body(b, carry):
            places = [start + b * APPLY + u for u in range(APPLY)]
            picked = [pick(c) for c in places]
            products = [multiply(c, value) for c, value in zip(places, picked)]
            for c, product in zip(places, products):
                add(c, product)
            return carry

        lax.fori_loop(0, count // APPLY, body, 0)

    def gram(left, right):
        both = mm_nt(left, right)
        rows = both[:cols] + both[cols:]
        full = fold(rows)
        return jnp.where(left_lanes[: cols // 2], full[: cols // 2], full[cols // 2 :])

    def reduction(number, value):
        for level, group in enumerate(groups):
            sums[number, level] = value
            copies = []
            for offset in range(1, group[2]):
                at = 3 * level + offset - 1
                sem = number * 3 * len(groups) + at
                copy = pltpu.make_async_remote_copy(
                    src_ref=sums.at[number, level],
                    dst_ref=slots.at[number, at],
                    send_sem=sum_send.at[sem],
                    recv_sem=sum_recv.at[sem],
                    device_id=peer(group, offset),
                    device_id_type=MESH,
                )
                copy.start()
                copies.append(copy)
            yield None
            for copy in copies:
                copy.wait()
            for offset in range(1, group[2]):
                value = value + slots[number, 3 * level + offset - 1]
        yield value

    def advance(steps):
        return next(steps)

    def square_of(packed):
        other = pltpu.roll(packed, cols, 1)
        return jnp.concatenate([packed, other], axis=0)[:, :cols]

    load_copy.wait()

    def spread(b):
        at = lanes_of(b)
        piece = loads[:, at]
        load_parts[:cols, at], load_parts[cols:, at] = parts(piece)
        running[2 * b], running[2 * b + 1] = one, two = unpack(piece)
        keep(2 * b, one)
        keep(2 * b + 1, two)

    loop(owned // 2, 4, spread)
    index_copy.wait()
    pack(send_a, lambda g: running[index[CUT, g]])
    pl.semaphore_wait(barrier, len(targets))
    ghosts = send(0, send_a, recv_a, next_id)
    ghosts.start()

    running[refs] = jnp.zeros((cols, 128), F32)
    landed[cut] = jnp.zeros((cols, 128), F32)
    field[ext] = jnp.zeros((2 * cols, 128), BF16)
    load_steps = reduction(0, gram(load_parts[...], load_parts[...]))
    load_gram = advance(load_steps)

    coupling_copy.wait()

    def move(c):
        couple_high, couple_low = parts(coupling[c])
        inverse_high, inverse_low = parts(inverse[arch[c]])
        moved = (
            mm(inverse_high, couple_high)
            + mm(inverse_high, couple_low)
            + mm(inverse_low, couple_high)
        )
        moved_high, moved_low = parts(moved)
        couple_parts[c, :bubbles] = couple_high
        couple_parts[c, bubbles : 2 * bubbles] = couple_low
        couple_parts[c, 2 * bubbles : 3 * bubbles] = moved_high
        couple_parts[c, 3 * bubbles :] = moved_low

    loop(comps, 2, move)

    def form(band, c):
        kind = arch[c]
        weight0, weight1 = theta[0, param[c]], theta[1, param[c]]
        first_row, begin, stiff = bands[band]
        right_of = pl.ds(begin, width - begin)
        moved_high = couple_parts[c, 2 * bubbles : 3 * bubbles, right_of]
        moved_low = couple_parts[c, 3 * bubbles :, right_of]
        moved = jnp.concatenate([moved_high, moved_high, moved_low], axis=0)
        for start in range(first_row, first_row + middle_at, 128):
            rows = pl.ds(start, 128)
            couple_both = couple_parts[c, : 2 * bubbles, rows]
            bubble = mm_tn(jnp.concatenate([couple_both, couple_both[:bubbles]], axis=0), moved)
            block = (
                weight0 * (stiff[2 * kind, pl.ds(start - first_row, 128), :] - bubble)
                + weight1 * stiff[2 * kind + 1, pl.ds(start - first_row, 128), :]
            )
            high, low = parts(block)
            blocks[c, rows, right_of] = high
            blocks[c, rows, pl.ds(width + begin, width - begin)] = low

    for band in range(len(bands)):
        stiff_copies[band].wait()
        loop(comps, FORM, functools.partial(form, band))
        if load_gram is None:
            load_gram = advance(load_steps)
    while load_gram is None:
        load_gram = advance(load_steps)

    ghosts.wait()

    def take_ghosts(g):
        one, two = unpack(recv_a[g])
        keep(owned + g, one)
        keep(owned + half + g, two)

    loop(half, 4, take_ghosts)

    apply(0, comps)

    pack(send_p, ghost_total)
    back = send(1, send_p, recv_p, prev_id)
    back.start()
    pack(send_l, lambda g: running[index[LAST, index[CUT, g]]])
    forth = send(2, send_l, recv_l, next_id)
    forth.start()
    back.wait()
    expand(recv_p)

    def first_owned(b):
        one, two = [running[index[LAST, p]] + landed[index[BACK, p]] for p in (2 * b, 2 * b + 1)]
        keep(2 * b, one)
        keep(2 * b + 1, two)
        keep_pair(first_parts, lanes_of(b), one, two)

    loop(owned // 2, 4, first_owned)
    forth.wait()
    expand(recv_l)

    def first_ghost(b):
        one, two = [ghost_total(g) + landed[g] for g in (2 * b, 2 * b + 1)]
        keep(owned + 2 * b, one)
        keep(owned + 2 * b + 1, two)
        keep_pair(first_parts, lanes_of(owned // 2 + b), one, two)

    loop(half, 4, first_ghost)

    first_owned_parts = first_parts[:, : owned * dofs]
    first_out[...] = first_owned_parts
    middle = [
        reduction(1, gram(load_parts[...], first_owned_parts)),
        reduction(2, gram(first_owned_parts, first_owned_parts)),
    ]
    found = [advance(steps) for steps in middle]
    for number in range(4):
        apply(number * quarter_comps, quarter_comps)
        found = [got if got is not None else advance(steps) for got, steps in zip(found, middle)]

    pack(send_t, ghost_total)
    last_back = send(3, send_t, recv_t, prev_id)
    last_back.start()

    def second_partial(b):
        one, two = [running[index[LAST, p]] for p in (2 * b, 2 * b + 1)]
        keep_pair(second_parts, lanes_of(b), one, two)

    loop(ext // 2, 4, second_partial)
    cube_steps = reduction(3, gram(first_parts[...], second_parts[...]))
    cube = advance(cube_steps)
    while any(got is None for got in found):
        found = [got if got is not None else advance(steps) for got, steps in zip(found, middle)]
    load_gram, cross, square = [square_of(packed) for packed in (load_gram, *found)]
    eliminated = elimination(
        [jnp.concatenate([cross, square], axis=1), jnp.concatenate([load_gram, load_gram], axis=1)],
        len(groups),
    )
    solved = None
    while cube is None:
        solved = next(eliminated, solved)
        cube = advance(cube_steps)
    for solved in eliminated:
        pass
    moved = solved[0][:, cols:]
    step = solved[1][:, :cols]
    small_out[0, :, cols:] = cross - exact(square, step)
    small_out[1, :, :cols] = moved
    small_out[1, :, cols:] = step
    small_out[0, :, :cols] = square_of(cube) - exact(square, moved)

    last_back.wait()
    expand(recv_t)

    def second_owned(b):
        one, two = [running[index[LAST, p]] + landed[index[BACK, p]] for p in (2 * b, 2 * b + 1)]
        keep_pair(second_out, lanes_of(b), one, two)

    loop(owned // 2, 4, second_owned)


def elimination(tiles, chunks=1, block=8):
    size = tiles[0].shape[0]
    row_index = lax.broadcasted_iota(jnp.int32, (size, 1), 0)
    steps = size // block
    for chunk in range(chunks):
        for k in range(chunk * steps // chunks * block, (chunk + 1) * steps // chunks * block, block):
            wide = [jnp.broadcast_to(tiles[0][:, k + j : k + j + 1], tiles[0].shape) for j in range(block)]
            pivots = [[wide[j][k + i : k + i + 1] for j in range(block)] for i in range(block)]
            rows = [[tile[k + i : k + i + 1] for tile in tiles] for i in range(block)]
            for i in range(block):
                scale = 1.0 / pivots[i][i]
                rows[i] = [row * scale for row in rows[i]]
                for j in range(i + 1, block):
                    pivots[i][j] = pivots[i][j] * scale
                for m in range(i + 1, block):
                    factor = pivots[m][i]
                    rows[m] = [row - factor * other for row, other in zip(rows[m], rows[i])]
                    for j in range(i + 1, block):
                        pivots[m][j] = pivots[m][j] - factor * pivots[i][j]
            for i in range(block - 1, 0, -1):
                for m in range(i):
                    rows[m] = [row - pivots[m][i] * other for row, other in zip(rows[m], rows[i])]
            out = []
            for number, tile in enumerate(tiles):
                new = tile
                for j in range(block):
                    new = new - wide[j] * rows[j][number]
                for j in range(block):
                    new = jnp.where(row_index == k + j, rows[j][number], new)
                out.append(new)
            tiles = out
        yield tiles


def combine_kernel(small, loads_hbm, first_hbm, second_hbm, solution_hbm, residual_hbm, loads, first, second, solution, residual, sems):
    cols = loads.shape[0]
    copies = []
    for number, (source, target) in enumerate(
        ((loads_hbm, loads), (first_hbm, first), (second_hbm, second))
    ):
        copy = pltpu.make_async_copy(source, target, sems.at[number])
        copy.start()
        copies.append(copy)

    ((solved,),) = elimination([small[0]])
    second_weight = solved[:, cols:]
    first_weight = small[1, :, cols:] - exact(small[1, :, :cols], second_weight)

    top_high, top_low = parts(first_weight.T)
    low_high, low_low = parts(second_weight.T)
    left = jnp.concatenate([top_high, top_high, top_low, low_high, low_high, low_low], axis=1)
    for copy in copies:
        copy.wait()

    chunk = 512
    writes = []
    for b in range(loads.shape[1] // chunk):
        at = pl.ds(b * chunk, chunk)
        load_piece, first_piece, second_piece = loads[:, at], first[:, at], second[:, at]
        load_high, load_low = parts(load_piece)
        solution[:, at] = mm(
            left,
            jnp.concatenate(
                [load_high, load_low, load_high, first_piece, first_piece[:cols]], axis=0
            ),
        )
        residual[:, at] = load_piece - mm(
            left,
            jnp.concatenate(
                [first_piece, first_piece[:cols], second_piece, second_piece[:cols]], axis=0
            ),
        )
        for number, (source, target) in enumerate(
            ((solution, solution_hbm), (residual, residual_hbm))
        ):
            copy = pltpu.make_async_copy(
                source.at[:, at], target.at[:, at], sems.at[3 + 2 * b + number]
            )
            copy.start()
            writes.append(copy)
    for copy in writes:
        copy.wait()


def mm_nt(left, right):
    return lax.dot_general(left, right, (((1,), (1,)), ((), ())), preferred_element_type=F32)


def local(
    sizes,
    port_loads,
    port_stiff,
    bubble_inverse,
    coupling,
    theta_table,
    comp_arch,
    comp_param,
    port_refs,
    slot_mask,
    cut_source,
):
    cols = port_loads.shape[0]
    comps, slot_count = port_refs.shape
    width = port_stiff.shape[2]
    dofs = width // slot_count
    cut = cut_source.shape[1]
    owned = port_loads.shape[1] // dofs
    refs = comps * slot_count
    ext = owned + cut
    archs, terms = port_stiff.shape[:2]
    bubbles = coupling.shape[1]

    groups = peers_of(sizes)
    levels = len(groups)
    smem = pl.BlockSpec(memory_space=pltpu.SMEM)
    vmem = pl.BlockSpec(memory_space=pltpu.VMEM)
    hbm = pl.BlockSpec(memory_space=pl.ANY)
    exchange = pltpu.VMEM((cut // 2, cols, 128), F32)
    half = cols // 2
    flops = 2 * comps * cols * width * width * 9
    first, second, small = pl.pallas_call(
        functools.partial(system_kernel, sizes, groups),
        out_shape=(
            jax.ShapeDtypeStruct((2 * cols, owned * dofs), BF16),
            jax.ShapeDtypeStruct((2 * cols, owned * dofs), BF16),
            jax.ShapeDtypeStruct((2, cols, 2 * cols), F32),
        ),
        in_specs=[smem, smem, smem] + [hbm] * 7,
        out_specs=(vmem, vmem, vmem),
        scratch_shapes=[
            pltpu.VMEM((slot_count, comps), jnp.int32),
            pltpu.VMEM((slot_count, comps), jnp.int32),
            pltpu.VMEM(cut_source.shape, jnp.int32),
            pltpu.VMEM(bubble_inverse.shape, F32),
            pltpu.VMEM(port_loads.shape, F32),
            pltpu.VMEM((archs * terms, width // 2, width), F32),
            pltpu.VMEM((archs * terms, width // 2, width // 2), F32),
            pltpu.VMEM(coupling.shape, F32),
            pltpu.VMEM((comps, 4 * bubbles, width), BF16),
            pltpu.VMEM((comps, width, 2 * width), BF16),
            pltpu.VMEM((ext + 1, 2 * cols, 128), BF16),
            pltpu.VMEM((refs + 1, cols, 128), F32),
            pltpu.VMEM((2 * cols, owned * dofs), BF16),
            pltpu.VMEM((2 * cols, ext * dofs), BF16),
            pltpu.VMEM((2 * cols, ext * dofs), BF16),
            pltpu.VMEM((cut + 1, cols, 128), F32),
        ]
        + [exchange] * 8
        + [
            pltpu.VMEM((4, levels, half, 128), F32),
            pltpu.VMEM((4, 3 * levels, half, 128), F32),
            pltpu.VMEM((8, 128), jnp.int32),
            pltpu.SMEM((8, 128), jnp.int32),
            pltpu.SemaphoreType.DMA((11,)),
            pltpu.SemaphoreType.DMA((4,)),
            pltpu.SemaphoreType.DMA((4,)),
            pltpu.SemaphoreType.DMA((12 * levels,)),
            pltpu.SemaphoreType.DMA((12 * levels,)),
        ],
        compiler_params=pltpu.CompilerParams(
            collective_id=0, has_side_effects=True, vmem_limit_bytes=60 * 1024 * 1024
        ),
        cost_estimate=pl.CostEstimate(flops=flops, bytes_accessed=12 << 20, transcendentals=0),
        name="system",
    )(
        comp_arch,
        comp_param,
        theta_table.T,
        port_refs.T,
        slot_mask.T,
        cut_source,
        bubble_inverse,
        port_loads,
        port_stiff.reshape(archs * terms, width, width),
        coupling,
    )
    return pl.pallas_call(
        combine_kernel,
        out_shape=(
            jax.ShapeDtypeStruct(port_loads.shape, F32),
            jax.ShapeDtypeStruct(port_loads.shape, F32),
        ),
        in_specs=[vmem, hbm, hbm, hbm],
        out_specs=(hbm, hbm),
        scratch_shapes=[
            pltpu.VMEM(port_loads.shape, F32),
            pltpu.VMEM((2 * cols, owned * dofs), BF16),
            pltpu.VMEM((2 * cols, owned * dofs), BF16),
            pltpu.VMEM(port_loads.shape, F32),
            pltpu.VMEM(port_loads.shape, F32),
            pltpu.SemaphoreType.DMA((3 + 2 * (owned * dofs // 512),)),
        ],
        compiler_params=pltpu.CompilerParams(vmem_limit_bytes=60 * 1024 * 1024),
        cost_estimate=pl.CostEstimate(flops=1 << 28, bytes_accessed=4 << 20, transcendentals=0),
        name="combine",
    )(small, port_loads, first, second)


def solution(mesh):
    sizes = (mesh.shape["gx"], mesh.shape["gy"])
    placed = (
        P(None, ("gx", "gy")),
        P(),
        P(),
        P(("gx", "gy"), None, None),
        P(),
        P(("gx", "gy")),
        P(("gx", "gy")),
        P(("gx", "gy"), None),
        P(("gx", "gy"), None),
        P(("gx", "gy"), None),
    )
    return jax.shard_map(
        functools.partial(local, sizes),
        mesh=mesh,
        in_specs=placed,
        out_specs=(P(None, ("gx", "gy")), P(None, ("gx", "gy"))),
        check_vma=False,
    )
```

```python
import functools
import itertools

import jax
import jax.numpy as jnp
from jax import lax
from jax.experimental import pallas as pl
from jax.experimental.pallas import tpu as pltpu
from jax.sharding import PartitionSpec as P

MESH = pl.DeviceIdType.MESH
APPLY = 8
FORM = 8
F32 = jnp.float32
BF16 = jnp.bfloat16


def parts(value):
    high = value.astype(BF16)
    return high, (value - high.astype(F32)).astype(BF16)


def mm(left, right):
    return jnp.dot(left, right, preferred_element_type=F32)


def mm_tn(left, right):
    return lax.dot_general(left, right, (((0,), (0,)), ((), ())), preferred_element_type=F32)


def exact(left, right):
    return lax.dot_general(
        left,
        right,
        (((1,), (0,)), ((), ())),
        precision=lax.Precision.HIGHEST,
        preferred_element_type=F32,
    )


def phases_of(mesh_sizes):
    sizes_x, sizes_y = mesh_sizes
    axes = []
    stride = 1
    for size in (2, 4, sizes_y):
        size = min(size, sizes_y // stride)
        if size > 1:
            axes.append(("gy", stride, size))
            stride *= size
    if sizes_x > 1:
        axes.append(("gx", 1, sizes_x))

    def phase(*members):
        steps = itertools.product(*[range(member[2]) for member in members])
        return [list(zip(members, step)) for step in steps if any(step)]

    return [phase(axis) for axis in axes], [phase(*axes[:2]), phase(*axes[2:])]


def system_kernel(
    sizes,
    phases,
    arch,
    param,
    theta,
    refs_hbm,
    mask_hbm,
    cut_hbm,
    inverse_hbm,
    loads_hbm,
    stiff_hbm,
    coupling_hbm,
    first_hbm,
    second_hbm,
    small_out,
    refs_in,
    mask_in,
    cut_in,
    inverse,
    loads,
    stiff_top,
    stiff_low,
    coupling,
    couple_parts,
    blocks,
    field,
    running,
    load_parts,
    first_parts,
    second_parts,
    second_out,
    landed,
    send_a,
    recv_a,
    send_l,
    recv_l,
    send_p,
    recv_p,
    send_t,
    recv_t,
    index_rows,
    index,
    load_sem,
    send_sem,
    recv_sem,
    *reducers,
):
    sizes_x, sizes_y = sizes
    comps = coupling.shape[0]
    bubbles = coupling.shape[1]
    cols, dofs = loads.shape[0], field.shape[2] // 2
    owned = loads.shape[1] // dofs
    slot_count = refs_in.shape[0]
    refs = comps * slot_count
    width = slot_count * dofs
    cut = cut_in.shape[1]
    half = cut // 2
    ext = owned + cut
    quarter_comps = comps // 4
    PICK, PREV, LAST, CUT, BACK = range(5)

    my_x, my_y = lax.axis_index("gx"), lax.axis_index("gy")
    here = my_x * sizes_y + my_y
    total = sizes_x * sizes_y
    after = lax.rem(here + 1, total)
    before = lax.rem(here + total - 1, total)
    next_id = (after // sizes_y, lax.rem(after, sizes_y))
    prev_id = (before // sizes_y, lax.rem(before, sizes_y))

    def peer(offset):
        x, y = my_x, my_y
        for (axis, stride, size), steps in offset:
            if steps and axis == "gx":
                x = lax.rem(my_x + steps, size)
            elif steps:
                place = lax.rem(my_y // stride, size)
                y = y + (lax.rem(place + steps, size) - place) * stride
        return (x, y)

    small_copies = []
    for number, (source, target) in enumerate(
        ((refs_hbm, refs_in), (mask_hbm, mask_in), (cut_hbm, cut_in), (inverse_hbm, inverse))
    ):
        copy = pltpu.make_async_copy(source, target, load_sem.at[1 + number])
        copy.start()
        small_copies.append(copy)
    load_copy = pltpu.make_async_copy(loads_hbm, loads, load_sem.at[0])
    load_copy.start()
    coupling_copy = pltpu.make_async_copy(coupling_hbm, coupling, load_sem.at[5])
    coupling_copy.start()
    middle_at = width // 2
    bands = ((0, 0, stiff_top), (middle_at, middle_at, stiff_low))
    stiff_copies = []
    for band, (start, begin, target) in enumerate(bands):
        at = (slice(None), pl.ds(start, middle_at), pl.ds(begin, width - begin))
        copy = pltpu.make_async_copy(stiff_hbm.at[at], target, load_sem.at[6 + band])
        copy.start()
        stiff_copies.append(copy)

    barrier = pltpu.get_barrier_semaphore()
    targets = [next_id, prev_id]
    targets += [peer(offset) for phase in phases[1] for offset in phase]
    for target in targets:
        pl.semaphore_signal(barrier, inc=1, device_id=target, device_id_type=MESH)

    left_lanes = lax.broadcasted_iota(jnp.int32, (cols, 128), 1) < dofs
    left_both = lax.broadcasted_iota(jnp.int32, (2 * cols, 128), 1) < dofs

    def fold(value):
        return value + pltpu.roll(value, dofs, 1)

    def keep(place, full):
        field[place, :cols], field[place, cols:] = parts(full)

    def keep_pair(target, at, one, two):
        target[:cols, at], target[cols:, at] = parts(jnp.where(left_lanes, one, two))

    def lanes_of(b):
        return pl.ds(pl.multiple_of(b * 128, 128), 128)

    def send(number, source, target_ref, device):
        return pltpu.make_async_remote_copy(
            src_ref=source,
            dst_ref=target_ref,
            send_sem=send_sem.at[number],
            recv_sem=recv_sem.at[number],
            device_id=device,
            device_id_type=MESH,
        )

    def loop(count, unroll, body):
        def step(b, carry):
            for u in range(unroll):
                body(b * unroll + u)
            return carry

        lax.fori_loop(0, count // unroll, step, 0)

    def unpack(pair):
        other = pltpu.roll(pair, dofs, 1)
        return jnp.where(left_lanes, pair, other), jnp.where(left_lanes, other, pair)

    def expand(received):
        def body(g):
            landed[g], landed[g + half] = unpack(received[g])

        loop(half, 4, body)

    def widen(row):
        return jnp.concatenate(
            [row, jnp.zeros((row.shape[0], 128 - row.shape[1]), row.dtype)], axis=1
        )

    for copy in small_copies:
        copy.wait()
    picks = widen(jnp.where(mask_in[...] != 0, refs_in[...], ext)).T[:comps]
    comp_lane = lax.broadcasted_iota(jnp.int32, (comps, refs), 1)
    comp_row = lax.broadcasted_iota(jnp.int32, (comps, refs), 0)
    wide = jnp.zeros((comps, refs), jnp.int32)
    for j in range(slot_count):
        wide = jnp.where(comp_lane == comp_row * slot_count + j, picks[:, j : j + 1], wide)
    pick_row = jnp.sum(wide, axis=0, keepdims=True)
    pick_row = jnp.clip(pick_row, 0, ext)
    down = lax.broadcasted_iota(jnp.int32, (refs, 128), 0)
    across = lax.broadcasted_iota(jnp.int32, (refs, 128), 1)
    pick_down = jnp.broadcast_to(pick_row, (refs, refs)).T
    same = (pick_down == pick_row) & (pick_down < ext) & (down < across)
    previous = jnp.max(jnp.where(same, down, -1), axis=0, keepdims=True)
    final = jnp.max(jnp.where((pick_down == across) & (across < ext), down, -1), axis=0, keepdims=True)
    cut_rows = widen(cut_in[...])
    lane_row = lax.broadcasted_iota(jnp.int32, (1, 128), 1)
    cut_marked = jnp.where(lane_row < cut, cut_rows, -1)
    cut_down = jnp.broadcast_to(cut_marked, (refs, 128)).T
    back_row = jnp.max(jnp.where(cut_down == across, down, -1), axis=0, keepdims=True)
    index_rows[PICK : PICK + 1, :] = pick_row
    index_rows[PREV : PREV + 1, :] = jnp.where(previous < 0, refs, previous)
    index_rows[LAST : LAST + 1, :] = jnp.where(final < 0, refs, final)
    index_rows[CUT : CUT + 1, :] = jnp.clip(cut_rows, 0, owned - 1)
    index_rows[BACK : BACK + 1, :] = jnp.where(back_row < 0, cut, back_row)
    index_copy = pltpu.make_async_copy(index_rows, index, load_sem.at[10])
    index_copy.start()
    def pack(target, source):
        def body(g):
            target[g] = jnp.where(left_lanes, source(g), source(g + half))

        loop(half, 4, body)

    def ghost_total(g):
        return running[index[LAST, owned + g]]

    def apply(start, count):
        def pick(c):
            first = c * slot_count
            return jnp.concatenate(
                [
                    jnp.where(
                        left_both, field[index[PICK, first + j]], field[index[PICK, first + j + 1]]
                    )
                    for j in range(0, slot_count, 2)
                ],
                axis=1,
            )

        def times(c, left, side):
            at = side * width
            near = pl.ds(at, middle_at)
            far = pl.ds(at + middle_at, middle_at)
            return jnp.concatenate(
                [
                    mm(left[:, :middle_at], blocks[c, :middle_at, near])
                    + mm_nt(left[:, middle_at:], blocks[c, :middle_at, far]),
                    mm(left, blocks[c, :, far]),
                ],
                axis=1,
            )

        def multiply(c, picked):
            both = times(c, picked, 0)
            return both[:cols] + both[cols:] + times(c, picked[:cols], 1)

        def add(c, product):
            first = c * slot_count
            for j in range(0, slot_count, 2):
                one, two = unpack(product[:, j * dofs : (j + 2) * dofs])
                running[first + j] = running[index[PREV, first + j]] + one
                running[first + j + 1] = running[index[PREV, first + j + 1]] + two

        def body(b, carry):
            places = [start + b * APPLY + u for u in range(APPLY)]
            picked = [pick(c) for c in places]
            products = [multiply(c, value) for c, value in zip(places, picked)]
            for c, product in zip(places, products):
                add(c, product)
            return carry

        lax.fori_loop(0, count // APPLY, body, 0)

    def gram(left, right):
        both = mm_nt(left, right)
        rows = both[:cols] + both[cols:]
        full = fold(rows)
        return jnp.where(left_lanes[: cols // 2], full[: cols // 2], full[cols // 2 :])

    sent = []

    def reduction(number, kind, value):
        sums, slots, sum_send, sum_recv = reducers[4 * number : 4 * number + 4]
        count = 0
        for level, phase in enumerate(phases[kind]):
            sums[level] = value
            copies = []
            for offset in phase:
                copy = pltpu.make_async_remote_copy(
                    src_ref=sums.at[level],
                    dst_ref=slots.at[count],
                    send_sem=sum_send.at[count],
                    recv_sem=sum_recv.at[count],
                    device_id=peer(offset),
                    device_id_type=MESH,
                )
                copy.start()
                copies.append((copy, count))
                count += 1
            sent.extend(copy for copy, at in copies)
            yield None
            for copy, at in copies:
                copy.wait_recv()
            for copy, at in copies:
                value = value + slots[at]
        yield value

    def advance(steps):
        return next(steps)

    def square_of(packed):
        other = pltpu.roll(packed, cols, 1)
        return jnp.concatenate([packed, other], axis=0)[:, :cols]

    load_copy.wait()

    def spread(b):
        at = lanes_of(b)
        piece = loads[:, at]
        load_parts[:cols, at], load_parts[cols:, at] = parts(piece)
        running[2 * b], running[2 * b + 1] = one, two = unpack(piece)
        keep(2 * b, one)
        keep(2 * b + 1, two)

    loop(owned // 2, 4, spread)
    index_copy.wait()
    pack(send_a, lambda g: running[index[CUT, g]])
    running[refs] = jnp.zeros((cols, 128), F32)
    landed[cut] = jnp.zeros((cols, 128), F32)
    field[ext] = jnp.zeros((2 * cols, 128), BF16)
    quarter = cols // 2
    own_gram = gram(load_parts[...], load_parts[...])

    coupling_copy.wait()

    def move(c):
        couple_high, couple_low = parts(coupling[c])
        inverse_high, inverse_low = parts(inverse[arch[c]])
        moved = (
            mm(inverse_high, couple_high)
            + mm(inverse_high, couple_low)
            + mm(inverse_low, couple_high)
        )
        moved_high, moved_low = parts(moved)
        couple_parts[c, :bubbles] = couple_high
        couple_parts[c, bubbles : 2 * bubbles] = couple_low
        couple_parts[c, 2 * bubbles : 3 * bubbles] = moved_high
        couple_parts[c, 3 * bubbles :] = moved_low

    loop(comps, 2, move)

    def form(band, c):
        kind = arch[c]
        weight0, weight1 = theta[0, param[c]], theta[1, param[c]]
        first_row, begin, stiff = bands[band]
        right_of = pl.ds(begin, width - begin)
        moved_high = couple_parts[c, 2 * bubbles : 3 * bubbles, right_of]
        moved_low = couple_parts[c, 3 * bubbles :, right_of]
        moved = jnp.concatenate([moved_high, moved_high, moved_low], axis=0)
        for start in range(first_row, first_row + middle_at, 128):
            rows = pl.ds(start, 128)
            couple_both = couple_parts[c, : 2 * bubbles, rows]
            bubble = mm_tn(jnp.concatenate([couple_both, couple_both[:bubbles]], axis=0), moved)
            block = (
                weight0 * (stiff[2 * kind, pl.ds(start - first_row, 128), :] - bubble)
                + weight1 * stiff[2 * kind + 1, pl.ds(start - first_row, 128), :]
            )
            high, low = parts(block)
            blocks[c, rows, right_of] = high
            blocks[c, rows, pl.ds(width + begin, width - begin)] = low

    pl.semaphore_wait(barrier, len(targets))
    ghosts = send(0, send_a, recv_a, next_id)
    ghosts.start()
    load_steps = reduction(0, 0, own_gram)
    load_gram = advance(load_steps)
    for band in range(len(bands)):
        stiff_copies[band].wait()
        loop(comps, FORM, functools.partial(form, band))
    load_gram = advance(load_steps)

    ghosts.wait()

    def take_ghosts(g):
        one, two = unpack(recv_a[g])
        keep(owned + g, one)
        keep(owned + half + g, two)

    loop(half, 4, take_ghosts)

    apply(0, comps)

    pack(send_p, ghost_total)
    back = send(1, send_p, recv_p, prev_id)
    back.start()
    pack(send_l, lambda g: running[index[LAST, index[CUT, g]]])
    forth = send(2, send_l, recv_l, next_id)
    forth.start()
    load_gram = advance(load_steps)
    back.wait()
    expand(recv_p)

    def first_owned(b):
        one, two = [running[index[LAST, p]] + landed[index[BACK, p]] for p in (2 * b, 2 * b + 1)]
        keep(2 * b, one)
        keep(2 * b + 1, two)
        keep_pair(first_parts, lanes_of(b), one, two)

    loop(owned // 2, 4, first_owned)
    forth.wait()
    expand(recv_l)

    def first_ghost(b):
        one, two = [ghost_total(g) + landed[g] for g in (2 * b, 2 * b + 1)]
        keep(owned + 2 * b, one)
        keep(owned + 2 * b + 1, two)
        keep_pair(first_parts, lanes_of(owned // 2 + b), one, two)

    loop(half, 4, first_ghost)

    first_owned_parts = first_parts[:, : owned * dofs]
    first_copy = pltpu.make_async_copy(
        first_parts.at[:, pl.ds(0, owned * dofs)], first_hbm, load_sem.at[8]
    )
    first_copy.start()
    middle_steps = reduction(
        1,
        0,
        jnp.concatenate(
            [gram(load_parts[...], first_owned_parts), gram(first_owned_parts, first_owned_parts)],
            axis=0,
        ),
    )
    middle = advance(middle_steps)
    apply(0, comps // 2)
    if load_gram is None:
        load_gram = advance(load_steps)
    middle = advance(middle_steps)
    apply(comps // 2, comps // 2)

    pack(send_t, ghost_total)
    last_back = send(3, send_t, recv_t, prev_id)
    last_back.start()

    def second_partial(b):
        one, two = [running[index[LAST, p]] for p in (2 * b, 2 * b + 1)]
        keep_pair(second_parts, lanes_of(b), one, two)

    loop(ext // 2, 4, second_partial)
    cube_steps = reduction(2, 1, gram(first_parts[...], second_parts[...]))
    cube = advance(cube_steps)
    while load_gram is None:
        load_gram = advance(load_steps)
    if middle is None:
        middle = advance(middle_steps)
    cube = advance(cube_steps)
    if middle is None:
        middle = advance(middle_steps)

    last_back.wait()
    expand(recv_t)

    def second_owned(b):
        one, two = [running[index[LAST, p]] + landed[index[BACK, p]] for p in (2 * b, 2 * b + 1)]
        keep_pair(second_out, lanes_of(b), one, two)

    loop(owned // 2, 4, second_owned)
    second_copy = pltpu.make_async_copy(second_out, second_hbm, load_sem.at[9])
    second_copy.start()
    while middle is None:
        middle = advance(middle_steps)
    load_gram, cross, square = [
        square_of(packed) for packed in (load_gram, middle[:quarter], middle[quarter:])
    ]
    solved = elimination(
        [jnp.concatenate([cross, square], axis=1), jnp.concatenate([load_gram, load_gram], axis=1)]
    )
    moved = solved[0][:, cols:]
    step = solved[1][:, :cols]
    small_out[0, :, cols:] = cross - exact(square, step)
    small_out[1, :, :cols] = moved
    small_out[1, :, cols:] = step
    while cube is None:
        cube = advance(cube_steps)
    small_out[0, :, :cols] = square_of(cube) - exact(square, moved)
    for copy in sent:
        copy.wait_send()
    first_copy.wait()
    second_copy.wait()


def elimination(tiles, block=8):
    size = tiles[0].shape[0]
    row_index = lax.broadcasted_iota(jnp.int32, (size, 1), 0)
    for k in range(0, size, block):
        wide = [jnp.broadcast_to(tiles[0][:, k + j : k + j + 1], tiles[0].shape) for j in range(block)]
        pivots = [[wide[j][k + i : k + i + 1] for j in range(block)] for i in range(block)]
        rows = [[tile[k + i : k + i + 1] for tile in tiles] for i in range(block)]
        for i in range(block):
            scale = 1.0 / pivots[i][i]
            rows[i] = [row * scale for row in rows[i]]
            for j in range(i + 1, block):
                pivots[i][j] = pivots[i][j] * scale
            for m in range(i + 1, block):
                factor = pivots[m][i]
                rows[m] = [row - factor * other for row, other in zip(rows[m], rows[i])]
                for j in range(i + 1, block):
                    pivots[m][j] = pivots[m][j] - factor * pivots[i][j]
        for i in range(block - 1, 0, -1):
            for m in range(i):
                rows[m] = [row - pivots[m][i] * other for row, other in zip(rows[m], rows[i])]
        out = []
        for number, tile in enumerate(tiles):
            new = tile
            for j in range(block):
                new = new - wide[j] * rows[j][number]
            for j in range(block):
                new = jnp.where(row_index == k + j, rows[j][number], new)
            out.append(new)
        tiles = out
    return tiles


def combine_kernel(small, loads_hbm, first_hbm, second_hbm, solution_hbm, residual_hbm, loads, first, second, solution, residual, sems):
    cols = loads.shape[0]
    copies = []
    for number, (source, target) in enumerate(
        ((loads_hbm, loads), (first_hbm, first), (second_hbm, second))
    ):
        copy = pltpu.make_async_copy(source, target, sems.at[number])
        copy.start()
        copies.append(copy)

    (solved,) = elimination([small[0]])
    second_weight = solved[:, cols:]
    first_weight = small[1, :, cols:] - exact(small[1, :, :cols], second_weight)

    top_high, top_low = parts(first_weight.T)
    low_high, low_low = parts(second_weight.T)
    left = jnp.concatenate([top_high, top_high, top_low, low_high, low_high, low_low], axis=1)
    for copy in copies:
        copy.wait()

    chunk = 512
    writes = []
    for b in range(loads.shape[1] // chunk):
        at = pl.ds(b * chunk, chunk)
        load_piece, first_piece, second_piece = loads[:, at], first[:, at], second[:, at]
        load_high, load_low = parts(load_piece)
        solution[:, at] = mm(
            left,
            jnp.concatenate(
                [load_high, load_low, load_high, first_piece, first_piece[:cols]], axis=0
            ),
        )
        residual[:, at] = load_piece - mm(
            left,
            jnp.concatenate(
                [first_piece, first_piece[:cols], second_piece, second_piece[:cols]], axis=0
            ),
        )
        for number, (source, target) in enumerate(
            ((solution, solution_hbm), (residual, residual_hbm))
        ):
            copy = pltpu.make_async_copy(
                source.at[:, at], target.at[:, at], sems.at[3 + 2 * b + number]
            )
            copy.start()
            writes.append(copy)
    for copy in writes:
        copy.wait()


def mm_nt(left, right):
    return lax.dot_general(left, right, (((1,), (1,)), ((), ())), preferred_element_type=F32)


def local(
    sizes,
    port_loads,
    port_stiff,
    bubble_inverse,
    coupling,
    theta_table,
    comp_arch,
    comp_param,
    port_refs,
    slot_mask,
    cut_source,
):
    cols = port_loads.shape[0]
    comps, slot_count = port_refs.shape
    width = port_stiff.shape[2]
    dofs = width // slot_count
    cut = cut_source.shape[1]
    owned = port_loads.shape[1] // dofs
    refs = comps * slot_count
    ext = owned + cut
    archs, terms = port_stiff.shape[:2]
    bubbles = coupling.shape[1]

    phases = phases_of(sizes)
    smem = pl.BlockSpec(memory_space=pltpu.SMEM)
    vmem = pl.BlockSpec(memory_space=pltpu.VMEM)
    hbm = pl.BlockSpec(memory_space=pl.ANY)
    reducers = []
    for kind, rows in ((0, cols // 2), (0, cols), (1, cols // 2)):
        messages = sum(len(phase) for phase in phases[kind])
        reducers += [
            pltpu.VMEM((len(phases[kind]), rows, 128), F32),
            pltpu.VMEM((messages, rows, 128), F32),
            pltpu.SemaphoreType.DMA((messages,)),
            pltpu.SemaphoreType.DMA((messages,)),
        ]
    exchange = pltpu.VMEM((cut // 2, cols, 128), F32)
    flops = 2 * comps * cols * width * width * 9
    first, second, small = pl.pallas_call(
        functools.partial(system_kernel, sizes, phases),
        out_shape=(
            jax.ShapeDtypeStruct((2 * cols, owned * dofs), BF16),
            jax.ShapeDtypeStruct((2 * cols, owned * dofs), BF16),
            jax.ShapeDtypeStruct((2, cols, 2 * cols), F32),
        ),
        in_specs=[smem, smem, smem] + [hbm] * 7,
        out_specs=(hbm, hbm, vmem),
        scratch_shapes=[
            pltpu.VMEM((slot_count, comps), jnp.int32),
            pltpu.VMEM((slot_count, comps), jnp.int32),
            pltpu.VMEM(cut_source.shape, jnp.int32),
            pltpu.VMEM(bubble_inverse.shape, F32),
            pltpu.VMEM(port_loads.shape, F32),
            pltpu.VMEM((archs * terms, width // 2, width), F32),
            pltpu.VMEM((archs * terms, width // 2, width // 2), F32),
            pltpu.VMEM(coupling.shape, F32),
            pltpu.VMEM((comps, 4 * bubbles, width), BF16),
            pltpu.VMEM((comps, width, 2 * width), BF16),
            pltpu.VMEM((ext + 1, 2 * cols, 128), BF16),
            pltpu.VMEM((refs + 1, cols, 128), F32),
            pltpu.VMEM((2 * cols, owned * dofs), BF16),
            pltpu.VMEM((2 * cols, ext * dofs), BF16),
            pltpu.VMEM((2 * cols, ext * dofs), BF16),
            pltpu.VMEM((2 * cols, owned * dofs), BF16),
            pltpu.VMEM((cut + 1, cols, 128), F32),
        ]
        + [exchange] * 8
        + [
            pltpu.VMEM((8, 128), jnp.int32),
            pltpu.SMEM((8, 128), jnp.int32),
            pltpu.SemaphoreType.DMA((11,)),
            pltpu.SemaphoreType.DMA((4,)),
            pltpu.SemaphoreType.DMA((4,)),
        ]
        + reducers,
        compiler_params=pltpu.CompilerParams(
            collective_id=0, has_side_effects=True, vmem_limit_bytes=60 * 1024 * 1024
        ),
        cost_estimate=pl.CostEstimate(flops=flops, bytes_accessed=12 << 20, transcendentals=0),
        name="system",
    )(
        comp_arch,
        comp_param,
        theta_table.T,
        port_refs.T,
        slot_mask.T,
        cut_source,
        bubble_inverse,
        port_loads,
        port_stiff.reshape(archs * terms, width, width),
        coupling,
    )
    return pl.pallas_call(
        combine_kernel,
        out_shape=(
            jax.ShapeDtypeStruct(port_loads.shape, F32),
            jax.ShapeDtypeStruct(port_loads.shape, F32),
        ),
        in_specs=[vmem, hbm, hbm, hbm],
        out_specs=(hbm, hbm),
        scratch_shapes=[
            pltpu.VMEM(port_loads.shape, F32),
            pltpu.VMEM((2 * cols, owned * dofs), BF16),
            pltpu.VMEM((2 * cols, owned * dofs), BF16),
            pltpu.VMEM(port_loads.shape, F32),
            pltpu.VMEM(port_loads.shape, F32),
            pltpu.SemaphoreType.DMA((3 + 2 * (owned * dofs // 512),)),
        ],
        compiler_params=pltpu.CompilerParams(vmem_limit_bytes=60 * 1024 * 1024),
        cost_estimate=pl.CostEstimate(flops=1 << 28, bytes_accessed=4 << 20, transcendentals=0),
        name="combine",
    )(small, port_loads, first, second)


def solution(mesh):
    sizes = (mesh.shape["gx"], mesh.shape["gy"])
    placed = (
        P(None, ("gx", "gy")),
        P(),
        P(),
        P(("gx", "gy"), None, None),
        P(),
        P(("gx", "gy")),
        P(("gx", "gy")),
        P(("gx", "gy"), None),
        P(("gx", "gy"), None),
        P(("gx", "gy"), None),
    )
    return jax.shard_map(
        functools.partial(local, sizes),
        mesh=mesh,
        in_specs=placed,
        out_specs=(P(None, ("gx", "gy")), P(None, ("gx", "gy"))),
        check_vma=False,
    )
```

```python
import functools
import itertools

import jax
import jax.numpy as jnp
from jax import lax
from jax.experimental import pallas as pl
from jax.experimental.pallas import tpu as pltpu
from jax.sharding import PartitionSpec as P

MESH = pl.DeviceIdType.MESH
APPLY = 8
FORM = 16
F32 = jnp.float32
BF16 = jnp.bfloat16


def parts(value):
    high = value.astype(BF16)
    return high, (value - high.astype(F32)).astype(BF16)


def mm(left, right):
    return jnp.dot(left, right, preferred_element_type=F32)


def mm_tn(left, right):
    return lax.dot_general(left, right, (((0,), (0,)), ((), ())), preferred_element_type=F32)


def exact(left, right):
    return lax.dot_general(
        left,
        right,
        (((1,), (0,)), ((), ())),
        precision=lax.Precision.HIGHEST,
        preferred_element_type=F32,
    )


def phases_of(mesh_sizes):
    sizes_x, sizes_y = mesh_sizes
    axes = []
    stride = 1
    for size in (2, 4, sizes_y):
        size = min(size, sizes_y // stride)
        if size > 1:
            axes.append(("gy", stride, size))
            stride *= size
    if sizes_x > 1:
        axes.append(("gx", 1, sizes_x))

    def phase(*members):
        steps = itertools.product(*[range(member[2]) for member in members])
        offsets = [list(zip(members, step)) for step in steps if any(step)]

        def hops(offset):
            return sum(min(steps, member[2] - steps) for member, steps in offset)

        return sorted(offsets, key=hops, reverse=True)

    return (
        [phase(axis) for axis in axes],
        [phase(*axes[:2]), phase(*axes[2:])],
        [phase(*axes[:2])] + [phase(axis) for axis in axes[2:]],
    )


def system_kernel(
    sizes,
    phases,
    arch,
    param,
    theta,
    refs_hbm,
    mask_hbm,
    cut_hbm,
    inverse_hbm,
    loads_hbm,
    stiff_hbm,
    coupling_hbm,
    first_hbm,
    second_hbm,
    small_out,
    refs_in,
    mask_in,
    cut_in,
    inverse,
    loads,
    stiff_top,
    stiff_low,
    coupling,
    couple_parts,
    blocks,
    field,
    running,
    load_parts,
    first_parts,
    second_parts,
    second_out,
    landed,
    send_a,
    recv_a,
    send_l,
    recv_l,
    send_p,
    recv_p,
    send_t,
    recv_t,
    index_rows,
    index,
    load_sem,
    send_sem,
    recv_sem,
    *reducers,
):
    sizes_x, sizes_y = sizes
    comps = coupling.shape[0]
    bubbles = coupling.shape[1]
    cols, dofs = loads.shape[0], field.shape[2] // 2
    owned = loads.shape[1] // dofs
    slot_count = refs_in.shape[0]
    refs = comps * slot_count
    width = slot_count * dofs
    cut = cut_in.shape[1]
    half = cut // 2
    ext = owned + cut
    quarter_comps = comps // 4
    PICK, PREV, LAST, CUT, BACK = range(5)

    my_x, my_y = lax.axis_index("gx"), lax.axis_index("gy")
    here = my_x * sizes_y + my_y
    total = sizes_x * sizes_y
    after = lax.rem(here + 1, total)
    before = lax.rem(here + total - 1, total)
    next_id = (after // sizes_y, lax.rem(after, sizes_y))
    prev_id = (before // sizes_y, lax.rem(before, sizes_y))

    def peer(offset):
        x, y = my_x, my_y
        for (axis, stride, size), steps in offset:
            if steps and axis == "gx":
                x = lax.rem(my_x + steps, size)
            elif steps:
                place = lax.rem(my_y // stride, size)
                y = y + (lax.rem(place + steps, size) - place) * stride
        return (x, y)

    small_copies = []
    for number, (source, target) in enumerate(
        ((refs_hbm, refs_in), (mask_hbm, mask_in), (cut_hbm, cut_in), (inverse_hbm, inverse))
    ):
        copy = pltpu.make_async_copy(source, target, load_sem.at[1 + number])
        copy.start()
        small_copies.append(copy)
    load_copy = pltpu.make_async_copy(loads_hbm, loads, load_sem.at[0])
    load_copy.start()
    coupling_copy = pltpu.make_async_copy(coupling_hbm, coupling, load_sem.at[5])
    coupling_copy.start()
    middle_at = width // 2
    bands = ((0, 0, stiff_top), (middle_at, middle_at, stiff_low))
    stiff_copies = []
    for band, (start, begin, target) in enumerate(bands):
        at = (slice(None), pl.ds(start, middle_at), pl.ds(begin, width - begin))
        copy = pltpu.make_async_copy(stiff_hbm.at[at], target, load_sem.at[6 + band])
        copy.start()
        stiff_copies.append(copy)

    barrier = pltpu.get_barrier_semaphore()
    targets = [next_id, prev_id]
    targets += [peer(offset) for phase in phases[1] for offset in phase]
    for target in targets:
        pl.semaphore_signal(barrier, inc=1, device_id=target, device_id_type=MESH)

    left_lanes = lax.broadcasted_iota(jnp.int32, (cols, 128), 1) < dofs
    left_both = lax.broadcasted_iota(jnp.int32, (2 * cols, 128), 1) < dofs

    def fold(value):
        return value + pltpu.roll(value, dofs, 1)

    def keep(place, full):
        field[place, :cols], field[place, cols:] = parts(full)

    def keep_pair(target, at, one, two):
        target[:cols, at], target[cols:, at] = parts(jnp.where(left_lanes, one, two))

    def lanes_of(b):
        return pl.ds(pl.multiple_of(b * 128, 128), 128)

    def send(number, source, target_ref, device):
        return pltpu.make_async_remote_copy(
            src_ref=source,
            dst_ref=target_ref,
            send_sem=send_sem.at[number],
            recv_sem=recv_sem.at[number],
            device_id=device,
            device_id_type=MESH,
        )

    def loop(count, unroll, body):
        def step(b, carry):
            for u in range(unroll):
                body(b * unroll + u)
            return carry

        lax.fori_loop(0, count // unroll, step, 0)

    def unpack(pair):
        other = pltpu.roll(pair, dofs, 1)
        return jnp.where(left_lanes, pair, other), jnp.where(left_lanes, other, pair)

    def expand(received):
        def body(g):
            landed[g], landed[g + half] = unpack(received[g])

        loop(half, 4, body)

    def widen(row):
        return jnp.concatenate(
            [row, jnp.zeros((row.shape[0], 128 - row.shape[1]), row.dtype)], axis=1
        )

    for copy in small_copies:
        copy.wait()
    picks = widen(jnp.where(mask_in[...] != 0, refs_in[...], ext)).T[:comps]
    comp_lane = lax.broadcasted_iota(jnp.int32, (comps, refs), 1)
    comp_row = lax.broadcasted_iota(jnp.int32, (comps, refs), 0)
    wide = jnp.zeros((comps, refs), jnp.int32)
    for j in range(slot_count):
        wide = jnp.where(comp_lane == comp_row * slot_count + j, picks[:, j : j + 1], wide)
    pick_row = jnp.sum(wide, axis=0, keepdims=True)
    pick_row = jnp.clip(pick_row, 0, ext)
    down = lax.broadcasted_iota(jnp.int32, (refs, 128), 0)
    across = lax.broadcasted_iota(jnp.int32, (refs, 128), 1)
    pick_down = jnp.broadcast_to(pick_row, (refs, refs)).T
    same = (pick_down == pick_row) & (pick_down < ext) & (down < across)
    previous = jnp.max(jnp.where(same, down, -1), axis=0, keepdims=True)
    final = jnp.max(jnp.where((pick_down == across) & (across < ext), down, -1), axis=0, keepdims=True)
    cut_rows = widen(cut_in[...])
    lane_row = lax.broadcasted_iota(jnp.int32, (1, 128), 1)
    cut_marked = jnp.where(lane_row < cut, cut_rows, -1)
    cut_down = jnp.broadcast_to(cut_marked, (refs, 128)).T
    back_row = jnp.max(jnp.where(cut_down == across, down, -1), axis=0, keepdims=True)
    index_rows[PICK : PICK + 1, :] = pick_row
    index_rows[PREV : PREV + 1, :] = jnp.where(previous < 0, refs, previous)
    index_rows[LAST : LAST + 1, :] = jnp.where(final < 0, refs, final)
    index_rows[CUT : CUT + 1, :] = jnp.clip(cut_rows, 0, owned - 1)
    index_rows[BACK : BACK + 1, :] = jnp.where(back_row < 0, cut, back_row)
    index_copy = pltpu.make_async_copy(index_rows, index, load_sem.at[10])
    index_copy.start()
    def pack(target, source):
        def body(g):
            target[g] = jnp.where(left_lanes, source(g), source(g + half))

        loop(half, 4, body)

    def ghost_total(g):
        return running[index[LAST, owned + g]]

    def apply(start, count):
        def pick(c):
            first = c * slot_count
            return jnp.concatenate(
                [
                    jnp.where(
                        left_both, field[index[PICK, first + j]], field[index[PICK, first + j + 1]]
                    )
                    for j in range(0, slot_count, 2)
                ],
                axis=1,
            )

        def times(c, left, side):
            at = side * width
            near = pl.ds(at, middle_at)
            far = pl.ds(at + middle_at, middle_at)
            return jnp.concatenate(
                [
                    mm(left[:, :middle_at], blocks[c, :middle_at, near])
                    + mm_nt(left[:, middle_at:], blocks[c, :middle_at, far]),
                    mm(left, blocks[c, :, far]),
                ],
                axis=1,
            )

        def multiply(c, picked):
            both = times(c, picked, 0)
            return both[:cols] + both[cols:] + times(c, picked[:cols], 1)

        def add(c, product):
            first = c * slot_count
            for j in range(0, slot_count, 2):
                one, two = unpack(product[:, j * dofs : (j + 2) * dofs])
                running[first + j] = running[index[PREV, first + j]] + one
                running[first + j + 1] = running[index[PREV, first + j + 1]] + two

        def body(b, carry):
            places = [start + b * APPLY + u for u in range(APPLY)]
            picked = [pick(c) for c in places]
            products = [multiply(c, value) for c, value in zip(places, picked)]
            for c, product in zip(places, products):
                add(c, product)
            return carry

        lax.fori_loop(0, count // APPLY, body, 0)

    def gram(left, right):
        both = mm_nt(left, right)
        rows = both[:cols] + both[cols:]
        full = fold(rows)
        return jnp.where(left_lanes[: cols // 2], full[: cols // 2], full[cols // 2 :])

    sent = []

    def reduction(number, kind, value):
        sums, slots, sum_send, sum_recv = reducers[4 * number : 4 * number + 4]
        count = 0
        for level, phase in enumerate(phases[kind]):
            sums[level] = value
            copies = []
            for offset in phase:
                copy = pltpu.make_async_remote_copy(
                    src_ref=sums.at[level],
                    dst_ref=slots.at[count],
                    send_sem=sum_send.at[count],
                    recv_sem=sum_recv.at[count],
                    device_id=peer(offset),
                    device_id_type=MESH,
                )
                copy.start()
                copies.append((copy, count))
                count += 1
            sent.extend(copy for copy, at in copies)
            yield None
            for copy, at in copies:
                copy.wait_recv()
            for copy, at in copies:
                value = value + slots[at]
        yield value

    def advance(steps):
        return next(steps)

    def square_of(packed):
        other = pltpu.roll(packed, cols, 1)
        return jnp.concatenate([packed, other], axis=0)[:, :cols]

    load_copy.wait()

    def spread(b):
        at = lanes_of(b)
        piece = loads[:, at]
        load_parts[:cols, at], load_parts[cols:, at] = parts(piece)
        running[2 * b], running[2 * b + 1] = one, two = unpack(piece)
        keep(2 * b, one)
        keep(2 * b + 1, two)

    loop(owned // 2, 4, spread)
    index_copy.wait()
    pack(send_a, lambda g: running[index[CUT, g]])
    running[refs] = jnp.zeros((cols, 128), F32)
    landed[cut] = jnp.zeros((cols, 128), F32)
    field[ext] = jnp.zeros((2 * cols, 128), BF16)
    quarter = cols // 2
    own_gram = gram(load_parts[...], load_parts[...])

    coupling_copy.wait()

    def move(c):
        couple_high, couple_low = parts(coupling[c])
        inverse_high, inverse_low = parts(inverse[arch[c]])
        moved = (
            mm(inverse_high, couple_high)
            + mm(inverse_high, couple_low)
            + mm(inverse_low, couple_high)
        )
        moved_high, moved_low = parts(moved)
        couple_parts[c, :bubbles] = couple_high
        couple_parts[c, bubbles : 2 * bubbles] = couple_low
        couple_parts[c, 2 * bubbles : 3 * bubbles] = moved_high
        couple_parts[c, 3 * bubbles :] = moved_low

    loop(comps, 2, move)

    def form(band, c):
        kind = arch[c]
        weight0, weight1 = theta[0, param[c]], theta[1, param[c]]
        first_row, begin, stiff = bands[band]
        right_of = pl.ds(begin, width - begin)
        moved_high = couple_parts[c, 2 * bubbles : 3 * bubbles, right_of]
        moved_low = couple_parts[c, 3 * bubbles :, right_of]
        moved = jnp.concatenate([moved_high, moved_high, moved_low], axis=0)
        for start in range(first_row, first_row + middle_at, 128):
            rows = pl.ds(start, 128)
            couple_both = couple_parts[c, : 2 * bubbles, rows]
            bubble = mm_tn(jnp.concatenate([couple_both, couple_both[:bubbles]], axis=0), moved)
            block = (
                weight0 * (stiff[2 * kind, pl.ds(start - first_row, 128), :] - bubble)
                + weight1 * stiff[2 * kind + 1, pl.ds(start - first_row, 128), :]
            )
            high, low = parts(block)
            blocks[c, rows, right_of] = high
            blocks[c, rows, pl.ds(width + begin, width - begin)] = low

    pl.semaphore_wait(barrier, len(targets))
    ghosts = send(0, send_a, recv_a, next_id)
    ghosts.start()
    load_steps = reduction(0, 0, own_gram)
    load_gram = advance(load_steps)
    for band in range(len(bands)):
        stiff_copies[band].wait()
        loop(comps, FORM, functools.partial(form, band))
    load_gram = advance(load_steps)

    ghosts.wait()

    def take_ghosts(g):
        one, two = unpack(recv_a[g])
        keep(owned + g, one)
        keep(owned + half + g, two)

    loop(half, 4, take_ghosts)

    apply(0, comps // 2)
    apply(comps // 2, comps // 2)

    pack(send_p, ghost_total)
    back = send(1, send_p, recv_p, prev_id)
    back.start()
    pack(send_l, lambda g: running[index[LAST, index[CUT, g]]])
    forth = send(2, send_l, recv_l, next_id)
    forth.start()
    load_gram = advance(load_steps)
    back.wait()
    expand(recv_p)

    def first_owned(b):
        one, two = [running[index[LAST, p]] + landed[index[BACK, p]] for p in (2 * b, 2 * b + 1)]
        keep(2 * b, one)
        keep(2 * b + 1, two)
        keep_pair(first_parts, lanes_of(b), one, two)

    loop(owned // 2, 4, first_owned)
    forth.wait()
    expand(recv_l)

    def first_ghost(b):
        one, two = [ghost_total(g) + landed[g] for g in (2 * b, 2 * b + 1)]
        keep(owned + 2 * b, one)
        keep(owned + 2 * b + 1, two)
        keep_pair(first_parts, lanes_of(owned // 2 + b), one, two)

    loop(half, 4, first_ghost)

    first_owned_parts = first_parts[:, : owned * dofs]
    first_copy = pltpu.make_async_copy(
        first_parts.at[:, pl.ds(0, owned * dofs)], first_hbm, load_sem.at[8]
    )
    first_copy.start()
    middle_steps = reduction(
        1,
        2,
        jnp.concatenate(
            [gram(load_parts[...], first_owned_parts), gram(first_owned_parts, first_owned_parts)],
            axis=0,
        ),
    )
    middle = advance(middle_steps)
    apply(0, comps // 2)
    if load_gram is None:
        load_gram = advance(load_steps)
    apply(comps // 2, comps // 2)

    def second_partial(b):
        one, two = [running[index[LAST, p]] for p in (2 * b, 2 * b + 1)]
        keep_pair(second_parts, lanes_of(b), one, two)

    loop(ext // 2, 4, second_partial)
    cube_steps = reduction(2, 1, gram(first_parts[...], second_parts[...]))
    cube = advance(cube_steps)
    pack(send_t, ghost_total)
    last_back = send(3, send_t, recv_t, prev_id)
    last_back.start()
    middle = advance(middle_steps)
    while load_gram is None:
        load_gram = advance(load_steps)
    cube = advance(cube_steps)
    if middle is None:
        middle = advance(middle_steps)

    last_back.wait()
    expand(recv_t)

    def second_owned(b):
        one, two = [running[index[LAST, p]] + landed[index[BACK, p]] for p in (2 * b, 2 * b + 1)]
        keep_pair(second_out, lanes_of(b), one, two)

    loop(owned // 2, 4, second_owned)
    second_copy = pltpu.make_async_copy(second_out, second_hbm, load_sem.at[9])
    second_copy.start()
    while middle is None:
        middle = advance(middle_steps)
    load_gram, cross, square = [
        square_of(packed) for packed in (load_gram, middle[:quarter], middle[quarter:])
    ]
    solved = elimination(
        [jnp.concatenate([cross, square], axis=1), jnp.concatenate([load_gram, load_gram], axis=1)]
    )
    moved = solved[0][:, cols:]
    step = solved[1][:, :cols]
    small_out[0, :, cols:] = cross - exact(square, step)
    small_out[1, :, :cols] = moved
    small_out[1, :, cols:] = step
    while cube is None:
        cube = advance(cube_steps)
    small_out[0, :, :cols] = square_of(cube) - exact(square, moved)
    for copy in sent:
        copy.wait_send()
    first_copy.wait()
    second_copy.wait()


def elimination(tiles, block=8, midway=None):
    size = tiles[0].shape[0]
    row_index = lax.broadcasted_iota(jnp.int32, (size, 1), 0)
    for k in range(0, size, block):
        if midway is not None and k == size // 2:
            midway()
        wide = [jnp.broadcast_to(tiles[0][:, k + j : k + j + 1], tiles[0].shape) for j in range(block)]
        pivots = [[wide[j][k + i : k + i + 1] for j in range(block)] for i in range(block)]
        rows = [[tile[k + i : k + i + 1] for tile in tiles] for i in range(block)]
        for i in range(block):
            scale = 1.0 / pivots[i][i]
            rows[i] = [row * scale for row in rows[i]]
            for j in range(i + 1, block):
                pivots[i][j] = pivots[i][j] * scale
            for m in range(i + 1, block):
                factor = pivots[m][i]
                rows[m] = [row - factor * other for row, other in zip(rows[m], rows[i])]
                for j in range(i + 1, block):
                    pivots[m][j] = pivots[m][j] - factor * pivots[i][j]
        for i in range(block - 1, 0, -1):
            for m in range(i):
                rows[m] = [row - pivots[m][i] * other for row, other in zip(rows[m], rows[i])]
        out = []
        for number, tile in enumerate(tiles):
            new = tile
            for j in range(block):
                new = new - wide[j] * rows[j][number]
            for j in range(block):
                new = jnp.where(row_index == k + j, rows[j][number], new)
            out.append(new)
        tiles = out
    return tiles


def combine_kernel(small, loads_hbm, first_hbm, second_hbm, solution_hbm, residual_hbm, loads, load_parts, first, second, solution, residual, sems):
    cols = loads.shape[0]
    copies = []
    for number, (source, target) in enumerate(
        ((loads_hbm, loads), (first_hbm, first), (second_hbm, second))
    ):
        copy = pltpu.make_async_copy(source, target, sems.at[number])
        copy.start()
        copies.append(copy)

    def split_loads():
        copies[0].wait()
        load_parts[:cols, :], load_parts[cols:, :] = parts(loads[...])

    (solved,) = elimination([small[0]], midway=split_loads)
    second_weight = solved[:, cols:]
    first_weight = small[1, :, cols:] - exact(small[1, :, :cols], second_weight)

    top_high, top_low = parts(first_weight.T)
    low_high, low_low = parts(second_weight.T)
    left = jnp.concatenate([top_high, top_high, top_low, low_high, low_high, low_low], axis=1)
    for copy in copies[1:]:
        copy.wait()

    chunk = 512
    writes = []
    for b in range(loads.shape[1] // chunk):
        at = pl.ds(b * chunk, chunk)
        load_piece, first_piece, second_piece = loads[:, at], first[:, at], second[:, at]
        both_piece = load_parts[:, at]
        solution[:, at] = mm(
            left,
            jnp.concatenate(
                [both_piece, both_piece[:cols], first_piece, first_piece[:cols]], axis=0
            ),
        )
        residual[:, at] = load_piece - mm(
            left,
            jnp.concatenate(
                [first_piece, first_piece[:cols], second_piece, second_piece[:cols]], axis=0
            ),
        )
        for number, (source, target) in enumerate(
            ((solution, solution_hbm), (residual, residual_hbm))
        ):
            copy = pltpu.make_async_copy(
                source.at[:, at], target.at[:, at], sems.at[3 + 2 * b + number]
            )
            copy.start()
            writes.append(copy)
    for copy in writes:
        copy.wait()


def mm_nt(left, right):
    return lax.dot_general(left, right, (((1,), (1,)), ((), ())), preferred_element_type=F32)


def local(
    sizes,
    port_loads,
    port_stiff,
    bubble_inverse,
    coupling,
    theta_table,
    comp_arch,
    comp_param,
    port_refs,
    slot_mask,
    cut_source,
):
    cols = port_loads.shape[0]
    comps, slot_count = port_refs.shape
    width = port_stiff.shape[2]
    dofs = width // slot_count
    cut = cut_source.shape[1]
    owned = port_loads.shape[1] // dofs
    refs = comps * slot_count
    ext = owned + cut
    archs, terms = port_stiff.shape[:2]
    bubbles = coupling.shape[1]

    phases = phases_of(sizes)
    smem = pl.BlockSpec(memory_space=pltpu.SMEM)
    vmem = pl.BlockSpec(memory_space=pltpu.VMEM)
    hbm = pl.BlockSpec(memory_space=pl.ANY)
    reducers = []
    for kind, rows in ((0, cols // 2), (2, cols), (1, cols // 2)):
        messages = sum(len(phase) for phase in phases[kind])
        reducers += [
            pltpu.VMEM((len(phases[kind]), rows, 128), F32),
            pltpu.VMEM((messages, rows, 128), F32),
            pltpu.SemaphoreType.DMA((messages,)),
            pltpu.SemaphoreType.DMA((messages,)),
        ]
    exchange = pltpu.VMEM((cut // 2, cols, 128), F32)
    flops = 2 * comps * cols * width * width * 9
    first, second, small = pl.pallas_call(
        functools.partial(system_kernel, sizes, phases),
        out_shape=(
            jax.ShapeDtypeStruct((2 * cols, owned * dofs), BF16),
            jax.ShapeDtypeStruct((2 * cols, owned * dofs), BF16),
            jax.ShapeDtypeStruct((2, cols, 2 * cols), F32),
        ),
        in_specs=[smem, smem, smem] + [hbm] * 7,
        out_specs=(hbm, hbm, vmem),
        scratch_shapes=[
            pltpu.VMEM((slot_count, comps), jnp.int32),
            pltpu.VMEM((slot_count, comps), jnp.int32),
            pltpu.VMEM(cut_source.shape, jnp.int32),
            pltpu.VMEM(bubble_inverse.shape, F32),
            pltpu.VMEM(port_loads.shape, F32),
            pltpu.VMEM((archs * terms, width // 2, width), F32),
            pltpu.VMEM((archs * terms, width // 2, width // 2), F32),
            pltpu.VMEM(coupling.shape, F32),
            pltpu.VMEM((comps, 4 * bubbles, width), BF16),
            pltpu.VMEM((comps, width, 2 * width), BF16),
            pltpu.VMEM((ext + 1, 2 * cols, 128), BF16),
            pltpu.VMEM((refs + 1, cols, 128), F32),
            pltpu.VMEM((2 * cols, owned * dofs), BF16),
            pltpu.VMEM((2 * cols, ext * dofs), BF16),
            pltpu.VMEM((2 * cols, ext * dofs), BF16),
            pltpu.VMEM((2 * cols, owned * dofs), BF16),
            pltpu.VMEM((cut + 1, cols, 128), F32),
        ]
        + [exchange] * 8
        + [
            pltpu.VMEM((8, 128), jnp.int32),
            pltpu.SMEM((8, 128), jnp.int32),
            pltpu.SemaphoreType.DMA((11,)),
            pltpu.SemaphoreType.DMA((4,)),
            pltpu.SemaphoreType.DMA((4,)),
        ]
        + reducers,
        compiler_params=pltpu.CompilerParams(
            collective_id=0, has_side_effects=True, vmem_limit_bytes=60 * 1024 * 1024
        ),
        cost_estimate=pl.CostEstimate(flops=flops, bytes_accessed=12 << 20, transcendentals=0),
        name="system",
    )(
        comp_arch,
        comp_param,
        theta_table.T,
        port_refs.T,
        slot_mask.T,
        cut_source,
        bubble_inverse,
        port_loads,
        port_stiff.reshape(archs * terms, width, width),
        coupling,
    )
    return pl.pallas_call(
        combine_kernel,
        out_shape=(
            jax.ShapeDtypeStruct(port_loads.shape, F32),
            jax.ShapeDtypeStruct(port_loads.shape, F32),
        ),
        in_specs=[vmem, hbm, hbm, hbm],
        out_specs=(hbm, hbm),
        scratch_shapes=[
            pltpu.VMEM(port_loads.shape, F32),
            pltpu.VMEM((2 * cols, owned * dofs), BF16),
            pltpu.VMEM((2 * cols, owned * dofs), BF16),
            pltpu.VMEM((2 * cols, owned * dofs), BF16),
            pltpu.VMEM(port_loads.shape, F32),
            pltpu.VMEM(port_loads.shape, F32),
            pltpu.SemaphoreType.DMA((3 + 2 * (owned * dofs // 512),)),
        ],
        compiler_params=pltpu.CompilerParams(vmem_limit_bytes=60 * 1024 * 1024),
        cost_estimate=pl.CostEstimate(flops=1 << 28, bytes_accessed=4 << 20, transcendentals=0),
        name="combine",
    )(small, port_loads, first, second)


def solution(mesh):
    sizes = (mesh.shape["gx"], mesh.shape["gy"])
    placed = (
        P(None, ("gx", "gy")),
        P(),
        P(),
        P(("gx", "gy"), None, None),
        P(),
        P(("gx", "gy")),
        P(("gx", "gy")),
        P(("gx", "gy"), None),
        P(("gx", "gy"), None),
        P(("gx", "gy"), None),
    )
    return jax.shard_map(
        functools.partial(local, sizes),
        mesh=mesh,
        in_specs=placed,
        out_specs=(P(None, ("gx", "gy")), P(None, ("gx", "gy"))),
        check_vma=False,
    )
```

```python
import functools
import itertools

import jax
import jax.numpy as jnp
from jax import lax
from jax.experimental import pallas as pl
from jax.experimental.pallas import tpu as pltpu
from jax.sharding import PartitionSpec as P

MESH = pl.DeviceIdType.MESH
APPLY = 8
FORM = 16
F32 = jnp.float32
BF16 = jnp.bfloat16


def parts(value):
    high = value.astype(BF16)
    return high, (value - high.astype(F32)).astype(BF16)


def mm(left, right):
    return jnp.dot(left, right, preferred_element_type=F32)


def mm_tn(left, right):
    return lax.dot_general(left, right, (((0,), (0,)), ((), ())), preferred_element_type=F32)


def exact(left, right):
    return lax.dot_general(
        left,
        right,
        (((1,), (0,)), ((), ())),
        precision=lax.Precision.HIGHEST,
        preferred_element_type=F32,
    )


def phases_of(mesh_sizes):
    sizes_x, sizes_y = mesh_sizes
    axes = []
    stride = 1
    for size in (2, 4, sizes_y):
        size = min(size, sizes_y // stride)
        if size > 1:
            axes.append(("gy", stride, size))
            stride *= size
    if sizes_x > 1:
        axes.append(("gx", 1, sizes_x))

    def phase(*members):
        steps = itertools.product(*[range(member[2]) for member in members])
        offsets = [list(zip(members, step)) for step in steps if any(step)]

        def hops(offset):
            return sum(min(steps, member[2] - steps) for member, steps in offset)

        return sorted(offsets, key=hops, reverse=True)

    return (
        [phase(axis) for axis in axes],
        [phase(*axes[:2]), phase(*axes[2:])],
        [phase(*axes[:2])] + [phase(axis) for axis in axes[2:]],
    )


def system_kernel(
    sizes,
    phases,
    arch,
    param,
    theta,
    refs_hbm,
    mask_hbm,
    cut_hbm,
    inverse_hbm,
    loads_hbm,
    stiff_hbm,
    coupling_hbm,
    first_hbm,
    second_hbm,
    small_out,
    refs_in,
    mask_in,
    cut_in,
    inverse,
    loads,
    stiff_top,
    stiff_low,
    coupling,
    couple_parts,
    blocks,
    field,
    running,
    load_parts,
    first_parts,
    second_parts,
    second_out,
    landed,
    send_a,
    recv_a,
    send_l,
    recv_l,
    send_p,
    recv_p,
    send_t,
    recv_t,
    index_rows,
    index,
    load_sem,
    send_sem,
    recv_sem,
    *reducers,
):
    sizes_x, sizes_y = sizes
    comps = coupling.shape[0]
    bubbles = coupling.shape[1]
    cols, dofs = loads.shape[0], field.shape[2] // 2
    owned = loads.shape[1] // dofs
    slot_count = refs_in.shape[0]
    refs = comps * slot_count
    width = slot_count * dofs
    cut = cut_in.shape[1]
    half = cut // 2
    ext = owned + cut
    quarter_comps = comps // 4
    PICK, PREV, LAST, CUT, BACK = range(5)

    my_x, my_y = lax.axis_index("gx"), lax.axis_index("gy")
    here = my_x * sizes_y + my_y
    total = sizes_x * sizes_y
    after = lax.rem(here + 1, total)
    before = lax.rem(here + total - 1, total)
    next_id = (after // sizes_y, lax.rem(after, sizes_y))
    prev_id = (before // sizes_y, lax.rem(before, sizes_y))

    def peer(offset):
        x, y = my_x, my_y
        for (axis, stride, size), steps in offset:
            if steps and axis == "gx":
                x = lax.rem(my_x + steps, size)
            elif steps:
                place = lax.rem(my_y // stride, size)
                y = y + (lax.rem(place + steps, size) - place) * stride
        return (x, y)

    small_copies = []
    for number, (source, target) in enumerate(
        ((refs_hbm, refs_in), (mask_hbm, mask_in), (cut_hbm, cut_in), (inverse_hbm, inverse))
    ):
        copy = pltpu.make_async_copy(source, target, load_sem.at[1 + number])
        copy.start()
        small_copies.append(copy)
    load_copy = pltpu.make_async_copy(loads_hbm, loads, load_sem.at[0])
    load_copy.start()
    coupling_copy = pltpu.make_async_copy(coupling_hbm, coupling, load_sem.at[5])
    coupling_copy.start()
    middle_at = width // 2
    bands = ((0, 0, stiff_top), (middle_at, middle_at, stiff_low))
    stiff_copies = []
    for band, (start, begin, target) in enumerate(bands):
        at = (slice(None), pl.ds(start, middle_at), pl.ds(begin, width - begin))
        copy = pltpu.make_async_copy(stiff_hbm.at[at], target, load_sem.at[6 + band])
        copy.start()
        stiff_copies.append(copy)

    barrier = pltpu.get_barrier_semaphore()
    targets = [next_id, prev_id]
    targets += [peer(offset) for phase in phases[1] for offset in phase]
    for target in targets:
        pl.semaphore_signal(barrier, inc=1, device_id=target, device_id_type=MESH)

    left_lanes = lax.broadcasted_iota(jnp.int32, (cols, 128), 1) < dofs
    left_both = lax.broadcasted_iota(jnp.int32, (2 * cols, 128), 1) < dofs

    def fold(value):
        return value + pltpu.roll(value, dofs, 1)

    def keep(place, full):
        field[place, :cols], field[place, cols:] = parts(full)

    def keep_pair(target, at, one, two):
        target[:cols, at], target[cols:, at] = parts(jnp.where(left_lanes, one, two))

    def lanes_of(b):
        return pl.ds(pl.multiple_of(b * 128, 128), 128)

    def send(number, source, target_ref, device):
        return pltpu.make_async_remote_copy(
            src_ref=source,
            dst_ref=target_ref,
            send_sem=send_sem.at[number],
            recv_sem=recv_sem.at[number],
            device_id=device,
            device_id_type=MESH,
        )

    def loop(count, unroll, body):
        def step(b, carry):
            for u in range(unroll):
                body(b * unroll + u)
            return carry

        lax.fori_loop(0, count // unroll, step, 0)

    def unpack(pair):
        other = pltpu.roll(pair, dofs, 1)
        return jnp.where(left_lanes, pair, other), jnp.where(left_lanes, other, pair)

    def expand(received):
        def body(g):
            landed[g], landed[g + half] = unpack(received[g])

        loop(half, 4, body)

    def widen(row):
        return jnp.concatenate(
            [row, jnp.zeros((row.shape[0], 128 - row.shape[1]), row.dtype)], axis=1
        )

    for copy in small_copies:
        copy.wait()
    picks = widen(jnp.where(mask_in[...] != 0, refs_in[...], ext)).T[:comps]
    comp_lane = lax.broadcasted_iota(jnp.int32, (comps, refs), 1)
    comp_row = lax.broadcasted_iota(jnp.int32, (comps, refs), 0)
    wide = jnp.zeros((comps, refs), jnp.int32)
    for j in range(slot_count):
        wide = jnp.where(comp_lane == comp_row * slot_count + j, picks[:, j : j + 1], wide)
    pick_row = jnp.sum(wide, axis=0, keepdims=True)
    pick_row = jnp.clip(pick_row, 0, ext)
    down = lax.broadcasted_iota(jnp.int32, (refs, 128), 0)
    across = lax.broadcasted_iota(jnp.int32, (refs, 128), 1)
    pick_down = jnp.broadcast_to(pick_row, (refs, refs)).T
    same = (pick_down == pick_row) & (pick_down < ext) & (down < across)
    previous = jnp.max(jnp.where(same, down, -1), axis=0, keepdims=True)
    final = jnp.max(jnp.where((pick_down == across) & (across < ext), down, -1), axis=0, keepdims=True)
    cut_rows = widen(cut_in[...])
    lane_row = lax.broadcasted_iota(jnp.int32, (1, 128), 1)
    cut_marked = jnp.where(lane_row < cut, cut_rows, -1)
    cut_down = jnp.broadcast_to(cut_marked, (refs, 128)).T
    back_row = jnp.max(jnp.where(cut_down == across, down, -1), axis=0, keepdims=True)
    index_rows[PICK : PICK + 1, :] = pick_row
    index_rows[PREV : PREV + 1, :] = jnp.where(previous < 0, refs, previous)
    index_rows[LAST : LAST + 1, :] = jnp.where(final < 0, refs, final)
    index_rows[CUT : CUT + 1, :] = jnp.clip(cut_rows, 0, owned - 1)
    index_rows[BACK : BACK + 1, :] = jnp.where(back_row < 0, cut, back_row)
    index_copy = pltpu.make_async_copy(index_rows, index, load_sem.at[10])
    index_copy.start()
    def pack(target, source):
        def body(g):
            target[g] = jnp.where(left_lanes, source(g), source(g + half))

        loop(half, 4, body)

    def ghost_total(g):
        return running[index[LAST, owned + g]]

    def apply(start, count):
        def pick(c):
            first = c * slot_count
            return jnp.concatenate(
                [
                    jnp.where(
                        left_both, field[index[PICK, first + j]], field[index[PICK, first + j + 1]]
                    )
                    for j in range(0, slot_count, 2)
                ],
                axis=1,
            )

        def times(c, left, side):
            at = side * width
            near = pl.ds(at, middle_at)
            far = pl.ds(at + middle_at, middle_at)
            return jnp.concatenate(
                [
                    mm(left[:, :middle_at], blocks[c, :middle_at, near])
                    + mm_nt(left[:, middle_at:], blocks[c, :middle_at, far]),
                    mm(left, blocks[c, :, far]),
                ],
                axis=1,
            )

        def multiply(c, picked):
            both = times(c, picked, 0)
            return both[:cols] + both[cols:] + times(c, picked[:cols], 1)

        def add(c, product):
            first = c * slot_count
            for j in range(0, slot_count, 2):
                one, two = unpack(product[:, j * dofs : (j + 2) * dofs])
                running[first + j] = running[index[PREV, first + j]] + one
                running[first + j + 1] = running[index[PREV, first + j + 1]] + two

        def body(b, carry):
            places = [start + b * APPLY + u for u in range(APPLY)]
            picked = [pick(c) for c in places]
            products = [multiply(c, value) for c, value in zip(places, picked)]
            for c, product in zip(places, products):
                add(c, product)
            return carry

        lax.fori_loop(0, count // APPLY, body, 0)

    def gram(left, right):
        both = mm_nt(left, right)
        rows = both[:cols] + both[cols:]
        full = fold(rows)
        return jnp.where(left_lanes[: cols // 2], full[: cols // 2], full[cols // 2 :])

    sent = []

    def reduction(number, kind, value):
        sums, slots, sum_send, sum_recv = reducers[4 * number : 4 * number + 4]
        count = 0
        for level, phase in enumerate(phases[kind]):
            sums[level] = value
            copies = []
            for offset in phase:
                copy = pltpu.make_async_remote_copy(
                    src_ref=sums.at[level],
                    dst_ref=slots.at[count],
                    send_sem=sum_send.at[count],
                    recv_sem=sum_recv.at[count],
                    device_id=peer(offset),
                    device_id_type=MESH,
                )
                copy.start()
                copies.append((copy, count))
                count += 1
            sent.extend(copy for copy, at in copies)
            yield None
            for copy, at in copies:
                copy.wait_recv()
            for copy, at in copies:
                value = value + slots[at]
        yield value

    def advance(steps):
        return next(steps)

    def square_of(packed):
        other = pltpu.roll(packed, cols, 1)
        return jnp.concatenate([packed, other], axis=0)[:, :cols]

    load_copy.wait()

    def spread(b):
        at = lanes_of(b)
        piece = loads[:, at]
        load_parts[:cols, at], load_parts[cols:, at] = parts(piece)
        running[2 * b], running[2 * b + 1] = one, two = unpack(piece)
        keep(2 * b, one)
        keep(2 * b + 1, two)

    loop(owned // 2, 4, spread)
    index_copy.wait()
    pack(send_a, lambda g: running[index[CUT, g]])
    running[refs] = jnp.zeros((cols, 128), F32)
    landed[cut] = jnp.zeros((cols, 128), F32)
    field[ext] = jnp.zeros((2 * cols, 128), BF16)
    pl.semaphore_wait(barrier, len(targets))
    ghosts = send(0, send_a, recv_a, next_id)
    ghosts.start()
    quarter = cols // 2
    own_gram = gram(load_parts[...], load_parts[...])

    coupling_copy.wait()

    def move(c):
        couple_high, couple_low = parts(coupling[c])
        inverse_high, inverse_low = parts(inverse[arch[c]])
        moved = (
            mm(inverse_high, couple_high)
            + mm(inverse_high, couple_low)
            + mm(inverse_low, couple_high)
        )
        moved_high, moved_low = parts(moved)
        couple_parts[c, :bubbles] = couple_high
        couple_parts[c, bubbles : 2 * bubbles] = couple_low
        couple_parts[c, 2 * bubbles : 3 * bubbles] = moved_high
        couple_parts[c, 3 * bubbles :] = moved_low

    loop(comps, 2, move)

    def form(band, c):
        kind = arch[c]
        weight0, weight1 = theta[0, param[c]], theta[1, param[c]]
        first_row, begin, stiff = bands[band]
        right_of = pl.ds(begin, width - begin)
        moved_high = couple_parts[c, 2 * bubbles : 3 * bubbles, right_of]
        moved_low = couple_parts[c, 3 * bubbles :, right_of]
        moved = jnp.concatenate([moved_high, moved_high, moved_low], axis=0)
        for start in range(first_row, first_row + middle_at, 128):
            rows = pl.ds(start, 128)
            couple_both = couple_parts[c, : 2 * bubbles, rows]
            bubble = mm_tn(jnp.concatenate([couple_both, couple_both[:bubbles]], axis=0), moved)
            block = (
                weight0 * (stiff[2 * kind, pl.ds(start - first_row, 128), :] - bubble)
                + weight1 * stiff[2 * kind + 1, pl.ds(start - first_row, 128), :]
            )
            high, low = parts(block)
            blocks[c, rows, right_of] = high
            blocks[c, rows, pl.ds(width + begin, width - begin)] = low

    load_steps = reduction(0, 0, own_gram)
    load_gram = advance(load_steps)
    for band in range(len(bands)):
        stiff_copies[band].wait()
        loop(comps, FORM, functools.partial(form, band))
    load_gram = advance(load_steps)

    ghosts.wait()

    def take_ghosts(g):
        one, two = unpack(recv_a[g])
        keep(owned + g, one)
        keep(owned + half + g, two)

    loop(half, 4, take_ghosts)

    apply(0, comps // 2)
    apply(comps // 2, comps // 2)

    pack(send_p, ghost_total)
    back = send(1, send_p, recv_p, prev_id)
    back.start()
    pack(send_l, lambda g: running[index[LAST, index[CUT, g]]])
    forth = send(2, send_l, recv_l, next_id)
    forth.start()
    load_gram = advance(load_steps)
    back.wait()
    expand(recv_p)

    def first_owned(b):
        one, two = [running[index[LAST, p]] + landed[index[BACK, p]] for p in (2 * b, 2 * b + 1)]
        keep(2 * b, one)
        keep(2 * b + 1, two)
        keep_pair(first_parts, lanes_of(b), one, two)

    loop(owned // 2, 4, first_owned)
    forth.wait()
    expand(recv_l)

    def first_ghost(b):
        one, two = [ghost_total(g) + landed[g] for g in (2 * b, 2 * b + 1)]
        keep(owned + 2 * b, one)
        keep(owned + 2 * b + 1, two)
        keep_pair(first_parts, lanes_of(owned // 2 + b), one, two)

    loop(half, 4, first_ghost)

    first_owned_parts = first_parts[:, : owned * dofs]
    first_copy = pltpu.make_async_copy(
        first_parts.at[:, pl.ds(0, owned * dofs)], first_hbm, load_sem.at[8]
    )
    first_copy.start()
    middle_steps = reduction(
        1,
        2,
        jnp.concatenate(
            [gram(load_parts[...], first_owned_parts), gram(first_owned_parts, first_owned_parts)],
            axis=0,
        ),
    )
    middle = advance(middle_steps)
    apply(0, comps // 2)
    if load_gram is None:
        load_gram = advance(load_steps)
    apply(comps // 2, comps // 2)

    def second_partial(b):
        one, two = [running[index[LAST, p]] for p in (2 * b, 2 * b + 1)]
        keep_pair(second_parts, lanes_of(b), one, two)

    loop(ext // 2, 4, second_partial)
    cube_steps = reduction(2, 1, gram(first_parts[...], second_parts[...]))
    cube = advance(cube_steps)
    pack(send_t, ghost_total)
    last_back = send(3, send_t, recv_t, prev_id)
    last_back.start()
    middle = advance(middle_steps)
    while load_gram is None:
        load_gram = advance(load_steps)
    cube = advance(cube_steps)
    if middle is None:
        middle = advance(middle_steps)

    last_back.wait()
    expand(recv_t)

    def second_owned(b):
        one, two = [running[index[LAST, p]] + landed[index[BACK, p]] for p in (2 * b, 2 * b + 1)]
        keep_pair(second_out, lanes_of(b), one, two)

    loop(owned // 2, 4, second_owned)
    second_copy = pltpu.make_async_copy(second_out, second_hbm, load_sem.at[9])
    second_copy.start()
    while middle is None:
        middle = advance(middle_steps)
    load_gram, cross, square = [
        square_of(packed) for packed in (load_gram, middle[:quarter], middle[quarter:])
    ]
    solved = elimination(
        [jnp.concatenate([cross, square], axis=1), jnp.concatenate([load_gram, load_gram], axis=1)]
    )
    moved = solved[0][:, cols:]
    step = solved[1][:, :cols]
    small_out[0, :, cols:] = cross - exact(square, step)
    small_out[1, :, :cols] = moved
    small_out[1, :, cols:] = step
    while cube is None:
        cube = advance(cube_steps)
    small_out[0, :, :cols] = square_of(cube) - exact(square, moved)
    for copy in sent:
        copy.wait_send()
    first_copy.wait()
    second_copy.wait()


def elimination(tiles, block=8, midway=None):
    size = tiles[0].shape[0]
    row_index = lax.broadcasted_iota(jnp.int32, (size, 1), 0)
    for k in range(0, size, block):
        if midway is not None and k == size // 2:
            midway()
        wide = [jnp.broadcast_to(tiles[0][:, k + j : k + j + 1], tiles[0].shape) for j in range(block)]
        pivots = [[wide[j][k + i : k + i + 1] for j in range(block)] for i in range(block)]
        rows = [[tile[k + i : k + i + 1] for tile in tiles] for i in range(block)]
        for i in range(block):
            scale = 1.0 / pivots[i][i]
            rows[i] = [row * scale for row in rows[i]]
            for j in range(i + 1, block):
                pivots[i][j] = pivots[i][j] * scale
            for m in range(i + 1, block):
                factor = pivots[m][i]
                rows[m] = [row - factor * other for row, other in zip(rows[m], rows[i])]
                for j in range(i + 1, block):
                    pivots[m][j] = pivots[m][j] - factor * pivots[i][j]
        for i in range(block - 1, 0, -1):
            for m in range(i):
                rows[m] = [row - pivots[m][i] * other for row, other in zip(rows[m], rows[i])]
        out = []
        for number, tile in enumerate(tiles):
            new = tile
            for j in range(block):
                new = new - wide[j] * rows[j][number]
            for j in range(block):
                new = jnp.where(row_index == k + j, rows[j][number], new)
            out.append(new)
        tiles = out
    return tiles


def combine_kernel(small, loads_hbm, first_hbm, second_hbm, solution_hbm, residual_hbm, loads, load_parts, first, second, solution, residual, sems):
    cols = loads.shape[0]
    copies = []
    for number, (source, target) in enumerate(
        ((loads_hbm, loads), (first_hbm, first), (second_hbm, second))
    ):
        copy = pltpu.make_async_copy(source, target, sems.at[number])
        copy.start()
        copies.append(copy)

    def split_loads():
        copies[0].wait()
        load_parts[:cols, :], load_parts[cols:, :] = parts(loads[...])

    (solved,) = elimination([small[0]], midway=split_loads)
    second_weight = solved[:, cols:]
    first_weight = small[1, :, cols:] - exact(small[1, :, :cols], second_weight)

    top_high, top_low = parts(first_weight.T)
    low_high, low_low = parts(second_weight.T)
    left = jnp.concatenate([top_high, top_high, top_low, low_high, low_high, low_low], axis=1)
    for copy in copies[1:]:
        copy.wait()

    chunk = 512
    writes = []
    for b in range(loads.shape[1] // chunk):
        at = pl.ds(b * chunk, chunk)
        load_piece, first_piece, second_piece = loads[:, at], first[:, at], second[:, at]
        both_piece = load_parts[:, at]
        solution[:, at] = mm(
            left,
            jnp.concatenate(
                [both_piece, both_piece[:cols], first_piece, first_piece[:cols]], axis=0
            ),
        )
        residual[:, at] = load_piece - mm(
            left,
            jnp.concatenate(
                [first_piece, first_piece[:cols], second_piece, second_piece[:cols]], axis=0
            ),
        )
        for number, (source, target) in enumerate(
            ((solution, solution_hbm), (residual, residual_hbm))
        ):
            copy = pltpu.make_async_copy(
                source.at[:, at], target.at[:, at], sems.at[3 + 2 * b + number]
            )
            copy.start()
            writes.append(copy)
    for copy in writes:
        copy.wait()


def mm_nt(left, right):
    return lax.dot_general(left, right, (((1,), (1,)), ((), ())), preferred_element_type=F32)


def local(
    sizes,
    port_loads,
    port_stiff,
    bubble_inverse,
    coupling,
    theta_table,
    comp_arch,
    comp_param,
    port_refs,
    slot_mask,
    cut_source,
):
    cols = port_loads.shape[0]
    comps, slot_count = port_refs.shape
    width = port_stiff.shape[2]
    dofs = width // slot_count
    cut = cut_source.shape[1]
    owned = port_loads.shape[1] // dofs
    refs = comps * slot_count
    ext = owned + cut
    archs, terms = port_stiff.shape[:2]
    bubbles = coupling.shape[1]

    phases = phases_of(sizes)
    smem = pl.BlockSpec(memory_space=pltpu.SMEM)
    vmem = pl.BlockSpec(memory_space=pltpu.VMEM)
    hbm = pl.BlockSpec(memory_space=pl.ANY)
    reducers = []
    for kind, rows in ((0, cols // 2), (2, cols), (1, cols // 2)):
        messages = sum(len(phase) for phase in phases[kind])
        reducers += [
            pltpu.VMEM((len(phases[kind]), rows, 128), F32),
            pltpu.VMEM((messages, rows, 128), F32),
            pltpu.SemaphoreType.DMA((messages,)),
            pltpu.SemaphoreType.DMA((messages,)),
        ]
    exchange = pltpu.VMEM((cut // 2, cols, 128), F32)
    flops = 2 * comps * cols * width * width * 9
    first, second, small = pl.pallas_call(
        functools.partial(system_kernel, sizes, phases),
        out_shape=(
            jax.ShapeDtypeStruct((2 * cols, owned * dofs), BF16),
            jax.ShapeDtypeStruct((2 * cols, owned * dofs), BF16),
            jax.ShapeDtypeStruct((2, cols, 2 * cols), F32),
        ),
        in_specs=[smem, smem, smem] + [hbm] * 7,
        out_specs=(hbm, hbm, vmem),
        scratch_shapes=[
            pltpu.VMEM((slot_count, comps), jnp.int32),
            pltpu.VMEM((slot_count, comps), jnp.int32),
            pltpu.VMEM(cut_source.shape, jnp.int32),
            pltpu.VMEM(bubble_inverse.shape, F32),
            pltpu.VMEM(port_loads.shape, F32),
            pltpu.VMEM((archs * terms, width // 2, width), F32),
            pltpu.VMEM((archs * terms, width // 2, width // 2), F32),
            pltpu.VMEM(coupling.shape, F32),
            pltpu.VMEM((comps, 4 * bubbles, width), BF16),
            pltpu.VMEM((comps, width, 2 * width), BF16),
            pltpu.VMEM((ext + 1, 2 * cols, 128), BF16),
            pltpu.VMEM((refs + 1, cols, 128), F32),
            pltpu.VMEM((2 * cols, owned * dofs), BF16),
            pltpu.VMEM((2 * cols, ext * dofs), BF16),
            pltpu.VMEM((2 * cols, ext * dofs), BF16),
            pltpu.VMEM((2 * cols, owned * dofs), BF16),
            pltpu.VMEM((cut + 1, cols, 128), F32),
        ]
        + [exchange] * 8
        + [
            pltpu.VMEM((8, 128), jnp.int32),
            pltpu.SMEM((8, 128), jnp.int32),
            pltpu.SemaphoreType.DMA((11,)),
            pltpu.SemaphoreType.DMA((4,)),
            pltpu.SemaphoreType.DMA((4,)),
        ]
        + reducers,
        compiler_params=pltpu.CompilerParams(
            collective_id=0, has_side_effects=True, vmem_limit_bytes=60 * 1024 * 1024
        ),
        cost_estimate=pl.CostEstimate(flops=flops, bytes_accessed=12 << 20, transcendentals=0),
        name="system",
    )(
        comp_arch,
        comp_param,
        theta_table.T,
        port_refs.T,
        slot_mask.T,
        cut_source,
        bubble_inverse,
        port_loads,
        port_stiff.reshape(archs * terms, width, width),
        coupling,
    )
    return pl.pallas_call(
        combine_kernel,
        out_shape=(
            jax.ShapeDtypeStruct(port_loads.shape, F32),
            jax.ShapeDtypeStruct(port_loads.shape, F32),
        ),
        in_specs=[vmem, hbm, hbm, hbm],
        out_specs=(hbm, hbm),
        scratch_shapes=[
            pltpu.VMEM(port_loads.shape, F32),
            pltpu.VMEM((2 * cols, owned * dofs), BF16),
            pltpu.VMEM((2 * cols, owned * dofs), BF16),
            pltpu.VMEM((2 * cols, owned * dofs), BF16),
            pltpu.VMEM(port_loads.shape, F32),
            pltpu.VMEM(port_loads.shape, F32),
            pltpu.SemaphoreType.DMA((3 + 2 * (owned * dofs // 512),)),
        ],
        compiler_params=pltpu.CompilerParams(vmem_limit_bytes=60 * 1024 * 1024),
        cost_estimate=pl.CostEstimate(flops=1 << 28, bytes_accessed=4 << 20, transcendentals=0),
        name="combine",
    )(small, port_loads, first, second)


def solution(mesh):
    sizes = (mesh.shape["gx"], mesh.shape["gy"])
    placed = (
        P(None, ("gx", "gy")),
        P(),
        P(),
        P(("gx", "gy"), None, None),
        P(),
        P(("gx", "gy")),
        P(("gx", "gy")),
        P(("gx", "gy"), None),
        P(("gx", "gy"), None),
        P(("gx", "gy"), None),
    )
    return jax.shard_map(
        functools.partial(local, sizes),
        mesh=mesh,
        in_specs=placed,
        out_specs=(P(None, ("gx", "gy")), P(None, ("gx", "gy"))),
        check_vma=False,
    )
```

```python
import functools
import itertools

import jax
import jax.numpy as jnp
from jax import lax
from jax.experimental import pallas as pl
from jax.experimental.pallas import tpu as pltpu
from jax.sharding import PartitionSpec as P

MESH = pl.DeviceIdType.MESH
APPLY = 8
FORM = 16
F32 = jnp.float32
BF16 = jnp.bfloat16


def parts(value):
    high = value.astype(BF16)
    return high, (value - high.astype(F32)).astype(BF16)


def mm(left, right):
    return jnp.dot(left, right, preferred_element_type=F32)


def mm_tn(left, right):
    return lax.dot_general(left, right, (((0,), (0,)), ((), ())), preferred_element_type=F32)


def exact(left, right):
    return lax.dot_general(
        left,
        right,
        (((1,), (0,)), ((), ())),
        precision=lax.Precision.HIGHEST,
        preferred_element_type=F32,
    )


def phases_of(mesh_sizes):
    sizes_x, sizes_y = mesh_sizes
    axes = []
    stride = 1
    for size in (2, 4, sizes_y):
        size = min(size, sizes_y // stride)
        if size > 1:
            axes.append(("gy", stride, size))
            stride *= size
    if sizes_x > 1:
        axes.append(("gx", 1, sizes_x))

    def phase(*members):
        steps = itertools.product(*[range(member[2]) for member in members])
        offsets = [list(zip(members, step)) for step in steps if any(step)]

        def hops(offset):
            return sum(min(steps, member[2] - steps) for member, steps in offset)

        return sorted(offsets, key=hops, reverse=True)

    return (
        [phase(axis) for axis in axes],
        [phase(*axes[:2]), phase(*axes[2:])],
        [phase(*axes[:2])] + [phase(axis) for axis in axes[2:]],
    )


def system_kernel(
    sizes,
    phases,
    arch,
    param,
    theta,
    refs_hbm,
    mask_hbm,
    cut_hbm,
    inverse_hbm,
    loads_hbm,
    stiff_hbm,
    coupling_hbm,
    first_hbm,
    second_hbm,
    small_out,
    refs_in,
    mask_in,
    cut_in,
    inverse,
    loads,
    stiff_top,
    stiff_low,
    coupling,
    couple_parts,
    blocks,
    field,
    running,
    load_parts,
    first_parts,
    second_parts,
    second_out,
    landed,
    send_a,
    recv_a,
    send_l,
    recv_l,
    send_p,
    recv_p,
    send_t,
    recv_t,
    index_rows,
    index,
    load_sem,
    send_sem,
    recv_sem,
    *reducers,
):
    sizes_x, sizes_y = sizes
    comps = coupling.shape[0]
    bubbles = coupling.shape[1]
    cols, dofs = loads.shape[0], field.shape[2] // 2
    owned = loads.shape[1] // dofs
    slot_count = refs_in.shape[0]
    refs = comps * slot_count
    width = slot_count * dofs
    cut = cut_in.shape[1]
    half = cut // 2
    ext = owned + cut
    quarter_comps = comps // 4
    PICK, PREV, LAST, CUT, BACK = range(5)

    my_x, my_y = lax.axis_index("gx"), lax.axis_index("gy")
    here = my_x * sizes_y + my_y
    total = sizes_x * sizes_y
    after = lax.rem(here + 1, total)
    before = lax.rem(here + total - 1, total)
    next_id = (after // sizes_y, lax.rem(after, sizes_y))
    prev_id = (before // sizes_y, lax.rem(before, sizes_y))

    def peer(offset):
        x, y = my_x, my_y
        for (axis, stride, size), steps in offset:
            if steps and axis == "gx":
                x = lax.rem(my_x + steps, size)
            elif steps:
                place = lax.rem(my_y // stride, size)
                y = y + (lax.rem(place + steps, size) - place) * stride
        return (x, y)

    small_copies = []
    for number, (source, target) in enumerate(
        ((refs_hbm, refs_in), (mask_hbm, mask_in), (cut_hbm, cut_in), (inverse_hbm, inverse))
    ):
        copy = pltpu.make_async_copy(source, target, load_sem.at[1 + number])
        copy.start()
        small_copies.append(copy)
    load_copy = pltpu.make_async_copy(loads_hbm, loads, load_sem.at[0])
    load_copy.start()
    coupling_copy = pltpu.make_async_copy(coupling_hbm, coupling, load_sem.at[5])
    coupling_copy.start()
    middle_at = width // 2
    bands = ((0, 0, stiff_top), (middle_at, middle_at, stiff_low))
    stiff_copies = []
    for band, (start, begin, target) in enumerate(bands):
        at = (slice(None), pl.ds(start, middle_at), pl.ds(begin, width - begin))
        copy = pltpu.make_async_copy(stiff_hbm.at[at], target, load_sem.at[6 + band])
        copy.start()
        stiff_copies.append(copy)

    barrier = pltpu.get_barrier_semaphore()
    targets = [next_id, prev_id]
    targets += [peer(offset) for phase in phases[1] for offset in phase]
    for target in targets:
        pl.semaphore_signal(barrier, inc=1, device_id=target, device_id_type=MESH)

    left_lanes = lax.broadcasted_iota(jnp.int32, (cols, 128), 1) < dofs
    left_both = lax.broadcasted_iota(jnp.int32, (2 * cols, 128), 1) < dofs

    def fold(value):
        return value + pltpu.roll(value, dofs, 1)

    def keep(place, full):
        field[place, :cols], field[place, cols:] = parts(full)

    def keep_pair(target, at, one, two):
        target[:cols, at], target[cols:, at] = parts(jnp.where(left_lanes, one, two))

    def lanes_of(b):
        return pl.ds(pl.multiple_of(b * 128, 128), 128)

    def send(number, source, target_ref, device):
        return pltpu.make_async_remote_copy(
            src_ref=source,
            dst_ref=target_ref,
            send_sem=send_sem.at[number],
            recv_sem=recv_sem.at[number],
            device_id=device,
            device_id_type=MESH,
        )

    def loop(count, unroll, body):
        def step(b, carry):
            for u in range(unroll):
                body(b * unroll + u)
            return carry

        lax.fori_loop(0, count // unroll, step, 0)

    def unpack(pair):
        other = pltpu.roll(pair, dofs, 1)
        return jnp.where(left_lanes, pair, other), jnp.where(left_lanes, other, pair)

    def expand(received):
        def body(g):
            landed[g], landed[g + half] = unpack(received[g])

        loop(half, 4, body)

    def widen(row):
        return jnp.concatenate(
            [row, jnp.zeros((row.shape[0], 128 - row.shape[1]), row.dtype)], axis=1
        )

    for copy in small_copies:
        copy.wait()
    picks = widen(jnp.where(mask_in[...] != 0, refs_in[...], ext)).T[:comps]
    comp_lane = lax.broadcasted_iota(jnp.int32, (comps, refs), 1)
    comp_row = lax.broadcasted_iota(jnp.int32, (comps, refs), 0)
    wide = jnp.zeros((comps, refs), jnp.int32)
    for j in range(slot_count):
        wide = jnp.where(comp_lane == comp_row * slot_count + j, picks[:, j : j + 1], wide)
    pick_row = jnp.sum(wide, axis=0, keepdims=True)
    pick_row = jnp.clip(pick_row, 0, ext)
    down = lax.broadcasted_iota(jnp.int32, (refs, 128), 0)
    across = lax.broadcasted_iota(jnp.int32, (refs, 128), 1)
    pick_down = jnp.broadcast_to(pick_row, (refs, refs)).T
    same = (pick_down == pick_row) & (pick_down < ext) & (down < across)
    previous = jnp.max(jnp.where(same, down, -1), axis=0, keepdims=True)
    final = jnp.max(jnp.where((pick_down == across) & (across < ext), down, -1), axis=0, keepdims=True)
    cut_rows = widen(cut_in[...])
    lane_row = lax.broadcasted_iota(jnp.int32, (1, 128), 1)
    cut_marked = jnp.where(lane_row < cut, cut_rows, -1)
    cut_down = jnp.broadcast_to(cut_marked, (refs, 128)).T
    back_row = jnp.max(jnp.where(cut_down == across, down, -1), axis=0, keepdims=True)
    index_rows[PICK : PICK + 1, :] = pick_row
    index_rows[PREV : PREV + 1, :] = jnp.where(previous < 0, refs, previous)
    index_rows[LAST : LAST + 1, :] = jnp.where(final < 0, refs, final)
    index_rows[CUT : CUT + 1, :] = jnp.clip(cut_rows, 0, owned - 1)
    index_rows[BACK : BACK + 1, :] = jnp.where(back_row < 0, cut, back_row)
    index_copy = pltpu.make_async_copy(index_rows, index, load_sem.at[10])
    index_copy.start()
    def pack(target, source):
        def body(g):
            target[g] = jnp.where(left_lanes, source(g), source(g + half))

        loop(half, 4, body)

    def ghost_total(g):
        return running[index[LAST, owned + g]]

    def apply(start, count):
        def pick(c):
            first = c * slot_count
            return jnp.concatenate(
                [
                    jnp.where(
                        left_both, field[index[PICK, first + j]], field[index[PICK, first + j + 1]]
                    )
                    for j in range(0, slot_count, 2)
                ],
                axis=1,
            )

        def times(c, left, side):
            at = side * width
            near = pl.ds(at, middle_at)
            far = pl.ds(at + middle_at, middle_at)
            return jnp.concatenate(
                [
                    mm(left[:, :middle_at], blocks[c, :middle_at, near])
                    + mm_nt(left[:, middle_at:], blocks[c, :middle_at, far]),
                    mm(left, blocks[c, :, far]),
                ],
                axis=1,
            )

        def multiply(c, picked):
            both = times(c, picked, 0)
            return both[:cols] + both[cols:] + times(c, picked[:cols], 1)

        def add(c, product):
            first = c * slot_count
            for j in range(0, slot_count, 2):
                one, two = unpack(product[:, j * dofs : (j + 2) * dofs])
                running[first + j] = running[index[PREV, first + j]] + one
                running[first + j + 1] = running[index[PREV, first + j + 1]] + two

        def body(b, carry):
            places = [start + b * APPLY + u for u in range(APPLY)]
            picked = [pick(c) for c in places]
            products = [multiply(c, value) for c, value in zip(places, picked)]
            for c, product in zip(places, products):
                add(c, product)
            return carry

        lax.fori_loop(0, count // APPLY, body, 0)

    def gram(left, right):
        both = mm_nt(left, right)
        rows = both[:cols] + both[cols:]
        full = fold(rows)
        return jnp.where(left_lanes[: cols // 2], full[: cols // 2], full[cols // 2 :])

    sent = []

    def reduction(number, kind, value):
        sums, slots, sum_send, sum_recv = reducers[4 * number : 4 * number + 4]
        count = 0
        for level, phase in enumerate(phases[kind]):
            sums[level] = value
            copies = []
            for offset in phase:
                copy = pltpu.make_async_remote_copy(
                    src_ref=sums.at[level],
                    dst_ref=slots.at[count],
                    send_sem=sum_send.at[count],
                    recv_sem=sum_recv.at[count],
                    device_id=peer(offset),
                    device_id_type=MESH,
                )
                copy.start()
                copies.append((copy, count))
                count += 1
            sent.extend(copy for copy, at in copies)
            yield None
            for copy, at in copies:
                copy.wait_recv()
            for copy, at in copies:
                value = value + slots[at]
        yield value

    def advance(steps):
        return next(steps)

    def square_of(packed):
        other = pltpu.roll(packed, cols, 1)
        return jnp.concatenate([packed, other], axis=0)[:, :cols]

    load_copy.wait()

    def spread(b):
        running[2 * b], running[2 * b + 1] = unpack(loads[:, lanes_of(b)])

    loop(owned // 2, 4, spread)
    index_copy.wait()
    pack(send_a, lambda g: running[index[CUT, g]])
    running[refs] = jnp.zeros((cols, 128), F32)
    landed[cut] = jnp.zeros((cols, 128), F32)
    field[ext] = jnp.zeros((2 * cols, 128), BF16)
    pl.semaphore_wait(barrier, len(targets))
    ghosts = send(0, send_a, recv_a, next_id)
    ghosts.start()

    def spread_parts(b):
        at = lanes_of(b)
        load_parts[:cols, at], load_parts[cols:, at] = parts(loads[:, at])
        keep(2 * b, running[2 * b])
        keep(2 * b + 1, running[2 * b + 1])

    loop(owned // 2, 4, spread_parts)
    quarter = cols // 2
    own_gram = gram(load_parts[...], load_parts[...])

    coupling_copy.wait()

    def move(c):
        couple_high, couple_low = parts(coupling[c])
        inverse_high, inverse_low = parts(inverse[arch[c]])
        moved = (
            mm(inverse_high, couple_high)
            + mm(inverse_high, couple_low)
            + mm(inverse_low, couple_high)
        )
        moved_high, moved_low = parts(moved)
        couple_parts[c, :bubbles] = couple_high
        couple_parts[c, bubbles : 2 * bubbles] = couple_low
        couple_parts[c, 2 * bubbles : 3 * bubbles] = moved_high
        couple_parts[c, 3 * bubbles :] = moved_low

    loop(comps, 2, move)

    def form(band, c):
        kind = arch[c]
        weight0, weight1 = theta[0, param[c]], theta[1, param[c]]
        first_row, begin, stiff = bands[band]
        right_of = pl.ds(begin, width - begin)
        moved_high = couple_parts[c, 2 * bubbles : 3 * bubbles, right_of]
        moved_low = couple_parts[c, 3 * bubbles :, right_of]
        moved = jnp.concatenate([moved_high, moved_high, moved_low], axis=0)
        for start in range(first_row, first_row + middle_at, 128):
            rows = pl.ds(start, 128)
            couple_both = couple_parts[c, : 2 * bubbles, rows]
            bubble = mm_tn(jnp.concatenate([couple_both, couple_both[:bubbles]], axis=0), moved)
            block = (
                weight0 * (stiff[2 * kind, pl.ds(start - first_row, 128), :] - bubble)
                + weight1 * stiff[2 * kind + 1, pl.ds(start - first_row, 128), :]
            )
            high, low = parts(block)
            blocks[c, rows, right_of] = high
            blocks[c, rows, pl.ds(width + begin, width - begin)] = low

    load_steps = reduction(0, 0, own_gram)
    load_gram = advance(load_steps)
    for band in range(len(bands)):
        stiff_copies[band].wait()
        loop(comps, FORM, functools.partial(form, band))
    load_gram = advance(load_steps)

    ghosts.wait()

    def take_ghosts(g):
        one, two = unpack(recv_a[g])
        keep(owned + g, one)
        keep(owned + half + g, two)

    loop(half, 4, take_ghosts)

    apply(0, comps // 2)
    apply(comps // 2, comps // 2)

    pack(send_p, ghost_total)
    back = send(1, send_p, recv_p, prev_id)
    back.start()
    pack(send_l, lambda g: running[index[LAST, index[CUT, g]]])
    forth = send(2, send_l, recv_l, next_id)
    forth.start()
    load_gram = advance(load_steps)
    back.wait()
    expand(recv_p)

    def first_owned(b):
        one, two = [running[index[LAST, p]] + landed[index[BACK, p]] for p in (2 * b, 2 * b + 1)]
        keep(2 * b, one)
        keep(2 * b + 1, two)
        keep_pair(first_parts, lanes_of(b), one, two)

    loop(owned // 2, 4, first_owned)
    forth.wait()
    expand(recv_l)

    def first_ghost(b):
        one, two = [ghost_total(g) + landed[g] for g in (2 * b, 2 * b + 1)]
        keep(owned + 2 * b, one)
        keep(owned + 2 * b + 1, two)
        keep_pair(first_parts, lanes_of(owned // 2 + b), one, two)

    loop(half, 4, first_ghost)

    first_owned_parts = first_parts[:, : owned * dofs]
    first_copy = pltpu.make_async_copy(
        first_parts.at[:, pl.ds(0, owned * dofs)], first_hbm, load_sem.at[8]
    )
    first_copy.start()
    middle_steps = reduction(
        1,
        2,
        jnp.concatenate(
            [gram(load_parts[...], first_owned_parts), gram(first_owned_parts, first_owned_parts)],
            axis=0,
        ),
    )
    middle = advance(middle_steps)
    apply(0, comps // 2)
    if load_gram is None:
        load_gram = advance(load_steps)
    apply(comps // 2, comps // 2)

    def second_partial(b):
        one, two = [running[index[LAST, p]] for p in (2 * b, 2 * b + 1)]
        keep_pair(second_parts, lanes_of(b), one, two)

    loop(ext // 2, 4, second_partial)
    cube_steps = reduction(2, 1, gram(first_parts[...], second_parts[...]))
    cube = advance(cube_steps)
    pack(send_t, ghost_total)
    last_back = send(3, send_t, recv_t, prev_id)
    last_back.start()
    middle = advance(middle_steps)
    while load_gram is None:
        load_gram = advance(load_steps)
    cube = advance(cube_steps)
    if middle is None:
        middle = advance(middle_steps)

    last_back.wait()
    expand(recv_t)

    def second_owned(b):
        one, two = [running[index[LAST, p]] + landed[index[BACK, p]] for p in (2 * b, 2 * b + 1)]
        keep_pair(second_out, lanes_of(b), one, two)

    loop(owned // 2, 4, second_owned)
    second_copy = pltpu.make_async_copy(second_out, second_hbm, load_sem.at[9])
    second_copy.start()
    while middle is None:
        middle = advance(middle_steps)
    load_gram, cross, square = [
        square_of(packed) for packed in (load_gram, middle[:quarter], middle[quarter:])
    ]
    solved = elimination(
        [jnp.concatenate([cross, square], axis=1), jnp.concatenate([load_gram, load_gram], axis=1)]
    )
    moved = solved[0][:, cols:]
    step = solved[1][:, :cols]
    small_out[0, :, cols:] = cross - exact(square, step)
    small_out[1, :, :cols] = moved
    small_out[1, :, cols:] = step
    while cube is None:
        cube = advance(cube_steps)
    small_out[0, :, :cols] = square_of(cube) - exact(square, moved)
    for copy in sent:
        copy.wait_send()
    first_copy.wait()
    second_copy.wait()


def elimination(tiles, block=8, midway=None):
    size = tiles[0].shape[0]
    row_index = lax.broadcasted_iota(jnp.int32, (size, 1), 0)
    for k in range(0, size, block):
        if midway is not None and k == size // 2:
            midway()
        wide = [jnp.broadcast_to(tiles[0][:, k + j : k + j + 1], tiles[0].shape) for j in range(block)]
        pivots = [[wide[j][k + i : k + i + 1] for j in range(block)] for i in range(block)]
        rows = [[tile[k + i : k + i + 1] for tile in tiles] for i in range(block)]
        for i in range(block):
            scale = 1.0 / pivots[i][i]
            rows[i] = [row * scale for row in rows[i]]
            for j in range(i + 1, block):
                pivots[i][j] = pivots[i][j] * scale
            for m in range(i + 1, block):
                factor = pivots[m][i]
                rows[m] = [row - factor * other for row, other in zip(rows[m], rows[i])]
                for j in range(i + 1, block):
                    pivots[m][j] = pivots[m][j] - factor * pivots[i][j]
        for i in range(block - 1, 0, -1):
            for m in range(i):
                rows[m] = [row - pivots[m][i] * other for row, other in zip(rows[m], rows[i])]
        out = []
        for number, tile in enumerate(tiles):
            new = tile
            for j in range(block):
                new = new - wide[j] * rows[j][number]
            for j in range(block):
                new = jnp.where(row_index == k + j, rows[j][number], new)
            out.append(new)
        tiles = out
    return tiles


def combine_kernel(small, loads_hbm, first_hbm, second_hbm, solution_hbm, residual_hbm, loads, load_parts, first, second, solution, residual, sems):
    cols = loads.shape[0]
    copies = []
    for number, (source, target) in enumerate(
        ((loads_hbm, loads), (first_hbm, first), (second_hbm, second))
    ):
        copy = pltpu.make_async_copy(source, target, sems.at[number])
        copy.start()
        copies.append(copy)

    def split_loads():
        copies[0].wait()
        load_parts[:cols, :], load_parts[cols:, :] = parts(loads[...])

    (solved,) = elimination([small[0]], midway=split_loads)
    second_weight = solved[:, cols:]
    first_weight = small[1, :, cols:] - exact(small[1, :, :cols], second_weight)

    top_high, top_low = parts(first_weight.T)
    low_high, low_low = parts(second_weight.T)
    left = jnp.concatenate([top_high, top_high, top_low, low_high, low_high, low_low], axis=1)
    for copy in copies[1:]:
        copy.wait()

    chunk = 512
    writes = []
    for b in range(loads.shape[1] // chunk):
        at = pl.ds(b * chunk, chunk)
        load_piece, first_piece, second_piece = loads[:, at], first[:, at], second[:, at]
        both_piece = load_parts[:, at]
        solution[:, at] = mm(
            left,
            jnp.concatenate(
                [both_piece, both_piece[:cols], first_piece, first_piece[:cols]], axis=0
            ),
        )
        residual[:, at] = load_piece - mm(
            left,
            jnp.concatenate(
                [first_piece, first_piece[:cols], second_piece, second_piece[:cols]], axis=0
            ),
        )
        for number, (source, target) in enumerate(
            ((solution, solution_hbm), (residual, residual_hbm))
        ):
            copy = pltpu.make_async_copy(
                source.at[:, at], target.at[:, at], sems.at[3 + 2 * b + number]
            )
            copy.start()
            writes.append(copy)
    for copy in writes:
        copy.wait()


def mm_nt(left, right):
    return lax.dot_general(left, right, (((1,), (1,)), ((), ())), preferred_element_type=F32)


def local(
    sizes,
    port_loads,
    port_stiff,
    bubble_inverse,
    coupling,
    theta_table,
    comp_arch,
    comp_param,
    port_refs,
    slot_mask,
    cut_source,
):
    cols = port_loads.shape[0]
    comps, slot_count = port_refs.shape
    width = port_stiff.shape[2]
    dofs = width // slot_count
    cut = cut_source.shape[1]
    owned = port_loads.shape[1] // dofs
    refs = comps * slot_count
    ext = owned + cut
    archs, terms = port_stiff.shape[:2]
    bubbles = coupling.shape[1]

    phases = phases_of(sizes)
    smem = pl.BlockSpec(memory_space=pltpu.SMEM)
    vmem = pl.BlockSpec(memory_space=pltpu.VMEM)
    hbm = pl.BlockSpec(memory_space=pl.ANY)
    reducers = []
    for kind, rows in ((0, cols // 2), (2, cols), (1, cols // 2)):
        messages = sum(len(phase) for phase in phases[kind])
        reducers += [
            pltpu.VMEM((len(phases[kind]), rows, 128), F32),
            pltpu.VMEM((messages, rows, 128), F32),
            pltpu.SemaphoreType.DMA((messages,)),
            pltpu.SemaphoreType.DMA((messages,)),
        ]
    exchange = pltpu.VMEM((cut // 2, cols, 128), F32)
    flops = 2 * comps * cols * width * width * 9
    first, second, small = pl.pallas_call(
        functools.partial(system_kernel, sizes, phases),
        out_shape=(
            jax.ShapeDtypeStruct((2 * cols, owned * dofs), BF16),
            jax.ShapeDtypeStruct((2 * cols, owned * dofs), BF16),
            jax.ShapeDtypeStruct((2, cols, 2 * cols), F32),
        ),
        in_specs=[smem, smem, smem] + [hbm] * 7,
        out_specs=(hbm, hbm, vmem),
        scratch_shapes=[
            pltpu.VMEM((slot_count, comps), jnp.int32),
            pltpu.VMEM((slot_count, comps), jnp.int32),
            pltpu.VMEM(cut_source.shape, jnp.int32),
            pltpu.VMEM(bubble_inverse.shape, F32),
            pltpu.VMEM(port_loads.shape, F32),
            pltpu.VMEM((archs * terms, width // 2, width), F32),
            pltpu.VMEM((archs * terms, width // 2, width // 2), F32),
            pltpu.VMEM(coupling.shape, F32),
            pltpu.VMEM((comps, 4 * bubbles, width), BF16),
            pltpu.VMEM((comps, width, 2 * width), BF16),
            pltpu.VMEM((ext + 1, 2 * cols, 128), BF16),
            pltpu.VMEM((refs + 1, cols, 128), F32),
            pltpu.VMEM((2 * cols, owned * dofs), BF16),
            pltpu.VMEM((2 * cols, ext * dofs), BF16),
            pltpu.VMEM((2 * cols, ext * dofs), BF16),
            pltpu.VMEM((2 * cols, owned * dofs), BF16),
            pltpu.VMEM((cut + 1, cols, 128), F32),
        ]
        + [exchange] * 8
        + [
            pltpu.VMEM((8, 128), jnp.int32),
            pltpu.SMEM((8, 128), jnp.int32),
            pltpu.SemaphoreType.DMA((11,)),
            pltpu.SemaphoreType.DMA((4,)),
            pltpu.SemaphoreType.DMA((4,)),
        ]
        + reducers,
        compiler_params=pltpu.CompilerParams(
            collective_id=0, has_side_effects=True, vmem_limit_bytes=60 * 1024 * 1024
        ),
        cost_estimate=pl.CostEstimate(flops=flops, bytes_accessed=12 << 20, transcendentals=0),
        name="system",
    )(
        comp_arch,
        comp_param,
        theta_table.T,
        port_refs.T,
        slot_mask.T,
        cut_source,
        bubble_inverse,
        port_loads,
        port_stiff.reshape(archs * terms, width, width),
        coupling,
    )
    return pl.pallas_call(
        combine_kernel,
        out_shape=(
            jax.ShapeDtypeStruct(port_loads.shape, F32),
            jax.ShapeDtypeStruct(port_loads.shape, F32),
        ),
        in_specs=[vmem, hbm, hbm, hbm],
        out_specs=(hbm, hbm),
        scratch_shapes=[
            pltpu.VMEM(port_loads.shape, F32),
            pltpu.VMEM((2 * cols, owned * dofs), BF16),
            pltpu.VMEM((2 * cols, owned * dofs), BF16),
            pltpu.VMEM((2 * cols, owned * dofs), BF16),
            pltpu.VMEM(port_loads.shape, F32),
            pltpu.VMEM(port_loads.shape, F32),
            pltpu.SemaphoreType.DMA((3 + 2 * (owned * dofs // 512),)),
        ],
        compiler_params=pltpu.CompilerParams(vmem_limit_bytes=60 * 1024 * 1024),
        cost_estimate=pl.CostEstimate(flops=1 << 28, bytes_accessed=4 << 20, transcendentals=0),
        name="combine",
    )(small, port_loads, first, second)


def solution(mesh):
    sizes = (mesh.shape["gx"], mesh.shape["gy"])
    placed = (
        P(None, ("gx", "gy")),
        P(),
        P(),
        P(("gx", "gy"), None, None),
        P(),
        P(("gx", "gy")),
        P(("gx", "gy")),
        P(("gx", "gy"), None),
        P(("gx", "gy"), None),
        P(("gx", "gy"), None),
    )
    return jax.shard_map(
        functools.partial(local, sizes),
        mesh=mesh,
        in_specs=placed,
        out_specs=(P(None, ("gx", "gy")), P(None, ("gx", "gy"))),
        check_vma=False,
    )
```

```python
import functools
import itertools

import jax
import jax.numpy as jnp
from jax import lax
from jax.experimental import pallas as pl
from jax.experimental.pallas import tpu as pltpu
from jax.sharding import PartitionSpec as P

MESH = pl.DeviceIdType.MESH
APPLY = 8
FORM = 16
F32 = jnp.float32
BF16 = jnp.bfloat16


def parts(value):
    high = value.astype(BF16)
    return high, (value - high.astype(F32)).astype(BF16)


def mm(left, right):
    return jnp.dot(left, right, preferred_element_type=F32)


def mm_tn(left, right):
    return lax.dot_general(left, right, (((0,), (0,)), ((), ())), preferred_element_type=F32)


def exact(left, right):
    return lax.dot_general(
        left,
        right,
        (((1,), (0,)), ((), ())),
        precision=lax.Precision.HIGHEST,
        preferred_element_type=F32,
    )


def phases_of(mesh_sizes):
    sizes_x, sizes_y = mesh_sizes
    axes = []
    stride = 1
    for size in (2, 4, sizes_y):
        size = min(size, sizes_y // stride)
        if size > 1:
            axes.append(("gy", stride, size))
            stride *= size
    if sizes_x > 1:
        axes.append(("gx", 1, sizes_x))

    def phase(*members):
        steps = itertools.product(*[range(member[2]) for member in members])
        offsets = [list(zip(members, step)) for step in steps if any(step)]

        def hops(offset):
            return sum(min(steps, member[2] - steps) for member, steps in offset)

        return sorted(offsets, key=hops, reverse=True)

    return (
        [phase(axis) for axis in axes],
        [phase(*axes[:2]), phase(*axes[2:])],
        [phase(*axes[:2])] + [phase(axis) for axis in axes[2:]],
    )


def system_kernel(
    sizes,
    phases,
    arch,
    param,
    theta,
    refs_hbm,
    mask_hbm,
    cut_hbm,
    inverse_hbm,
    loads_hbm,
    stiff_hbm,
    coupling_hbm,
    first_hbm,
    second_hbm,
    small_out,
    refs_in,
    mask_in,
    cut_in,
    inverse,
    loads,
    stiff_top,
    stiff_low,
    coupling,
    couple_parts,
    blocks,
    field,
    running,
    load_parts,
    first_parts,
    second_parts,
    second_out,
    landed,
    send_a,
    recv_a,
    send_l,
    recv_l,
    send_p,
    recv_p,
    send_t,
    recv_t,
    index_rows,
    index,
    load_sem,
    send_sem,
    recv_sem,
    *reducers,
):
    sizes_x, sizes_y = sizes
    comps = coupling.shape[0]
    bubbles = coupling.shape[1]
    cols, dofs = loads.shape[0], field.shape[2] // 2
    owned = loads.shape[1] // dofs
    slot_count = refs_in.shape[0]
    refs = comps * slot_count
    width = slot_count * dofs
    cut = cut_in.shape[1]
    half = cut // 2
    ext = owned + cut
    quarter_comps = comps // 4
    PICK, PREV, LAST, CUT, BACK = range(5)

    my_x, my_y = lax.axis_index("gx"), lax.axis_index("gy")
    here = my_x * sizes_y + my_y
    total = sizes_x * sizes_y
    after = lax.rem(here + 1, total)
    before = lax.rem(here + total - 1, total)
    next_id = (after // sizes_y, lax.rem(after, sizes_y))
    prev_id = (before // sizes_y, lax.rem(before, sizes_y))

    def peer(offset):
        x, y = my_x, my_y
        for (axis, stride, size), steps in offset:
            if steps and axis == "gx":
                x = lax.rem(my_x + steps, size)
            elif steps:
                place = lax.rem(my_y // stride, size)
                y = y + (lax.rem(place + steps, size) - place) * stride
        return (x, y)

    small_copies = []
    for number, (source, target) in enumerate(
        ((refs_hbm, refs_in), (mask_hbm, mask_in), (cut_hbm, cut_in), (inverse_hbm, inverse))
    ):
        copy = pltpu.make_async_copy(source, target, load_sem.at[1 + number])
        copy.start()
        small_copies.append(copy)
    load_copy = pltpu.make_async_copy(loads_hbm, loads, load_sem.at[0])
    load_copy.start()
    coupling_copy = pltpu.make_async_copy(coupling_hbm, coupling, load_sem.at[5])
    coupling_copy.start()
    middle_at = width // 2
    bands = ((0, 0, stiff_top), (middle_at, middle_at, stiff_low))
    stiff_copies = []
    for band, (start, begin, target) in enumerate(bands):
        at = (slice(None), pl.ds(start, middle_at), pl.ds(begin, width - begin))
        copy = pltpu.make_async_copy(stiff_hbm.at[at], target, load_sem.at[6 + band])
        copy.start()
        stiff_copies.append(copy)

    barrier = pltpu.get_barrier_semaphore()
    targets = [next_id, prev_id]
    targets += [peer(offset) for phase in phases[2] for offset in phase]
    for target in targets:
        pl.semaphore_signal(barrier, inc=1, device_id=target, device_id_type=MESH)

    left_lanes = lax.broadcasted_iota(jnp.int32, (cols, 128), 1) < dofs
    left_both = lax.broadcasted_iota(jnp.int32, (2 * cols, 128), 1) < dofs

    def fold(value):
        return value + pltpu.roll(value, dofs, 1)

    def keep(place, full):
        field[place, :cols], field[place, cols:] = parts(full)

    def keep_pair(target, at, one, two):
        target[:cols, at], target[cols:, at] = parts(jnp.where(left_lanes, one, two))

    def lanes_of(b):
        return pl.ds(pl.multiple_of(b * 128, 128), 128)

    def send(number, source, target_ref, device):
        return pltpu.make_async_remote_copy(
            src_ref=source,
            dst_ref=target_ref,
            send_sem=send_sem.at[number],
            recv_sem=recv_sem.at[number],
            device_id=device,
            device_id_type=MESH,
        )

    def loop(count, unroll, body):
        def step(b, carry):
            for u in range(unroll):
                body(b * unroll + u)
            return carry

        lax.fori_loop(0, count // unroll, step, 0)

    def unpack(pair):
        other = pltpu.roll(pair, dofs, 1)
        return jnp.where(left_lanes, pair, other), jnp.where(left_lanes, other, pair)

    def expand(received):
        def body(g):
            landed[g], landed[g + half] = unpack(received[g])

        loop(half, 4, body)

    def widen(row):
        return jnp.concatenate(
            [row, jnp.zeros((row.shape[0], 128 - row.shape[1]), row.dtype)], axis=1
        )

    for copy in small_copies:
        copy.wait()
    picks = widen(jnp.where(mask_in[...] != 0, refs_in[...], ext)).T[:comps]
    comp_lane = lax.broadcasted_iota(jnp.int32, (comps, refs), 1)
    comp_row = lax.broadcasted_iota(jnp.int32, (comps, refs), 0)
    wide = jnp.zeros((comps, refs), jnp.int32)
    for j in range(slot_count):
        wide = jnp.where(comp_lane == comp_row * slot_count + j, picks[:, j : j + 1], wide)
    pick_row = jnp.sum(wide, axis=0, keepdims=True)
    pick_row = jnp.clip(pick_row, 0, ext)
    down = lax.broadcasted_iota(jnp.int32, (refs, 128), 0)
    across = lax.broadcasted_iota(jnp.int32, (refs, 128), 1)
    pick_down = jnp.broadcast_to(pick_row, (refs, refs)).T
    same = (pick_down == pick_row) & (pick_down < ext) & (down < across)
    previous = jnp.max(jnp.where(same, down, -1), axis=0, keepdims=True)
    final = jnp.max(jnp.where((pick_down == across) & (across < ext), down, -1), axis=0, keepdims=True)
    cut_rows = widen(cut_in[...])
    lane_row = lax.broadcasted_iota(jnp.int32, (1, 128), 1)
    cut_marked = jnp.where(lane_row < cut, cut_rows, -1)
    cut_down = jnp.broadcast_to(cut_marked, (refs, 128)).T
    back_row = jnp.max(jnp.where(cut_down == across, down, -1), axis=0, keepdims=True)
    index_rows[PICK : PICK + 1, :] = pick_row
    index_rows[PREV : PREV + 1, :] = jnp.where(previous < 0, refs, previous)
    index_rows[LAST : LAST + 1, :] = jnp.where(final < 0, refs, final)
    index_rows[CUT : CUT + 1, :] = jnp.clip(cut_rows, 0, owned - 1)
    index_rows[BACK : BACK + 1, :] = jnp.where(back_row < 0, cut, back_row)
    index_copy = pltpu.make_async_copy(index_rows, index, load_sem.at[10])
    index_copy.start()
    def pack(target, source):
        def body(g):
            target[g] = jnp.where(left_lanes, source(g), source(g + half))

        loop(half, 4, body)

    def ghost_total(g):
        return running[index[LAST, owned + g]]

    def apply(start, count):
        def pick(c):
            first = c * slot_count
            return jnp.concatenate(
                [
                    jnp.where(
                        left_both, field[index[PICK, first + j]], field[index[PICK, first + j + 1]]
                    )
                    for j in range(0, slot_count, 2)
                ],
                axis=1,
            )

        def times(c, left, side):
            at = side * width
            near = pl.ds(at, middle_at)
            far = pl.ds(at + middle_at, middle_at)
            return jnp.concatenate(
                [
                    mm(left[:, :middle_at], blocks[c, :middle_at, near])
                    + mm_nt(left[:, middle_at:], blocks[c, :middle_at, far]),
                    mm(left, blocks[c, :, far]),
                ],
                axis=1,
            )

        def multiply(c, picked):
            both = times(c, picked, 0)
            return both[:cols] + both[cols:] + times(c, picked[:cols], 1)

        def add(c, product):
            first = c * slot_count
            for j in range(0, slot_count, 2):
                one, two = unpack(product[:, j * dofs : (j + 2) * dofs])
                running[first + j] = running[index[PREV, first + j]] + one
                running[first + j + 1] = running[index[PREV, first + j + 1]] + two

        def body(b, carry):
            places = [start + b * APPLY + u for u in range(APPLY)]
            picked = [pick(c) for c in places]
            products = [multiply(c, value) for c, value in zip(places, picked)]
            for c, product in zip(places, products):
                add(c, product)
            return carry

        lax.fori_loop(0, count // APPLY, body, 0)

    def gram(left, right):
        both = mm_nt(left, right)
        rows = both[:cols] + both[cols:]
        full = fold(rows)
        return jnp.where(left_lanes[: cols // 2], full[: cols // 2], full[cols // 2 :])

    sent = []

    def reduction(number, kind, value):
        sums, slots, sum_send, sum_recv = reducers[4 * number : 4 * number + 4]
        count = 0
        for level, phase in enumerate(phases[kind]):
            sums[level] = value
            copies = []
            for offset in phase:
                copy = pltpu.make_async_remote_copy(
                    src_ref=sums.at[level],
                    dst_ref=slots.at[count],
                    send_sem=sum_send.at[count],
                    recv_sem=sum_recv.at[count],
                    device_id=peer(offset),
                    device_id_type=MESH,
                )
                copy.start()
                copies.append((copy, count))
                count += 1
            sent.extend(copy for copy, at in copies)
            yield None
            for copy, at in copies:
                copy.wait_recv()
            for copy, at in copies:
                value = value + slots[at]
        yield value

    def advance(steps):
        return next(steps)

    def square_of(packed):
        other = pltpu.roll(packed, cols, 1)
        return jnp.concatenate([packed, other], axis=0)[:, :cols]

    load_copy.wait()

    def spread(b):
        at = lanes_of(b)
        piece = loads[:, at]
        load_parts[:cols, at], load_parts[cols:, at] = parts(piece)
        running[2 * b], running[2 * b + 1] = one, two = unpack(piece)
        keep(2 * b, one)
        keep(2 * b + 1, two)

    loop(owned // 2, 4, spread)
    index_copy.wait()
    pack(send_a, lambda g: running[index[CUT, g]])
    running[refs] = jnp.zeros((cols, 128), F32)
    landed[cut] = jnp.zeros((cols, 128), F32)
    field[ext] = jnp.zeros((2 * cols, 128), BF16)
    pl.semaphore_wait(barrier, len(targets))
    ghosts = send(0, send_a, recv_a, next_id)
    ghosts.start()
    quarter = cols // 2
    own_gram = gram(load_parts[...], load_parts[...])

    coupling_copy.wait()

    def move(c):
        couple_high, couple_low = parts(coupling[c])
        inverse_high, inverse_low = parts(inverse[arch[c]])
        moved = (
            mm(inverse_high, couple_high)
            + mm(inverse_high, couple_low)
            + mm(inverse_low, couple_high)
        )
        moved_high, moved_low = parts(moved)
        couple_parts[c, :bubbles] = couple_high
        couple_parts[c, bubbles : 2 * bubbles] = couple_low
        couple_parts[c, 2 * bubbles : 3 * bubbles] = moved_high
        couple_parts[c, 3 * bubbles :] = moved_low

    loop(comps, 2, move)

    def form(band, c):
        kind = arch[c]
        weight0, weight1 = theta[0, param[c]], theta[1, param[c]]
        first_row, begin, stiff = bands[band]
        right_of = pl.ds(begin, width - begin)
        moved_high = couple_parts[c, 2 * bubbles : 3 * bubbles, right_of]
        moved_low = couple_parts[c, 3 * bubbles :, right_of]
        moved = jnp.concatenate([moved_high, moved_high, moved_low], axis=0)
        for start in range(first_row, first_row + middle_at, 128):
            rows = pl.ds(start, 128)
            couple_both = couple_parts[c, : 2 * bubbles, rows]
            bubble = mm_tn(jnp.concatenate([couple_both, couple_both[:bubbles]], axis=0), moved)
            block = (
                weight0 * (stiff[2 * kind, pl.ds(start - first_row, 128), :] - bubble)
                + weight1 * stiff[2 * kind + 1, pl.ds(start - first_row, 128), :]
            )
            high, low = parts(block)
            blocks[c, rows, right_of] = high
            blocks[c, rows, pl.ds(width + begin, width - begin)] = low

    load_steps = reduction(0, 0, own_gram)
    load_gram = advance(load_steps)
    for band in range(len(bands)):
        stiff_copies[band].wait()
        loop(comps, FORM, functools.partial(form, band))
    load_gram = advance(load_steps)

    ghosts.wait()

    def take_ghosts(g):
        one, two = unpack(recv_a[g])
        keep(owned + g, one)
        keep(owned + half + g, two)

    loop(half, 4, take_ghosts)

    apply(0, comps // 2)
    apply(comps // 2, comps // 2)

    pack(send_p, ghost_total)
    back = send(1, send_p, recv_p, prev_id)
    back.start()
    pack(send_l, lambda g: running[index[LAST, index[CUT, g]]])
    forth = send(2, send_l, recv_l, next_id)
    forth.start()
    load_gram = advance(load_steps)
    back.wait()
    expand(recv_p)

    def first_owned(b):
        one, two = [running[index[LAST, p]] + landed[index[BACK, p]] for p in (2 * b, 2 * b + 1)]
        keep(2 * b, one)
        keep(2 * b + 1, two)
        keep_pair(first_parts, lanes_of(b), one, two)

    loop(owned // 2, 4, first_owned)
    forth.wait()
    expand(recv_l)

    def first_ghost(b):
        one, two = [ghost_total(g) + landed[g] for g in (2 * b, 2 * b + 1)]
        keep(owned + 2 * b, one)
        keep(owned + 2 * b + 1, two)
        keep_pair(first_parts, lanes_of(owned // 2 + b), one, two)

    loop(half, 4, first_ghost)

    first_owned_parts = first_parts[:, : owned * dofs]
    first_copy = pltpu.make_async_copy(
        first_parts.at[:, pl.ds(0, owned * dofs)], first_hbm, load_sem.at[8]
    )
    first_copy.start()
    middle_steps = reduction(
        1,
        2,
        jnp.concatenate(
            [gram(load_parts[...], first_owned_parts), gram(first_owned_parts, first_owned_parts)],
            axis=0,
        ),
    )
    middle = advance(middle_steps)
    apply(0, comps // 2)
    if load_gram is None:
        load_gram = advance(load_steps)
    apply(comps // 2, comps // 2)

    def second_partial(b):
        one, two = [running[index[LAST, p]] for p in (2 * b, 2 * b + 1)]
        keep_pair(second_parts, lanes_of(b), one, two)

    loop(ext // 2, 4, second_partial)
    cube_steps = reduction(2, 1, gram(first_parts[...], second_parts[...]))
    cube = advance(cube_steps)
    pack(send_t, ghost_total)
    last_back = send(3, send_t, recv_t, prev_id)
    last_back.start()
    middle = advance(middle_steps)
    while load_gram is None:
        load_gram = advance(load_steps)
    cube = advance(cube_steps)
    if middle is None:
        middle = advance(middle_steps)

    last_back.wait()
    expand(recv_t)

    def second_owned(b):
        one, two = [running[index[LAST, p]] + landed[index[BACK, p]] for p in (2 * b, 2 * b + 1)]
        keep_pair(second_out, lanes_of(b), one, two)

    loop(owned // 2, 4, second_owned)
    second_copy = pltpu.make_async_copy(second_out, second_hbm, load_sem.at[9])
    second_copy.start()
    while middle is None:
        middle = advance(middle_steps)
    load_gram, cross, square = [
        square_of(packed) for packed in (load_gram, middle[:quarter], middle[quarter:])
    ]
    solved = elimination(
        [jnp.concatenate([cross, square], axis=1), jnp.concatenate([load_gram, load_gram], axis=1)]
    )
    moved = solved[0][:, cols:]
    step = solved[1][:, :cols]
    small_out[0, :, cols:] = cross - exact(square, step)
    small_out[1, :, :cols] = moved
    small_out[1, :, cols:] = step
    while cube is None:
        cube = advance(cube_steps)
    small_out[0, :, :cols] = square_of(cube) - exact(square, moved)
    for copy in sent:
        copy.wait_send()
    first_copy.wait()
    second_copy.wait()


def elimination(tiles, block=8, midway=None):
    size = tiles[0].shape[0]
    row_index = lax.broadcasted_iota(jnp.int32, (size, 1), 0)
    for k in range(0, size, block):
        if midway is not None and k == size // 2:
            midway()
        wide = [jnp.broadcast_to(tiles[0][:, k + j : k + j + 1], tiles[0].shape) for j in range(block)]
        pivots = [[wide[j][k + i : k + i + 1] for j in range(block)] for i in range(block)]
        rows = [[tile[k + i : k + i + 1] for tile in tiles] for i in range(block)]
        for i in range(block):
            scale = 1.0 / pivots[i][i]
            rows[i] = [row * scale for row in rows[i]]
            for j in range(i + 1, block):
                pivots[i][j] = pivots[i][j] * scale
            for m in range(i + 1, block):
                factor = pivots[m][i]
                rows[m] = [row - factor * other for row, other in zip(rows[m], rows[i])]
                for j in range(i + 1, block):
                    pivots[m][j] = pivots[m][j] - factor * pivots[i][j]
        for i in range(block - 1, 0, -1):
            for m in range(i):
                rows[m] = [row - pivots[m][i] * other for row, other in zip(rows[m], rows[i])]
        out = []
        for number, tile in enumerate(tiles):
            new = tile
            for j in range(block):
                new = new - wide[j] * rows[j][number]
            for j in range(block):
                new = jnp.where(row_index == k + j, rows[j][number], new)
            out.append(new)
        tiles = out
    return tiles


def combine_kernel(small, loads_hbm, first_hbm, second_hbm, solution_hbm, residual_hbm, loads, load_parts, first, second, solution, residual, sems):
    cols = loads.shape[0]
    copies = []
    for number, (source, target) in enumerate(
        ((loads_hbm, loads), (first_hbm, first), (second_hbm, second))
    ):
        copy = pltpu.make_async_copy(source, target, sems.at[number])
        copy.start()
        copies.append(copy)

    def split_loads():
        copies[0].wait()
        load_parts[:cols, :], load_parts[cols:, :] = parts(loads[...])

    (solved,) = elimination([small[0]], midway=split_loads)
    second_weight = solved[:, cols:]
    first_weight = small[1, :, cols:] - exact(small[1, :, :cols], second_weight)

    top_high, top_low = parts(first_weight.T)
    low_high, low_low = parts(second_weight.T)
    left = jnp.concatenate([top_high, top_high, top_low, low_high, low_high, low_low], axis=1)
    for copy in copies[1:]:
        copy.wait()

    chunk = 512
    writes = []
    for b in range(loads.shape[1] // chunk):
        at = pl.ds(b * chunk, chunk)
        load_piece, first_piece, second_piece = loads[:, at], first[:, at], second[:, at]
        both_piece = load_parts[:, at]
        solution[:, at] = mm(
            left,
            jnp.concatenate(
                [both_piece, both_piece[:cols], first_piece, first_piece[:cols]], axis=0
            ),
        )
        residual[:, at] = load_piece - mm(
            left,
            jnp.concatenate(
                [first_piece, first_piece[:cols], second_piece, second_piece[:cols]], axis=0
            ),
        )
        for number, (source, target) in enumerate(
            ((solution, solution_hbm), (residual, residual_hbm))
        ):
            copy = pltpu.make_async_copy(
                source.at[:, at], target.at[:, at], sems.at[3 + 2 * b + number]
            )
            copy.start()
            writes.append(copy)
    for copy in writes:
        copy.wait()


def mm_nt(left, right):
    return lax.dot_general(left, right, (((1,), (1,)), ((), ())), preferred_element_type=F32)


def local(
    sizes,
    port_loads,
    port_stiff,
    bubble_inverse,
    coupling,
    theta_table,
    comp_arch,
    comp_param,
    port_refs,
    slot_mask,
    cut_source,
):
    cols = port_loads.shape[0]
    comps, slot_count = port_refs.shape
    width = port_stiff.shape[2]
    dofs = width // slot_count
    cut = cut_source.shape[1]
    owned = port_loads.shape[1] // dofs
    refs = comps * slot_count
    ext = owned + cut
    archs, terms = port_stiff.shape[:2]
    bubbles = coupling.shape[1]

    phases = phases_of(sizes)
    smem = pl.BlockSpec(memory_space=pltpu.SMEM)
    vmem = pl.BlockSpec(memory_space=pltpu.VMEM)
    hbm = pl.BlockSpec(memory_space=pl.ANY)
    reducers = []
    for kind, rows in ((0, cols // 2), (2, cols), (1, cols // 2)):
        messages = sum(len(phase) for phase in phases[kind])
        reducers += [
            pltpu.VMEM((len(phases[kind]), rows, 128), F32),
            pltpu.VMEM((messages, rows, 128), F32),
            pltpu.SemaphoreType.DMA((messages,)),
            pltpu.SemaphoreType.DMA((messages,)),
        ]
    exchange = pltpu.VMEM((cut // 2, cols, 128), F32)
    flops = 2 * comps * cols * width * width * 9
    first, second, small = pl.pallas_call(
        functools.partial(system_kernel, sizes, phases),
        out_shape=(
            jax.ShapeDtypeStruct((2 * cols, owned * dofs), BF16),
            jax.ShapeDtypeStruct((2 * cols, owned * dofs), BF16),
            jax.ShapeDtypeStruct((2, cols, 2 * cols), F32),
        ),
        in_specs=[smem, smem, smem] + [hbm] * 7,
        out_specs=(hbm, hbm, vmem),
        scratch_shapes=[
            pltpu.VMEM((slot_count, comps), jnp.int32),
            pltpu.VMEM((slot_count, comps), jnp.int32),
            pltpu.VMEM(cut_source.shape, jnp.int32),
            pltpu.VMEM(bubble_inverse.shape, F32),
            pltpu.VMEM(port_loads.shape, F32),
            pltpu.VMEM((archs * terms, width // 2, width), F32),
            pltpu.VMEM((archs * terms, width // 2, width // 2), F32),
            pltpu.VMEM(coupling.shape, F32),
            pltpu.VMEM((comps, 4 * bubbles, width), BF16),
            pltpu.VMEM((comps, width, 2 * width), BF16),
            pltpu.VMEM((ext + 1, 2 * cols, 128), BF16),
            pltpu.VMEM((refs + 1, cols, 128), F32),
            pltpu.VMEM((2 * cols, owned * dofs), BF16),
            pltpu.VMEM((2 * cols, ext * dofs), BF16),
            pltpu.VMEM((2 * cols, ext * dofs), BF16),
            pltpu.VMEM((2 * cols, owned * dofs), BF16),
            pltpu.VMEM((cut + 1, cols, 128), F32),
        ]
        + [exchange] * 8
        + [
            pltpu.VMEM((8, 128), jnp.int32),
            pltpu.SMEM((8, 128), jnp.int32),
            pltpu.SemaphoreType.DMA((11,)),
            pltpu.SemaphoreType.DMA((4,)),
            pltpu.SemaphoreType.DMA((4,)),
        ]
        + reducers,
        compiler_params=pltpu.CompilerParams(
            collective_id=0, has_side_effects=True, vmem_limit_bytes=60 * 1024 * 1024
        ),
        cost_estimate=pl.CostEstimate(flops=flops, bytes_accessed=12 << 20, transcendentals=0),
        name="system",
    )(
        comp_arch,
        comp_param,
        theta_table.T,
        port_refs.T,
        slot_mask.T,
        cut_source,
        bubble_inverse,
        port_loads,
        port_stiff.reshape(archs * terms, width, width),
        coupling,
    )
    return pl.pallas_call(
        combine_kernel,
        out_shape=(
            jax.ShapeDtypeStruct(port_loads.shape, F32),
            jax.ShapeDtypeStruct(port_loads.shape, F32),
        ),
        in_specs=[vmem, hbm, hbm, hbm],
        out_specs=(hbm, hbm),
        scratch_shapes=[
            pltpu.VMEM(port_loads.shape, F32),
            pltpu.VMEM((2 * cols, owned * dofs), BF16),
            pltpu.VMEM((2 * cols, owned * dofs), BF16),
            pltpu.VMEM((2 * cols, owned * dofs), BF16),
            pltpu.VMEM(port_loads.shape, F32),
            pltpu.VMEM(port_loads.shape, F32),
            pltpu.SemaphoreType.DMA((3 + 2 * (owned * dofs // 512),)),
        ],
        compiler_params=pltpu.CompilerParams(vmem_limit_bytes=60 * 1024 * 1024),
        cost_estimate=pl.CostEstimate(flops=1 << 28, bytes_accessed=4 << 20, transcendentals=0),
        name="combine",
    )(small, port_loads, first, second)


def solution(mesh):
    sizes = (mesh.shape["gx"], mesh.shape["gy"])
    placed = (
        P(None, ("gx", "gy")),
        P(),
        P(),
        P(("gx", "gy"), None, None),
        P(),
        P(("gx", "gy")),
        P(("gx", "gy")),
        P(("gx", "gy"), None),
        P(("gx", "gy"), None),
        P(("gx", "gy"), None),
    )
    return jax.shard_map(
        functools.partial(local, sizes),
        mesh=mesh,
        in_specs=placed,
        out_specs=(P(None, ("gx", "gy")), P(None, ("gx", "gy"))),
        check_vma=False,
    )
```

```python
import functools
import itertools

import jax
import jax.numpy as jnp
from jax import lax
from jax.experimental import pallas as pl
from jax.experimental.pallas import tpu as pltpu
from jax.sharding import PartitionSpec as P

MESH = pl.DeviceIdType.MESH
APPLY = 8
FORM = 16
F32 = jnp.float32
BF16 = jnp.bfloat16


def parts(value):
    high = value.astype(BF16)
    return high, (value - high.astype(F32)).astype(BF16)


def mm(left, right):
    return jnp.dot(left, right, preferred_element_type=F32)


def mm_tn(left, right):
    return lax.dot_general(left, right, (((0,), (0,)), ((), ())), preferred_element_type=F32)


def exact(left, right):
    return lax.dot_general(
        left,
        right,
        (((1,), (0,)), ((), ())),
        precision=lax.Precision.HIGHEST,
        preferred_element_type=F32,
    )


def phases_of(mesh_sizes):
    sizes_x, sizes_y = mesh_sizes
    axes = []
    stride = 1
    for size in (2, 4, sizes_y):
        size = min(size, sizes_y // stride)
        if size > 1:
            axes.append(("gy", stride, size))
            stride *= size
    if sizes_x > 1:
        axes.append(("gx", 1, sizes_x))

    def phase(*members):
        steps = itertools.product(*[range(member[2]) for member in members])
        offsets = [list(zip(members, step)) for step in steps if any(step)]

        def hops(offset):
            return sum(min(steps, member[2] - steps) for member, steps in offset)

        return sorted(offsets, key=hops, reverse=True)

    return (
        [phase(axis) for axis in axes],
        [phase(*axes[:2]), phase(*axes[2:])],
        [phase(*axes[:2])] + [phase(axis) for axis in axes[2:]],
    )


def system_kernel(
    sizes,
    phases,
    arch,
    param,
    theta,
    refs_hbm,
    mask_hbm,
    cut_hbm,
    inverse_hbm,
    loads_hbm,
    stiff_hbm,
    coupling_hbm,
    first_hbm,
    second_hbm,
    small_out,
    refs_in,
    mask_in,
    cut_in,
    inverse,
    loads,
    stiff_top,
    stiff_low,
    coupling,
    couple_parts,
    blocks,
    field,
    running,
    load_parts,
    first_parts,
    second_parts,
    second_out,
    landed,
    send_a,
    recv_a,
    send_l,
    recv_l,
    send_p,
    recv_p,
    send_t,
    recv_t,
    index_rows,
    index,
    load_sem,
    send_sem,
    recv_sem,
    *reducers,
):
    sizes_x, sizes_y = sizes
    comps = coupling.shape[0]
    bubbles = coupling.shape[1]
    cols, dofs = loads.shape[0], field.shape[2] // 2
    owned = loads.shape[1] // dofs
    slot_count = refs_in.shape[0]
    refs = comps * slot_count
    width = slot_count * dofs
    cut = cut_in.shape[1]
    half = cut // 2
    ext = owned + cut
    quarter_comps = comps // 4
    PICK, PREV, LAST, CUT, BACK = range(5)

    my_x, my_y = lax.axis_index("gx"), lax.axis_index("gy")
    here = my_x * sizes_y + my_y
    total = sizes_x * sizes_y
    after = lax.rem(here + 1, total)
    before = lax.rem(here + total - 1, total)
    next_id = (after // sizes_y, lax.rem(after, sizes_y))
    prev_id = (before // sizes_y, lax.rem(before, sizes_y))

    def peer(offset):
        x, y = my_x, my_y
        for (axis, stride, size), steps in offset:
            if steps and axis == "gx":
                x = lax.rem(my_x + steps, size)
            elif steps:
                place = lax.rem(my_y // stride, size)
                y = y + (lax.rem(place + steps, size) - place) * stride
        return (x, y)

    small_copies = []
    for number, (source, target) in enumerate(
        ((refs_hbm, refs_in), (mask_hbm, mask_in), (cut_hbm, cut_in), (inverse_hbm, inverse))
    ):
        copy = pltpu.make_async_copy(source, target, load_sem.at[1 + number])
        copy.start()
        small_copies.append(copy)
    load_copy = pltpu.make_async_copy(loads_hbm, loads, load_sem.at[0])
    load_copy.start()
    coupling_copy = pltpu.make_async_copy(coupling_hbm, coupling, load_sem.at[5])
    coupling_copy.start()
    middle_at = width // 2
    bands = ((0, 0, stiff_top), (middle_at, middle_at, stiff_low))
    stiff_copies = []
    for band, (start, begin, target) in enumerate(bands):
        at = (slice(None), pl.ds(start, middle_at), pl.ds(begin, width - begin))
        copy = pltpu.make_async_copy(stiff_hbm.at[at], target, load_sem.at[6 + band])
        copy.start()
        stiff_copies.append(copy)

    barrier = pltpu.get_barrier_semaphore()
    targets = [next_id, prev_id]
    targets += [peer(offset) for phase in phases[2] for offset in phase]
    for target in targets:
        pl.semaphore_signal(barrier, inc=1, device_id=target, device_id_type=MESH)

    left_lanes = lax.broadcasted_iota(jnp.int32, (cols, 128), 1) < dofs
    left_both = lax.broadcasted_iota(jnp.int32, (2 * cols, 128), 1) < dofs

    def fold(value):
        return value + pltpu.roll(value, dofs, 1)

    def keep(place, full):
        field[place, :cols], field[place, cols:] = parts(full)

    def keep_pair(target, at, one, two):
        target[:cols, at], target[cols:, at] = parts(jnp.where(left_lanes, one, two))

    def lanes_of(b):
        return pl.ds(pl.multiple_of(b * 128, 128), 128)

    def send(number, source, target_ref, device):
        return pltpu.make_async_remote_copy(
            src_ref=source,
            dst_ref=target_ref,
            send_sem=send_sem.at[number],
            recv_sem=recv_sem.at[number],
            device_id=device,
            device_id_type=MESH,
        )

    def loop(count, unroll, body):
        def step(b, carry):
            for u in range(unroll):
                body(b * unroll + u)
            return carry

        lax.fori_loop(0, count // unroll, step, 0)

    def unpack(pair):
        other = pltpu.roll(pair, dofs, 1)
        return jnp.where(left_lanes, pair, other), jnp.where(left_lanes, other, pair)

    def expand(received):
        def body(g):
            landed[g], landed[g + half] = unpack(received[g])

        loop(half, 4, body)

    def widen(row):
        return jnp.concatenate(
            [row, jnp.zeros((row.shape[0], 128 - row.shape[1]), row.dtype)], axis=1
        )

    for copy in small_copies:
        copy.wait()
    picks = widen(jnp.where(mask_in[...] != 0, refs_in[...], ext)).T[:comps]
    comp_lane = lax.broadcasted_iota(jnp.int32, (comps, refs), 1)
    comp_row = lax.broadcasted_iota(jnp.int32, (comps, refs), 0)
    wide = jnp.zeros((comps, refs), jnp.int32)
    for j in range(slot_count):
        wide = jnp.where(comp_lane == comp_row * slot_count + j, picks[:, j : j + 1], wide)
    pick_row = jnp.sum(wide, axis=0, keepdims=True)
    pick_row = jnp.clip(pick_row, 0, ext)
    down = lax.broadcasted_iota(jnp.int32, (refs, 128), 0)
    across = lax.broadcasted_iota(jnp.int32, (refs, 128), 1)
    pick_down = jnp.broadcast_to(pick_row, (refs, refs)).T
    same = (pick_down == pick_row) & (pick_down < ext) & (down < across)
    previous = jnp.max(jnp.where(same, down, -1), axis=0, keepdims=True)
    final = jnp.max(jnp.where((pick_down == across) & (across < ext), down, -1), axis=0, keepdims=True)
    cut_rows = widen(cut_in[...])
    lane_row = lax.broadcasted_iota(jnp.int32, (1, 128), 1)
    cut_marked = jnp.where(lane_row < cut, cut_rows, -1)
    cut_down = jnp.broadcast_to(cut_marked, (refs, 128)).T
    back_row = jnp.max(jnp.where(cut_down == across, down, -1), axis=0, keepdims=True)
    index_rows[PICK : PICK + 1, :] = pick_row
    index_rows[PREV : PREV + 1, :] = jnp.where(previous < 0, refs, previous)
    index_rows[LAST : LAST + 1, :] = jnp.where(final < 0, refs, final)
    index_rows[CUT : CUT + 1, :] = jnp.clip(cut_rows, 0, owned - 1)
    index_rows[BACK : BACK + 1, :] = jnp.where(back_row < 0, cut, back_row)
    index_copy = pltpu.make_async_copy(index_rows, index, load_sem.at[10])
    index_copy.start()
    def pack(target, source):
        def body(g):
            target[g] = jnp.where(left_lanes, source(g), source(g + half))

        loop(half, 4, body)

    def ghost_total(g):
        return running[index[LAST, owned + g]]

    def apply(start, count):
        def pick(c):
            first = c * slot_count
            return jnp.concatenate(
                [
                    jnp.where(
                        left_both, field[index[PICK, first + j]], field[index[PICK, first + j + 1]]
                    )
                    for j in range(0, slot_count, 2)
                ],
                axis=1,
            )

        def times(c, left, side):
            at = side * width
            near = pl.ds(at, middle_at)
            far = pl.ds(at + middle_at, middle_at)
            return jnp.concatenate(
                [
                    mm(left[:, :middle_at], blocks[c, :middle_at, near])
                    + mm_nt(left[:, middle_at:], blocks[c, :middle_at, far]),
                    mm(left, blocks[c, :, far]),
                ],
                axis=1,
            )

        def multiply(c, picked):
            both = times(c, picked, 0)
            return both[:cols] + both[cols:] + times(c, picked[:cols], 1)

        def add(c, product):
            first = c * slot_count
            for j in range(0, slot_count, 2):
                one, two = unpack(product[:, j * dofs : (j + 2) * dofs])
                running[first + j] = running[index[PREV, first + j]] + one
                running[first + j + 1] = running[index[PREV, first + j + 1]] + two

        def body(b, carry):
            places = [start + b * APPLY + u for u in range(APPLY)]
            picked = [pick(c) for c in places]
            products = [multiply(c, value) for c, value in zip(places, picked)]
            for c, product in zip(places, products):
                add(c, product)
            return carry

        lax.fori_loop(0, count // APPLY, body, 0)

    def gram(left, right):
        both = mm_nt(left, right)
        rows = both[:cols] + both[cols:]
        full = fold(rows)
        return jnp.where(left_lanes[: cols // 2], full[: cols // 2], full[cols // 2 :])

    sent = []

    def reduction(number, kind, value):
        sums, slots, sum_send, sum_recv = reducers[4 * number : 4 * number + 4]
        count = 0
        for level, phase in enumerate(phases[kind]):
            sums[level] = value
            copies = []
            for offset in phase:
                copy = pltpu.make_async_remote_copy(
                    src_ref=sums.at[level],
                    dst_ref=slots.at[count],
                    send_sem=sum_send.at[count],
                    recv_sem=sum_recv.at[count],
                    device_id=peer(offset),
                    device_id_type=MESH,
                )
                copy.start()
                copies.append((copy, count))
                count += 1
            sent.extend(copy for copy, at in copies)
            yield None
            for copy, at in copies:
                copy.wait_recv()
            for copy, at in copies:
                value = value + slots[at]
        yield value

    def advance(steps):
        return next(steps)

    def square_of(packed):
        other = pltpu.roll(packed, cols, 1)
        return jnp.concatenate([packed, other], axis=0)[:, :cols]

    load_copy.wait()

    def spread(b):
        at = lanes_of(b)
        piece = loads[:, at]
        load_parts[:cols, at], load_parts[cols:, at] = parts(piece)
        running[2 * b], running[2 * b + 1] = one, two = unpack(piece)
        keep(2 * b, one)
        keep(2 * b + 1, two)

    loop(owned // 2, 4, spread)
    index_copy.wait()
    pack(send_a, lambda g: running[index[CUT, g]])
    running[refs] = jnp.zeros((cols, 128), F32)
    landed[cut] = jnp.zeros((cols, 128), F32)
    field[ext] = jnp.zeros((2 * cols, 128), BF16)
    pl.semaphore_wait(barrier, len(targets))
    ghosts = send(0, send_a, recv_a, next_id)
    ghosts.start()
    quarter = cols // 2
    own_gram = gram(load_parts[...], load_parts[...])

    coupling_copy.wait()

    def move(c):
        couple_high, couple_low = parts(coupling[c])
        inverse_high, inverse_low = parts(inverse[arch[c]])
        moved = (
            mm(inverse_high, couple_high)
            + mm(inverse_high, couple_low)
            + mm(inverse_low, couple_high)
        )
        moved_high, moved_low = parts(moved)
        couple_parts[c, :bubbles] = couple_high
        couple_parts[c, bubbles : 2 * bubbles] = couple_low
        couple_parts[c, 2 * bubbles : 3 * bubbles] = moved_high
        couple_parts[c, 3 * bubbles :] = moved_low

    loop(comps, 2, move)

    def form(band, c):
        kind = arch[c]
        weight0, weight1 = theta[0, param[c]], theta[1, param[c]]
        first_row, begin, stiff = bands[band]
        right_of = pl.ds(begin, width - begin)
        moved_high = couple_parts[c, 2 * bubbles : 3 * bubbles, right_of]
        moved_low = couple_parts[c, 3 * bubbles :, right_of]
        moved = jnp.concatenate([moved_high, moved_high, moved_low], axis=0)
        for start in range(first_row, first_row + middle_at, 128):
            rows = pl.ds(start, 128)
            couple_both = couple_parts[c, : 2 * bubbles, rows]
            bubble = mm_tn(jnp.concatenate([couple_both, couple_both[:bubbles]], axis=0), moved)
            block = (
                weight0 * (stiff[2 * kind, pl.ds(start - first_row, 128), :] - bubble)
                + weight1 * stiff[2 * kind + 1, pl.ds(start - first_row, 128), :]
            )
            high, low = parts(block)
            blocks[c, rows, right_of] = high
            blocks[c, rows, pl.ds(width + begin, width - begin)] = low

    load_steps = reduction(0, 0, own_gram)
    load_gram = advance(load_steps)
    for band in range(len(bands)):
        stiff_copies[band].wait()
        loop(comps, FORM, functools.partial(form, band))
    load_gram = advance(load_steps)

    ghosts.wait()

    def take_ghosts(g):
        one, two = unpack(recv_a[g])
        keep(owned + g, one)
        keep(owned + half + g, two)

    loop(half, 4, take_ghosts)

    apply(0, comps // 2)
    apply(comps // 2, comps // 2)

    pack(send_p, ghost_total)
    back = send(1, send_p, recv_p, prev_id)
    back.start()
    pack(send_l, lambda g: running[index[LAST, index[CUT, g]]])
    forth = send(2, send_l, recv_l, next_id)
    forth.start()
    load_gram = advance(load_steps)
    back.wait()
    expand(recv_p)

    def first_owned(b):
        one, two = [running[index[LAST, p]] + landed[index[BACK, p]] for p in (2 * b, 2 * b + 1)]
        keep(2 * b, one)
        keep(2 * b + 1, two)
        keep_pair(first_parts, lanes_of(b), one, two)

    loop(owned // 2, 4, first_owned)
    forth.wait()
    expand(recv_l)

    def first_ghost(b):
        one, two = [ghost_total(g) + landed[g] for g in (2 * b, 2 * b + 1)]
        keep(owned + 2 * b, one)
        keep(owned + 2 * b + 1, two)
        keep_pair(first_parts, lanes_of(owned // 2 + b), one, two)

    loop(half, 4, first_ghost)

    first_owned_parts = first_parts[:, : owned * dofs]
    first_copy = pltpu.make_async_copy(
        first_parts.at[:, pl.ds(0, owned * dofs)], first_hbm, load_sem.at[8]
    )
    first_copy.start()
    middle_steps = reduction(
        1,
        2,
        jnp.concatenate(
            [gram(load_parts[...], first_owned_parts), gram(first_owned_parts, first_owned_parts)],
            axis=0,
        ),
    )
    middle = advance(middle_steps)
    apply(0, comps // 2)
    if load_gram is None:
        load_gram = advance(load_steps)
    apply(comps // 2, comps // 2)

    def second_partial(b):
        one, two = [running[index[LAST, p]] for p in (2 * b, 2 * b + 1)]
        keep_pair(second_parts, lanes_of(b), one, two)

    loop(ext // 2, 4, second_partial)
    cube_steps = reduction(2, 1, gram(first_parts[...], second_parts[...]))
    cube = advance(cube_steps)
    pack(send_t, ghost_total)
    last_back = send(3, send_t, recv_t, prev_id)
    last_back.start()
    middle = advance(middle_steps)
    while load_gram is None:
        load_gram = advance(load_steps)
    cube = advance(cube_steps)
    if middle is None:
        middle = advance(middle_steps)

    last_back.wait()
    expand(recv_t)

    def second_owned(b):
        one, two = [running[index[LAST, p]] + landed[index[BACK, p]] for p in (2 * b, 2 * b + 1)]
        keep_pair(second_out, lanes_of(b), one, two)

    loop(owned // 2, 4, second_owned)
    second_copy = pltpu.make_async_copy(second_out, second_hbm, load_sem.at[9])
    second_copy.start()
    while middle is None:
        middle = advance(middle_steps)
    load_gram, cross, square = [
        square_of(packed) for packed in (load_gram, middle[:quarter], middle[quarter:])
    ]
    solved = elimination(
        [jnp.concatenate([cross, square], axis=1), jnp.concatenate([load_gram, load_gram], axis=1)]
    )
    moved = solved[0][:, cols:]
    step = solved[1][:, :cols]
    small_out[0, :, cols:] = cross - exact(square, step)
    small_out[1, :, :cols] = moved
    small_out[1, :, cols:] = step
    small_out[0, :, :cols] = exact(square, moved)
    while cube is None:
        cube = advance(cube_steps)
    small_out[0, :, :cols] = square_of(cube) - small_out[0, :, :cols]
    for copy in sent:
        copy.wait_send()
    first_copy.wait()
    second_copy.wait()


def elimination(tiles, block=8, midway=None):
    size = tiles[0].shape[0]
    row_index = lax.broadcasted_iota(jnp.int32, (size, 1), 0)
    for k in range(0, size, block):
        if midway is not None and k == size // 2:
            midway()
        wide = [jnp.broadcast_to(tiles[0][:, k + j : k + j + 1], tiles[0].shape) for j in range(block)]
        pivots = [[wide[j][k + i : k + i + 1] for j in range(block)] for i in range(block)]
        rows = [[tile[k + i : k + i + 1] for tile in tiles] for i in range(block)]
        for i in range(block):
            scale = 1.0 / pivots[i][i]
            rows[i] = [row * scale for row in rows[i]]
            for j in range(i + 1, block):
                pivots[i][j] = pivots[i][j] * scale
            for m in range(i + 1, block):
                factor = pivots[m][i]
                rows[m] = [row - factor * other for row, other in zip(rows[m], rows[i])]
                for j in range(i + 1, block):
                    pivots[m][j] = pivots[m][j] - factor * pivots[i][j]
        for i in range(block - 1, 0, -1):
            for m in range(i):
                rows[m] = [row - pivots[m][i] * other for row, other in zip(rows[m], rows[i])]
        out = []
        for number, tile in enumerate(tiles):
            new = tile
            for j in range(block):
                new = new - wide[j] * rows[j][number]
            for j in range(block):
                new = jnp.where(row_index == k + j, rows[j][number], new)
            out.append(new)
        tiles = out
    return tiles


def combine_kernel(small, loads_hbm, first_hbm, second_hbm, solution_hbm, residual_hbm, loads, load_parts, first, second, solution, residual, sems):
    cols = loads.shape[0]
    copies = []
    for number, (source, target) in enumerate(
        ((loads_hbm, loads), (first_hbm, first), (second_hbm, second))
    ):
        copy = pltpu.make_async_copy(source, target, sems.at[number])
        copy.start()
        copies.append(copy)

    def split_loads():
        copies[0].wait()
        load_parts[:cols, :], load_parts[cols:, :] = parts(loads[...])

    (solved,) = elimination([small[0]], midway=split_loads)
    second_weight = solved[:, cols:]
    first_weight = small[1, :, cols:] - exact(small[1, :, :cols], second_weight)

    top_high, top_low = parts(first_weight.T)
    low_high, low_low = parts(second_weight.T)
    left = jnp.concatenate([top_high, top_high, top_low, low_high, low_high, low_low], axis=1)
    for copy in copies[1:]:
        copy.wait()

    chunk = 512
    writes = []
    for b in range(loads.shape[1] // chunk):
        at = pl.ds(b * chunk, chunk)
        load_piece, first_piece, second_piece = loads[:, at], first[:, at], second[:, at]
        both_piece = load_parts[:, at]
        solution[:, at] = mm(
            left,
            jnp.concatenate(
                [both_piece, both_piece[:cols], first_piece, first_piece[:cols]], axis=0
            ),
        )
        residual[:, at] = load_piece - mm(
            left,
            jnp.concatenate(
                [first_piece, first_piece[:cols], second_piece, second_piece[:cols]], axis=0
            ),
        )
        for number, (source, target) in enumerate(
            ((solution, solution_hbm), (residual, residual_hbm))
        ):
            copy = pltpu.make_async_copy(
                source.at[:, at], target.at[:, at], sems.at[3 + 2 * b + number]
            )
            copy.start()
            writes.append(copy)
    for copy in writes:
        copy.wait()


def mm_nt(left, right):
    return lax.dot_general(left, right, (((1,), (1,)), ((), ())), preferred_element_type=F32)


def local(
    sizes,
    port_loads,
    port_stiff,
    bubble_inverse,
    coupling,
    theta_table,
    comp_arch,
    comp_param,
    port_refs,
    slot_mask,
    cut_source,
):
    cols = port_loads.shape[0]
    comps, slot_count = port_refs.shape
    width = port_stiff.shape[2]
    dofs = width // slot_count
    cut = cut_source.shape[1]
    owned = port_loads.shape[1] // dofs
    refs = comps * slot_count
    ext = owned + cut
    archs, terms = port_stiff.shape[:2]
    bubbles = coupling.shape[1]

    phases = phases_of(sizes)
    smem = pl.BlockSpec(memory_space=pltpu.SMEM)
    vmem = pl.BlockSpec(memory_space=pltpu.VMEM)
    hbm = pl.BlockSpec(memory_space=pl.ANY)
    reducers = []
    for kind, rows in ((0, cols // 2), (2, cols), (1, cols // 2)):
        messages = sum(len(phase) for phase in phases[kind])
        reducers += [
            pltpu.VMEM((len(phases[kind]), rows, 128), F32),
            pltpu.VMEM((messages, rows, 128), F32),
            pltpu.SemaphoreType.DMA((messages,)),
            pltpu.SemaphoreType.DMA((messages,)),
        ]
    exchange = pltpu.VMEM((cut // 2, cols, 128), F32)
    flops = 2 * comps * cols * width * width * 9
    first, second, small = pl.pallas_call(
        functools.partial(system_kernel, sizes, phases),
        out_shape=(
            jax.ShapeDtypeStruct((2 * cols, owned * dofs), BF16),
            jax.ShapeDtypeStruct((2 * cols, owned * dofs), BF16),
            jax.ShapeDtypeStruct((2, cols, 2 * cols), F32),
        ),
        in_specs=[smem, smem, smem] + [hbm] * 7,
        out_specs=(hbm, hbm, vmem),
        scratch_shapes=[
            pltpu.VMEM((slot_count, comps), jnp.int32),
            pltpu.VMEM((slot_count, comps), jnp.int32),
            pltpu.VMEM(cut_source.shape, jnp.int32),
            pltpu.VMEM(bubble_inverse.shape, F32),
            pltpu.VMEM(port_loads.shape, F32),
            pltpu.VMEM((archs * terms, width // 2, width), F32),
            pltpu.VMEM((archs * terms, width // 2, width // 2), F32),
            pltpu.VMEM(coupling.shape, F32),
            pltpu.VMEM((comps, 4 * bubbles, width), BF16),
            pltpu.VMEM((comps, width, 2 * width), BF16),
            pltpu.VMEM((ext + 1, 2 * cols, 128), BF16),
            pltpu.VMEM((refs + 1, cols, 128), F32),
            pltpu.VMEM((2 * cols, owned * dofs), BF16),
            pltpu.VMEM((2 * cols, ext * dofs), BF16),
            pltpu.VMEM((2 * cols, ext * dofs), BF16),
            pltpu.VMEM((2 * cols, owned * dofs), BF16),
            pltpu.VMEM((cut + 1, cols, 128), F32),
        ]
        + [exchange] * 8
        + [
            pltpu.VMEM((8, 128), jnp.int32),
            pltpu.SMEM((8, 128), jnp.int32),
            pltpu.SemaphoreType.DMA((11,)),
            pltpu.SemaphoreType.DMA((4,)),
            pltpu.SemaphoreType.DMA((4,)),
        ]
        + reducers,
        compiler_params=pltpu.CompilerParams(
            collective_id=0, has_side_effects=True, vmem_limit_bytes=60 * 1024 * 1024
        ),
        cost_estimate=pl.CostEstimate(flops=flops, bytes_accessed=12 << 20, transcendentals=0),
        name="system",
    )(
        comp_arch,
        comp_param,
        theta_table.T,
        port_refs.T,
        slot_mask.T,
        cut_source,
        bubble_inverse,
        port_loads,
        port_stiff.reshape(archs * terms, width, width),
        coupling,
    )
    return pl.pallas_call(
        combine_kernel,
        out_shape=(
            jax.ShapeDtypeStruct(port_loads.shape, F32),
            jax.ShapeDtypeStruct(port_loads.shape, F32),
        ),
        in_specs=[vmem, hbm, hbm, hbm],
        out_specs=(hbm, hbm),
        scratch_shapes=[
            pltpu.VMEM(port_loads.shape, F32),
            pltpu.VMEM((2 * cols, owned * dofs), BF16),
            pltpu.VMEM((2 * cols, owned * dofs), BF16),
            pltpu.VMEM((2 * cols, owned * dofs), BF16),
            pltpu.VMEM(port_loads.shape, F32),
            pltpu.VMEM(port_loads.shape, F32),
            pltpu.SemaphoreType.DMA((3 + 2 * (owned * dofs // 512),)),
        ],
        compiler_params=pltpu.CompilerParams(vmem_limit_bytes=60 * 1024 * 1024),
        cost_estimate=pl.CostEstimate(flops=1 << 28, bytes_accessed=4 << 20, transcendentals=0),
        name="combine",
    )(small, port_loads, first, second)


def solution(mesh):
    sizes = (mesh.shape["gx"], mesh.shape["gy"])
    placed = (
        P(None, ("gx", "gy")),
        P(),
        P(),
        P(("gx", "gy"), None, None),
        P(),
        P(("gx", "gy")),
        P(("gx", "gy")),
        P(("gx", "gy"), None),
        P(("gx", "gy"), None),
        P(("gx", "gy"), None),
    )
    return jax.shard_map(
        functools.partial(local, sizes),
        mesh=mesh,
        in_specs=placed,
        out_specs=(P(None, ("gx", "gy")), P(None, ("gx", "gy"))),
        check_vma=False,
    )
```
